32 devices in a mesh: group: 8 (over y, x, core), member: 4 (over z).
Axes of the slice: x: 2, y: 2, z: 4, core: 2. Of those that a mesh axis runs over, the one named last changes fastest.
Arguments:
- state: bfloat16 [8, 4, 128, 9, 256], P('group', 'member'), may hold values from -6 to 6
- coef: bfloat16 [8, 4, 128, 256], P('group', 'member'), may hold values from 0.5 to 2
- new_group: int32 [8, 4, 128], P('group', 'member'), may hold values from -1 to 7, as said below
- face_lists: int32 [8, 4, 6, 128], P('group', 'member'), may hold values from -1 to 127
- lewis: float32 [9], replicated, may hold values from 0.3 to 3
Outputs:
- smoothed: float32 [8, 4, 128, 9, 256], P('group', 'member')
The draws below stay inside these ranges and needn't reach their ends.
Inputs may be any that keep to these rules, and one draw needn't show every extreme that they name: -1 marks an old slot that holds no patch. A patch keeps its member index. At most 16 patches go from one device to one device, and at most 128 arrive at one device. Counts, offsets and slot numbers derived from new_group may cross devices in any integer encoding.
All inputs are finite; a program needn't handle non-finite values.
Results may differ from the reference program's by a relative error of at most 0.0003.
Values may be sent and summed in bfloat16 or wider, within the bound.
No kernel may reach another device: no remote copies, remote signals or barrier semaphores. Data moves between devices by JAX's collectives and lax.ppermute only.
A program may use at most 128 MiB of HBM per device.

```python
import math
import jax
import jax.numpy as jnp
from jax import lax

SPECIES = 9
PX = 16
PY = 16
SLOTS = 128
SWEEPS = 2
CELLS = 256
GROUPS = 8
MEMBERS = 4


def draw_new_group(key, part):
    key = jax.random.fold_in(key, 11)
    first, second, third, fourth = jax.random.split(key, 4)
    lane_shift = jax.random.randint(first, (MEMBERS,), 0, GROUPS)
    group_index = jnp.arange(GROUPS, dtype=jnp.int32)[:, None, None]
    slot_index = jnp.arange(SLOTS, dtype=jnp.int32)[None, None, :]
    dest = (group_index + slot_index + lane_shift[None, :, None]) % GROUPS
    busy = jax.random.randint(second, (MEMBERS, GROUPS), 0, 8) == 0
    forced = jax.random.randint(third, (MEMBERS,), 0, GROUPS)
    busy = busy | (jnp.arange(GROUPS, dtype=jnp.int32)[None, :] == forced[:, None])
    member_index = jnp.broadcast_to(jnp.arange(MEMBERS, dtype=jnp.int32)[None, :, None], dest.shape)
    hot = busy[member_index, dest]
    coin = jax.random.randint(fourth, dest.shape, 0, 2) == 0
    return jnp.where(hot | coin, dest, -1).astype(jnp.int32)


def touch_ends(array, key, least, top_value):
    longest = array.shape.index(max(array.shape))
    spots = []
    for shift in (0, 1):
        where = [jax.random.randint(jax.random.fold_in(key, axis), (), 0, length) for axis, length in enumerate(array.shape)]
        where[longest] = (where[longest] + shift) % array.shape[longest]
        spots.append(tuple(where))
    return array.at[spots[0]].set(least).at[spots[1]].set(top_value)


def block_scale(own_key, shape, shards, low, largest):
    def one(dim, blocks):
        steps = jax.random.uniform(jax.random.fold_in(jax.random.fold_in(own_key, 6), dim), (blocks,), jnp.float32, low / len(shards), largest / len(shards))
        return jnp.repeat(jnp.exp(steps), shape[dim] // blocks).reshape((-1,) + (1,) * (len(shape) - dim - 1))

    level = one(*shards[0])
    for cut in shards[1:]:
        level = level * one(*cut)
    return level


def normal_values(key, extent, width, limit, cuts=(), kind=jnp.bfloat16):
    drawn = width * jax.random.normal(key, extent, jnp.float32)
    if cuts:
        drawn = drawn * block_scale(key, extent, cuts, -0.22, 0.18)
    return jnp.clip(drawn, -limit, limit).astype(kind)


def setup_inputs(seed: int = 0) -> dict:
    key_list = jax.random.split(jax.random.key(seed), 6)
    state = normal_values(key_list[0], (GROUPS, MEMBERS, SLOTS, SPECIES, CELLS), 1.0, 6.0, ((0, 8), (1, 4)))
    coef = jnp.clip(jnp.exp(math.log(2.0) - 1.3862944 * jax.random.uniform(key_list[1], (GROUPS, MEMBERS, SLOTS, CELLS), jnp.float32) ** block_scale(key_list[1], (GROUPS, MEMBERS, SLOTS, CELLS), ((0, 8), (1, 4)), -0.2, 0.2)), 0.5, 2.0).astype(jnp.bfloat16)
    new_group = draw_new_group(jax.random.fold_in(key_list[5], 71), 0)
    face_lists = touch_ends(jax.random.randint(key_list[3], (GROUPS, MEMBERS, 6, SLOTS), -1, SLOTS), jax.random.fold_in(key_list[3], 1), -1, SLOTS - 1).astype(jnp.int32)
    lewis = jnp.clip(jnp.exp(jax.random.uniform(key_list[4], (SPECIES,), jnp.float32, math.log(0.3), math.log(3.0))), 0.3, 3.0)
    return dict(state=state, coef=coef, new_group=new_group, face_lists=face_lists, lewis=lewis)


def pick_rows(field, index):
    taken = jnp.take(field, jnp.clip(index, 0, field.shape[0] - 1), axis=0)
    return jnp.where((index >= 0)[:, None, None], taken, 0.0)


def beside_all(field, lists, lower, upper):
    count = field.shape[-1]
    span = lower.shape[-1]
    cell = jnp.arange(count, dtype=jnp.int32)
    xpos = cell % PX
    ypos = (cell // PX) % PY
    zpos = cell // span
    x_low = jnp.where(xpos == 0, jnp.roll(pick_rows(field, lists[0]), -(PX - 1), -1), jnp.roll(field, 1, -1))
    x_high = jnp.where(xpos == PX - 1, jnp.roll(pick_rows(field, lists[1]), PX - 1, -1), jnp.roll(field, -1, -1))
    y_low = jnp.where(ypos == 0, jnp.roll(pick_rows(field, lists[2]), -(PY - 1) * PX, -1), jnp.roll(field, PX, -1))
    y_high = jnp.where(ypos == PY - 1, jnp.roll(pick_rows(field, lists[3]), (PY - 1) * PX, -1), jnp.roll(field, -PX, -1))
    filler = jnp.zeros(field.shape[:-1] + (count - span,), jnp.float32)
    below = jnp.concatenate([pick_rows(lower, lists[4]), filler], -1)
    above = jnp.concatenate([filler, pick_rows(upper, lists[5])], -1)
    z_low = jnp.where(zpos == 0, below, jnp.roll(field, span, -1))
    z_high = jnp.where(zpos == count // span - 1, above, jnp.roll(field, -span, -1))
    return (x_low, x_high, y_low, y_high, z_low, z_high)


def sweep(phi, rhs, weights, lists, lower, upper, lewis):
    near = beside_all(phi, lists, lower, upper)
    flow = weights[0] * near[0]
    total = weights[0]
    for face in range(1, 6):
        flow = flow + weights[face] * near[face]
        total = total + weights[face]
    factor = lewis[:, None]
    return (rhs + factor * flow) / (1.0 + factor * total)


def stacked_faces(field):
    span = PX * PY
    tops = field[..., -span:]
    bottoms = field[..., :span]
    empty = jnp.zeros_like(tops[:1])
    return jnp.concatenate([empty, tops[:-1]], 0), jnp.concatenate([bottoms[1:], empty], 0)


def reference(state, coef, new_group, face_lists, lewis):
    groups, members, slots = new_group.shape
    valid = new_group >= 0
    onehot = (new_group[..., None] == jnp.arange(groups, dtype=jnp.int32)).astype(jnp.int32)
    lane = jnp.transpose(onehot, (1, 0, 2, 3)).reshape(members, groups * slots, groups)
    running = jnp.sum(jnp.cumsum(lane, 1) * lane, -1) - 1
    running = jnp.transpose(running.reshape(members, groups, slots), (1, 0, 2)).astype(jnp.int32)
    running = jnp.where(valid, running, slots).astype(jnp.int32)
    target = jnp.where(valid, new_group, groups).astype(jnp.int32)
    member_index = jnp.broadcast_to(jnp.arange(members, dtype=jnp.int32)[None, :, None], new_group.shape)
    rhs = jnp.zeros(state.shape, jnp.float32).at[target, member_index, running].set(state.astype(jnp.float32), mode="drop")
    new_coef = jnp.zeros(coef.shape, jnp.float32).at[target, member_index, running].set(coef.astype(jnp.float32), mode="drop")

    def one_group(items):
        rhs_g, coef_g, lists_g = items
        cell_coef = coef_g[:, :, None, :]
        coef_low, coef_high = stacked_faces(cell_coef)
        near = jax.vmap(beside_all)(cell_coef, lists_g, coef_low, coef_high)
        weights = tuple(0.5 * (cell_coef + item) for item in near)
        phi = rhs_g
        for step in range(SWEEPS):
            lower, upper = stacked_faces(phi)
            phi = jax.vmap(sweep, in_axes=(0, 0, 0, 0, 0, 0, None))(phi, rhs_g, weights, lists_g, lower, upper, lewis)
        return phi

    return lax.map(one_group, (rhs, new_coef, face_lists))
```

```python
import functools

import jax
import jax.numpy as jnp
from jax import lax
from jax.experimental import pallas as pl
from jax.experimental.pallas import tpu as pltpu
from jax.sharding import PartitionSpec as P

PX = 16
PY = 16
FACES = 6
LANES = 128
BLOCK = 32
F32 = jnp.float32
BF16 = jnp.bfloat16
VMEM_LIMIT = 28 * 1024 * 1024


def dot(a, b):
    return jnp.dot(a, b, preferred_element_type=F32)


def dot_t(a, b):
    return lax.dot_general(a, b, (((1,), (1,)), ((), ())), preferred_element_type=F32)


def iota(shape, dim):
    return lax.broadcasted_iota(jnp.int32, shape, dim)


def ones_where(mask):
    return jnp.where(mask, 1.0, 0.0).astype(BF16)


def before(n):
    return ones_where(iota((n, n), 0) < iota((n, n), 1))


def list_columns(groups):
    return -(-FACES * groups // LANES) * LANES


def pack_kernel(groups, capacity, dest_ref, lists_ref, state_ref, coef_ref, send_ref):
    species, slots, cells = state_ref.shape
    extra = list_columns(groups)
    dest = dest_ref[...]
    onehot = iota((groups, slots), 0) == dest
    earlier = dot(ones_where(onehot), before(slots))
    running = jnp.sum(jnp.where(onehot, earlier, 0.0), axis=0, keepdims=True).astype(jnp.int32)
    position = jnp.where(dest >= 0, dest * capacity + running, -1)
    place = ones_where(iota((slots, slots), 0) == position)
    send_ref[:, :cells] = dot(place, coef_ref[...]).astype(BF16)
    first = (iota((slots, slots), 0) - lax.axis_index("group") * capacity) * groups
    ahead = iota((slots, slots), 1) - first
    rows = (ahead >= 0) & (ahead < groups)
    slot = lax.rem(iota((slots, extra), 0), groups)
    column = iota((slots, extra), 1)
    packed = jnp.zeros((slots, extra), F32)
    for face in range(FACES):
        entry = (lists_ref[face] + 1).astype(F32)
        packed = packed + dot(
            jnp.where(rows, entry, 0.0).astype(BF16), ones_where(column == slot + face * groups)
        )
    send_ref[:, cells : cells + extra] = packed.astype(BF16)
    start = cells + extra
    for k in range(species):
        at = slice(start + k * cells, start + (k + 1) * cells)
        send_ref[:, at] = dot(place, state_ref[k]).astype(BF16)


def unpack_lists(groups, extra_rows):
    slots, extra = extra_rows.shape
    capacity = slots // groups
    row = lax.rem(iota((slots, slots), 1), capacity)
    ahead = iota((slots, slots), 0) - row * groups
    own = dot(ones_where((ahead >= 0) & (ahead < groups)), extra_rows)
    same = lax.rem(iota((slots, extra), 1), groups) == lax.rem(iota((slots, extra), 0), groups)
    own = jnp.where(same, own, 0.0).astype(BF16)
    ahead = iota((extra, LANES), 0) - iota((extra, LANES), 1) * groups
    return dot(own, ones_where((ahead >= 0) & (ahead < groups))).astype(jnp.int32) - 1


def sorting(coef_rows):
    slots, cells = coef_rows.shape
    lead = dot_t(ones_where(iota((8, cells), 1) == 0), coef_rows)
    valid = lead > 0.0
    slot = dot(ones_where(valid), before(slots)).astype(jnp.int32)
    slot = jnp.where(valid, slot, -1)[:1]
    return ones_where(iota((slots, slots), 0) == slot)


def picking(lists, face):
    slots = lists.shape[0]
    return ones_where(iota((slots, slots), 1) == lists[:, face : face + 1])


def edge_sources(field):
    rows = field.shape[0]
    lane = iota((rows, LANES), 1)
    x = lax.rem(lane, PX)
    sides = (field[:, :LANES], field[:, LANES:])
    turn = LANES - (PX - 1)
    x_low = [jnp.where(x == 0, pltpu.roll(s, turn, 1), 0.0) for s in sides]
    x_high = [jnp.where(x == PX - 1, pltpu.roll(s, PX - 1, 1), 0.0) for s in sides]
    y_low = jnp.where(lane < PX, pltpu.roll(sides[1], PX, 1), 0.0)
    y_high = jnp.where(lane >= LANES - PX, pltpu.roll(sides[0], LANES - PX, 1), 0.0)
    none = jnp.zeros_like(y_low)
    x_faces = jnp.concatenate([jnp.concatenate(x_low, 1), jnp.concatenate(x_high, 1)], 0)
    y_faces = jnp.concatenate(
        [jnp.concatenate([y_low, none], 1), jnp.concatenate([none, y_high], 1)], 0
    )
    return x_faces.astype(BF16), y_faces.astype(BF16)


def beside_xy(field, x_edge, y_edge):
    rows = field.shape[0]
    lane = iota((rows, LANES), 1)
    x = lax.rem(lane, PX)
    low, top = lane < PX, lane >= LANES - PX
    a, b = field[:, :LANES], field[:, LANES:]
    xa, xb = x_edge[:, :LANES], x_edge[:, LANES:]
    ya, yb = y_edge[:, :LANES], y_edge[:, LANES:]
    near0 = [jnp.where(x == 0, e, pltpu.roll(f, 1, 1)) for f, e in ((a, xa), (b, xb))]
    near1 = [jnp.where(x == PX - 1, e, pltpu.roll(f, LANES - 1, 1)) for f, e in ((a, xa), (b, xb))]
    ra, rb = pltpu.roll(a, PX, 1), pltpu.roll(b, PX, 1)
    near2 = [jnp.where(low, ya, ra), jnp.where(low, ra, rb)]
    ra, rb = pltpu.roll(a, LANES - PX, 1), pltpu.roll(b, LANES - PX, 1)
    near3 = [jnp.where(top, rb, ra), jnp.where(top, yb, rb)]
    return [jnp.concatenate(n, 1) for n in (near0, near1, near2, near3)]


def split(field):
    high = field.astype(BF16)
    return high, (field - high.astype(F32)).astype(BF16)


def blocks(slots):
    return [slice(r, r + BLOCK) for r in range(0, slots, BLOCK)]


def prepare_kernel(
    groups, head0, head_lo, head_hi,
    sort_ref, x_pick, y_pick, z_pick, weights_ref, total_ref, coef_lo, coef_hi,
):
    slots = head0.shape[0]
    cells = coef_lo.shape[1]
    heads = (head0, head_lo, head_hi)
    coefs, flat, lists = [], [], []
    for d in range(3):
        rows = heads[d][:, :cells]
        sort_ref[d] = sorting(rows)
        coef = dot(sort_ref[d], rows)
        coefs.append(coef)
        flat.append(coef.astype(BF16))
        lists.append(unpack_lists(groups, heads[d][:, cells : cells + list_columns(groups)]))
        for face, target in ((0, x_pick), (2, y_pick)):
            target[d] = jnp.concatenate(
                [picking(lists[d], face), picking(lists[d], face + 1)], 1
            )
    for i, (d, face) in enumerate(((0, 4), (0, 5), (1, 5), (2, 4), (1, 4), (2, 5))):
        z_pick[i] = picking(lists[d], face)
    coef_lo[...] = coefs[1]
    coef_hi[...] = coefs[2]
    for d in range(3):
        x_faces, y_faces = edge_sources(coefs[d])
        near = beside_xy(coefs[d], dot(x_pick[d], x_faces), dot(y_pick[d], y_faces))
        for i, source in (((0, 1), (1, 2)), ((2, 0),), ((3, 0),))[d]:
            near.append(dot(z_pick[i], flat[source]))
        total = None
        for i, n in enumerate(near):
            w = 0.5 * (coefs[d] + n)
            weights_ref[d, i] = w
            total = w if total is None else total + w
        total_ref[d] = total


def inner_kernel(
    first, start, lewis_ref, sort_ref, x_pick, y_pick, z_pick, weights_ref, total_ref,
    got0, got_lo, got_hi, num0, num_lo, num_hi, field_ref, x_ref, y_ref, z_ref, phi_ref,
):
    species, slots, cells = num0.shape
    gots = (got0, got_lo, got_hi)
    numbers = (num0, num_lo, num_hi)
    depth = field_ref.shape[0]
    for k in range(species):
        b = k % depth
        at = slice(start + k * cells, start + (k + 1) * cells)
        factor = lewis_ref[first + k]
        flat = []
        for d in range(3):
            field = dot(sort_ref[d], gots[d][:, at])
            field_ref[b, d] = field
            flat.append(field.astype(BF16))
            x_faces, y_faces = edge_sources(field)
            x_ref[b, d] = dot(x_pick[d], x_faces)
            y_ref[b, d] = dot(y_pick[d], y_faces)
        for i, source in enumerate((1, 2, 0, 0)):
            z_ref[b, i] = dot(z_pick[i], flat[source])
        for d in range(3):
            for rows in blocks(slots):
                field = field_ref[b, d, rows]
                near = beside_xy(field, x_ref[b, d, rows], y_ref[b, d, rows])
                flow = weights_ref[d, 0, rows] * near[0]
                for f in range(1, 4):
                    flow = flow + weights_ref[d, f, rows] * near[f]
                if d == 0:
                    flow = flow + weights_ref[0, 4, rows] * z_ref[b, 0, rows]
                    flow = flow + weights_ref[0, 5, rows] * z_ref[b, 1, rows]
                    number = field + factor * flow
                    phi_ref[b, rows] = number / (1.0 + factor * total_ref[0, rows])
                else:
                    flow = flow + weights_ref[d, 4, rows] * z_ref[b, 1 + d, rows]
                    numbers[d][k, rows] = field + factor * flow
        high, low = split(phi_ref[b])
        x_high, y_high = edge_sources(high.astype(F32))
        x_low, y_low = edge_sources(low.astype(F32))
        x_two = jnp.concatenate([x_pick[0], x_pick[0]], 1)
        y_two = jnp.concatenate([y_pick[0], y_pick[0]], 1)
        x_ref[b, 3] = dot(x_two, jnp.concatenate([x_high, x_low], 0))
        y_ref[b, 3] = dot(y_two, jnp.concatenate([y_high, y_low], 0))
        for rows in blocks(slots):
            near = beside_xy(phi_ref[b, rows], x_ref[b, 3, rows], y_ref[b, 3, rows])
            flow = weights_ref[0, 0, rows] * near[0]
            for f in range(1, 4):
                flow = flow + weights_ref[0, f, rows] * near[f]
            num0[k, rows] = field_ref[b, 0, rows] + factor * flow


def outer_kernel(
    first, start, head, lewis_ref, z_pick, weights_ref, total_ref, coef_lo, coef_hi,
    num0, num_lo, num_hi, got_lo2, got_hi2, head_lo2, head_hi2,
    out_ref, far_ref, w_ref, t_ref, two_ref, flow_ref,
):
    species, slots, cells = num0.shape
    gots, numbers = (got_lo2, got_hi2), (num_lo, num_hi)
    for i, (rows, coef) in enumerate(((head_lo2, coef_lo), (head_hi2, coef_hi))):
        far = dot(z_pick[4 + i], sorting(rows[:, :cells])).astype(BF16)
        far_ref[i] = far
        w = 0.5 * (coef[...] + dot(far, rows[:, :cells]))
        w_ref[i] = w
        t_ref[i] = total_ref[1 + i] + w
        two_ref[i] = jnp.concatenate([z_pick[i], z_pick[i]], 1)
    for k in range(species):
        at = slice(start + k * cells, start + (k + 1) * cells)
        factor = lewis_ref[first + k]
        for i in range(2):
            ghost = dot(far_ref[i], gots[i][:, at])
            phi = (numbers[i][k] + factor * (w_ref[i] * ghost)) / (1.0 + factor * t_ref[i])
            high, low = split(phi)
            flow_ref[k % 3, i] = dot(two_ref[i], jnp.concatenate([high, low], 0))
        for rows in blocks(slots):
            flow = weights_ref[0, 4, rows] * flow_ref[k % 3, 0, rows]
            flow = flow + weights_ref[0, 5, rows] * flow_ref[k % 3, 1, rows]
            number = num0[k, rows] + factor * flow
            out_ref[k, rows] = number / (1.0 + factor * total_ref[0, rows])


def call(kernel, out_shape, scratch, operands, specs=None, flops=0):
    whole = pl.BlockSpec(memory_space=pltpu.VMEM)
    specs = specs or {}
    moved = sum(o.size * o.dtype.itemsize for o in operands)
    moved += sum(o.size * o.dtype.itemsize for o in out_shape)
    return pl.pallas_call(
        kernel,
        out_shape=out_shape,
        grid=(1,),
        in_specs=[specs.get(i, whole) for i in range(len(operands))],
        out_specs=[whole] * len(out_shape),
        scratch_shapes=scratch,
        compiler_params=pltpu.CompilerParams(vmem_limit_bytes=VMEM_LIMIT),
        cost_estimate=pl.CostEstimate(flops=flops, bytes_accessed=moved, transcendentals=0),
    )(*operands)


def per_device(state, coef, new_group, face_lists, lewis):
    groups = lax.axis_size("group")
    members = lax.axis_size("member")
    up = [(i, i + 1) for i in range(members - 1)]
    down = [(i + 1, i) for i in range(members - 1)]
    slots, species, cells = state.shape[2:]
    capacity = slots // groups
    extra = list_columns(groups)
    start = cells + extra
    smem = pl.BlockSpec(memory_space=pltpu.SMEM)

    def shape(*dims, dtype=F32):
        return jax.ShapeDtypeStruct(dims, dtype)

    (send,) = call(
        functools.partial(pack_kernel, groups, capacity),
        [shape(slots, start + species * cells, dtype=BF16)],
        [],
        (
            new_group[0],
            jnp.transpose(face_lists[0], (1, 0, 2)),
            jnp.transpose(state[0, 0], (1, 0, 2)),
            coef[0, 0],
        ),
    )
    got = lax.all_to_all(send, "group", split_axis=0, concat_axis=0, tiled=True)
    got_lo = lax.ppermute(got, "member", up)
    got_hi = lax.ppermute(got, "member", down)
    got_lo2 = lax.ppermute(got_lo, "member", up)
    got_hi2 = lax.ppermute(got_hi, "member", down)
    head = pl.BlockSpec((slots, start), lambda i: (0, 0))
    sort, x_pick, y_pick, z_pick, weights, total, coef_lo, coef_hi = call(
        functools.partial(prepare_kernel, groups),
        [
            shape(3, slots, slots, dtype=BF16),
            shape(3, slots, 2 * slots, dtype=BF16),
            shape(3, slots, 2 * slots, dtype=BF16),
            shape(6, slots, slots, dtype=BF16),
            shape(3, 6, slots, cells),
            shape(3, slots, cells),
            shape(slots, cells),
            shape(slots, cells),
        ],
        [],
        (got, got_lo, got_hi),
        specs={0: head, 1: head, 2: head},
        flops=100_000_000,
    )
    num0, num_lo, num_hi = call(
        functools.partial(inner_kernel, 0, start),
        [shape(species, slots, cells)] * 3,
        [
            pltpu.VMEM((3, 3, slots, cells), F32),
            pltpu.VMEM((3, 4, slots, cells), F32),
            pltpu.VMEM((3, 4, slots, cells), F32),
            pltpu.VMEM((3, 4, slots, cells), F32),
            pltpu.VMEM((3, slots, cells), F32),
        ],
        (lewis, sort, x_pick, y_pick, z_pick, weights, total, got, got_lo, got_hi),
        specs={0: smem},
        flops=2_000_000_000,
    )
    (out,) = call(
        functools.partial(outer_kernel, 0, start, start),
        [shape(species, slots, cells)],
        [
            pltpu.VMEM((2, slots, slots), BF16),
            pltpu.VMEM((2, slots, cells), F32),
            pltpu.VMEM((2, slots, cells), F32),
            pltpu.VMEM((2, slots, 2 * slots), BF16),
            pltpu.VMEM((3, 2, slots, cells), F32),
        ],
        (
            lewis, z_pick, weights, total, coef_lo, coef_hi, num0, num_lo, num_hi,
            got_lo2, got_hi2, got_lo2, got_hi2,
        ),
        specs={0: smem, 11: head, 12: head},
        flops=1_000_000_000,
    )
    return jnp.transpose(out, (1, 0, 2))[None, None]


def solution(mesh):
    return jax.shard_map(
        per_device,
        mesh=mesh,
        in_specs=(
            P("group", "member", None, None, None),
            P("group", "member", None, None),
            P("group", "member", None),
            P("group", "member", None, None),
            P(),
        ),
        out_specs=P("group", "member", None, None, None),
        check_vma=False,
    )
```

```python
import functools

import jax
import jax.numpy as jnp
from jax import lax
from jax.experimental import pallas as pl
from jax.experimental.pallas import tpu as pltpu
from jax.sharding import PartitionSpec as P

PX = 16
PY = 16
FACES = 6
LANES = 128
F32 = jnp.float32
BF16 = jnp.bfloat16
VMEM_LIMIT = 28 * 1024 * 1024


def dot(a, b):
    return jnp.dot(a, b, preferred_element_type=F32)


def dot_first(a, b):
    return lax.dot_general(a, b, (((0,), (0,)), ((), ())), preferred_element_type=F32)


def iota(shape, dim):
    return lax.broadcasted_iota(jnp.int32, shape, dim)


def ones_where(mask):
    return jnp.where(mask, 1.0, 0.0).astype(BF16)


def list_blocks(capacity):
    return -(-FACES // capacity)


def pack_kernel(
    groups, capacity, cuts, dest_ref, lists_ref, state_hbm, coef_hbm, *rest
):
    sends = rest[: len(cuts)]
    state_ref, coef_ref, sems = rest[len(cuts) :]
    species, slots, cells = state_ref.shape
    coef_copy = pltpu.make_async_copy(coef_hbm, coef_ref, sems.at[species])
    coef_copy.start()
    copies = [
        pltpu.make_async_copy(state_hbm.at[k], state_ref.at[k], sems.at[k]) for k in range(species)
    ]
    for copy in copies:
        copy.start()
    dest = dest_ref[...]
    onehot = iota((groups, slots), 0) == dest
    earlier = dot(
        ones_where(onehot), ones_where(iota((slots, slots), 0) < iota((slots, slots), 1))
    )
    running = jnp.sum(jnp.where(onehot, earlier, 0.0), axis=0, keepdims=True).astype(jnp.int32)
    position = jnp.where(dest >= 0, dest * capacity + running, -1)
    place = ones_where(iota((slots, slots), 0) == position)
    first = lax.axis_index("group") * capacity
    row = iota((slots, slots), 0) - first
    for b in range(list_blocks(capacity)):
        block = jnp.zeros((slots, slots), F32)
        for i in range(min(capacity, FACES - b * capacity)):
            entry = (lists_ref[b * capacity + i] + 1).astype(F32)
            block = jnp.where(row == i, entry, block)
        at = slice(cells + b * slots, cells + (b + 1) * slots)
        sends[0][:, at] = block.astype(BF16)
    coef_copy.wait()
    sends[0][:, :cells] = dot(place, coef_ref[...]).astype(BF16)
    k = 0
    for send, count in zip(sends, cuts):
        start = send.shape[1] - count * cells
        for i in range(count):
            copies[k].wait()
            at = slice(start + i * cells, start + (i + 1) * cells)
            send[:, at] = dot(place, state_ref[k]).astype(BF16)
            k += 1


def unpack_lists(capacity, blocks):
    slots = blocks.shape[0]
    select = ones_where(lax.rem(iota((8, slots), 1), capacity) == iota((8, slots), 0))
    lists = []
    for face in range(FACES):
        b, i = divmod(face, capacity)
        if i == 0:
            rows = dot(select, blocks[:, b * slots : (b + 1) * slots]).astype(jnp.int32) - 1
        lists.append(rows[i : i + 1])
    return lists


def sorting(coef_rows):
    slots = coef_rows.shape[0]
    lead = coef_rows[:, :slots].astype(F32)[:, :1]
    valid = jnp.broadcast_to(lead, (slots, slots)) > 0.0
    slot = dot(
        ones_where(iota((slots, slots), 1) < iota((slots, slots), 0)), ones_where(valid)
    ).astype(jnp.int32)
    return ones_where(valid & (slot == iota((slots, slots), 1)))


def picking(entry):
    slots = entry.shape[1]
    return ones_where(iota((slots, slots), 0) == entry)


def twice(matrix):
    return jnp.concatenate([matrix, matrix], 0)


def split(field):
    high = field.astype(BF16)
    low = (field - high.astype(F32)).astype(BF16)
    return jnp.concatenate([high, low], 1)


def weighted_xy(weights, field_ref, edge_ref, y):
    at = PX + y * PX
    first = iota((8, LANES), 0) == 0
    last = iota((8, LANES), 0) == 7
    left = field_ref[at - 1 : at - 1 + PX]
    left = jnp.concatenate([jnp.where(first, edge_ref[0, y : y + 1], left[:8]), left[8:]], 0)
    right = field_ref[at + 1 : at + 1 + PX]
    right = jnp.concatenate([right[:8], jnp.where(last, edge_ref[1, y : y + 1], right[8:])], 0)
    flow = weights[0] * left + weights[1] * right
    flow = flow + weights[2] * field_ref[at - PX : at]
    return flow + weights[3] * field_ref[at + PX : at + 2 * PX]


def fill_edges(picks, fields, edges, exact):
    cells = fields[0].shape[0] - 2 * PX
    for face in range(4):
        if face < 2:
            rows = pl.ds(PX + (PX - 1 if face == 0 else 0), PY, stride=PX)
        else:
            rows = pl.ds(cells if face == 2 else PX, PX)
        taken = jnp.concatenate([field[rows] for field in fields], 0)
        if exact:
            got = dot(taken.astype(BF16), picks[face])
        else:
            got = dot(split(taken), twice(picks[face]))
        for i, (field, edge) in enumerate(zip(fields, edges)):
            part = got[i * PX : (i + 1) * PX]
            if face < 2:
                edge[face] = part
            elif face == 2:
                field[:PX] = part
            else:
                field[PX + cells :] = part


def prepare_kernel(
    capacity, head0, head_lo, head_hi,
    sort_ref, xy_pick, z_pick, weights_ref, total_ref, coef_lo, coef_hi, field_ref, edge_ref,
):
    slots = head0.shape[0]
    cells = coef_lo.shape[0]
    heads = (head0, head_lo, head_hi)
    coefs, lists = [], []
    for d in range(3):
        rows = heads[d][:, :cells]
        sort_ref[d] = sorting(rows)
        coef = dot_first(rows, sort_ref[d])
        coefs.append(coef.astype(BF16))
        field_ref[d, PX : PX + cells] = coef
        lists.append(unpack_lists(capacity, heads[d][:, cells:]))
        for face in range(4):
            xy_pick[d, face] = picking(lists[d][face])
        fill_edges(
            [xy_pick[d, f] for f in range(4)], [field_ref.at[d]], [edge_ref.at[d]], True
        )
    for i, (d, face) in enumerate(((0, 4), (0, 5), (1, 5), (2, 4), (1, 4), (2, 5))):
        z_pick[i] = picking(lists[d][face])
    coef_lo[...] = field_ref[1, PX : PX + cells]
    coef_hi[...] = field_ref[2, PX : PX + cells]
    for d in range(3):
        field = field_ref[d, PX : PX + cells]
        for i, source in (((0, 1), (1, 2)), ((2, 0),), ((3, 0),))[d]:
            near = dot(coefs[source], z_pick[i])
            weights_ref[d, 4 + (i if d == 0 else 0)] = 0.5 * (field + near)
        first = iota((8, LANES), 0) == 0
        last = iota((8, LANES), 0) == 7
        for y in range(PY):
            at = PX + y * PX
            rows = slice(y * PX, (y + 1) * PX)
            own = field_ref[d, at : at + PX]
            left = field_ref[d, at - 1 : at - 1 + PX]
            edge = edge_ref[d, 0, y : y + 1]
            left = jnp.concatenate([jnp.where(first, edge, left[:8]), left[8:]], 0)
            right = field_ref[d, at + 1 : at + 1 + PX]
            edge = edge_ref[d, 1, y : y + 1]
            right = jnp.concatenate([right[:8], jnp.where(last, edge, right[8:])], 0)
            near = (left, right, field_ref[d, at - PX : at], field_ref[d, at + PX : at + 2 * PX])
            total = weights_ref[d, 4, rows]
            if d == 0:
                total = total + weights_ref[d, 5, rows]
            for f in range(4):
                w = 0.5 * (own + near[f])
                weights_ref[d, f, rows] = w
                total = total + w
            total_ref[d, rows] = total


def inner_kernel(
    first, lewis_ref, sort_ref, xy_pick, z_pick, weights_ref, total_ref, got0, got_lo, got_hi,
    num0, num_lo, num_hi, field_ref, edge_ref, z_ref, phi_ref,
):
    species, cells, slots = num0.shape
    start = got0.shape[1] - species * cells
    gots = (got0, got_lo, got_hi)
    numbers = (num0, num_lo, num_hi)
    factor = [lewis_ref[first + k] for k in range(species)]
    for k in range(species):
        at = slice(start + k * cells, start + (k + 1) * cells)
        flat = []
        for d in range(3):
            field = dot_first(gots[d][:, at], sort_ref[d])
            field_ref[d, k, PX : PX + cells] = field
            flat.append(field.astype(BF16))
        for i, source in enumerate((1, 2, 0, 0)):
            z_ref[i, k] = dot(flat[source], z_pick[i])
    for d in range(3):
        fill_edges(
            [xy_pick[d, f] for f in range(4)],
            [field_ref.at[d, k] for k in range(species)],
            [edge_ref.at[d, k] for k in range(species)],
            True,
        )
    for d in range(3):
        for y in range(PY):
            rows = slice(y * PX, (y + 1) * PX)
            weights = [weights_ref[d, f, rows] for f in range(6 if d == 0 else 5)]
            for k in range(species):
                field = field_ref[d, k, PX + y * PX : 2 * PX + y * PX]
                flow = weighted_xy(weights, field_ref.at[d, k], edge_ref.at[d, k], y)
                if d == 0:
                    flow = flow + weights[4] * z_ref[0, k, rows] + weights[5] * z_ref[1, k, rows]
                    number = field + factor[k] * flow
                    phi = number / (1.0 + factor[k] * total_ref[0, rows])
                    phi_ref[k, PX + y * PX : 2 * PX + y * PX] = phi
                else:
                    flow = flow + weights[4] * z_ref[1 + d, k, rows]
                    numbers[d][k, rows] = field + factor[k] * flow
    fill_edges(
        [xy_pick[0, f] for f in range(4)],
        [phi_ref.at[k] for k in range(species)],
        [edge_ref.at[0, k] for k in range(species)],
        False,
    )
    for y in range(PY):
        rows = slice(y * PX, (y + 1) * PX)
        weights = [weights_ref[0, f, rows] for f in range(4)]
        for k in range(species):
            flow = weighted_xy(weights, phi_ref.at[k], edge_ref.at[0, k], y)
            num0[k, rows] = field_ref[0, k, PX + y * PX : 2 * PX + y * PX] + factor[k] * flow


def outer_kernel(
    first, lewis_ref, z_pick, weights_ref, total_ref, coef_lo, coef_hi,
    num0, num_lo, num_hi, got_lo2, got_hi2, head_lo2, head_hi2,
    out_ref, far_ref, w_ref, t_ref, two_ref,
):
    species, cells, slots = num0.shape
    start = got_lo2.shape[1] - species * cells
    gots, numbers = (got_lo2, got_hi2), (num_lo, num_hi)
    for i, (rows, coef) in enumerate(((head_lo2, coef_lo), (head_hi2, coef_hi))):
        far = dot(sorting(rows[:, :cells]), z_pick[4 + i]).astype(BF16)
        far_ref[i] = far
        w = 0.5 * (coef[...] + dot_first(rows[:, :cells], far))
        w_ref[i] = w
        t_ref[i] = total_ref[1 + i] + w
        two_ref[i] = twice(z_pick[i])
    for k in range(species):
        at = slice(start + k * cells, start + (k + 1) * cells)
        factor = lewis_ref[first + k]
        flow = None
        for i in range(2):
            ghost = dot_first(gots[i][:, at], far_ref[i])
            phi = (numbers[i][k] + factor * (w_ref[i] * ghost)) / (1.0 + factor * t_ref[i])
            term = weights_ref[0, 4 + i] * dot(split(phi), two_ref[i])
            flow = term if flow is None else flow + term
        out = (num0[k] + factor * flow) / (1.0 + factor * total_ref[0])
        out_ref[k] = jnp.transpose(out, (1, 0))


def call(kernel, out_shape, scratch, operands, specs=None, flops=0):
    whole = pl.BlockSpec(memory_space=pltpu.VMEM)
    specs = specs or {}
    moved = sum(o.size * o.dtype.itemsize for o in operands)
    moved += sum(o.size * o.dtype.itemsize for o in out_shape)
    return pl.pallas_call(
        kernel,
        out_shape=out_shape,
        grid=(1,),
        in_specs=[specs.get(i, whole) for i in range(len(operands))],
        out_specs=[whole] * len(out_shape),
        scratch_shapes=scratch,
        compiler_params=pltpu.CompilerParams(vmem_limit_bytes=VMEM_LIMIT),
        cost_estimate=pl.CostEstimate(flops=flops, bytes_accessed=moved, transcendentals=0),
    )(*operands)


def per_device(state, coef, new_group, face_lists, lewis):
    groups = lax.axis_size("group")
    members = lax.axis_size("member")
    up = [(i, i + 1) for i in range(members - 1)]
    down = [(i + 1, i) for i in range(members - 1)]
    slots, species, cells = state.shape[2:]
    capacity = slots // groups
    start = cells + list_blocks(capacity) * slots
    cuts = (3, species - 3)
    firsts = (0, 3)
    smem = pl.BlockSpec(memory_space=pltpu.SMEM)
    hbm = pl.BlockSpec(memory_space=pltpu.HBM)
    head = pl.BlockSpec((slots, start), lambda i: (0, 0))

    def shape(*dims, dtype=F32):
        return jax.ShapeDtypeStruct(dims, dtype)

    sends = call(
        functools.partial(pack_kernel, groups, capacity, cuts),
        [
            shape(slots, count * cells + (0 if c else start), dtype=BF16)
            for c, count in enumerate(cuts)
        ],
        [
            pltpu.VMEM((species, slots, cells), BF16),
            pltpu.VMEM((slots, cells), BF16),
            pltpu.SemaphoreType.DMA((species + 1,)),
        ],
        (
            new_group[0],
            jnp.transpose(face_lists[0], (1, 0, 2)),
            jnp.transpose(state[0, 0], (1, 0, 2)),
            coef[0, 0],
        ),
        specs={2: hbm, 3: hbm},
    )
    got = [
        lax.all_to_all(send, "group", split_axis=0, concat_axis=0, tiled=True) for send in sends
    ]
    got_lo = [lax.ppermute(rows, "member", up) for rows in got]
    got_hi = [lax.ppermute(rows, "member", down) for rows in got]
    got_lo2 = [lax.ppermute(rows, "member", up) for rows in got_lo]
    got_hi2 = [lax.ppermute(rows, "member", down) for rows in got_hi]
    padded = cells + 2 * PX
    sort, xy_pick, z_pick, weights, total, coef_lo, coef_hi = call(
        functools.partial(prepare_kernel, capacity),
        [
            shape(3, slots, slots, dtype=BF16),
            shape(3, 4, slots, slots, dtype=BF16),
            shape(6, slots, slots, dtype=BF16),
            shape(3, 6, cells, slots),
            shape(3, cells, slots),
            shape(cells, slots),
            shape(cells, slots),
        ],
        [pltpu.VMEM((3, padded, slots), F32), pltpu.VMEM((3, 2, PY, slots), F32)],
        (got[0], got_lo[0], got_hi[0]),
        specs={0: head, 1: head, 2: head},
        flops=100_000_000,
    )
    inner = [
        call(
            functools.partial(inner_kernel, first),
            [shape(count, cells, slots)] * 3,
            [
                pltpu.VMEM((3, count, padded, slots), F32),
                pltpu.VMEM((3, count, 2, PY, slots), F32),
                pltpu.VMEM((4, count, cells, slots), F32),
                pltpu.VMEM((count, padded, slots), F32),
            ],
            (lewis, sort, xy_pick, z_pick, weights, total, got[c], got_lo[c], got_hi[c]),
            specs={0: smem},
            flops=200_000_000 * count,
        )
        for c, (first, count) in enumerate(zip(firsts, cuts))
    ]
    outs = [
        call(
            functools.partial(outer_kernel, first),
            [shape(count, slots, cells)],
            [
                pltpu.VMEM((2, slots, slots), BF16),
                pltpu.VMEM((2, cells, slots), F32),
                pltpu.VMEM((2, cells, slots), F32),
                pltpu.VMEM((2, 2 * slots, slots), BF16),
            ],
            (
                lewis, z_pick, weights, total, coef_lo, coef_hi, *inner[c],
                got_lo2[c], got_hi2[c], got_lo2[0], got_hi2[0],
            ),
            specs={0: smem, 11: head, 12: head},
            flops=100_000_000 * count,
        )[0]
        for c, (first, count) in enumerate(zip(firsts, cuts))
    ]
    out = jnp.concatenate(outs, 0)
    return jnp.transpose(out, (1, 0, 2))[None, None]


def solution(mesh):
    return jax.shard_map(
        per_device,
        mesh=mesh,
        in_specs=(
            P("group", "member", None, None, None),
            P("group", "member", None, None),
            P("group", "member", None),
            P("group", "member", None, None),
            P(),
        ),
        out_specs=P("group", "member", None, None, None),
        check_vma=False,
    )
```

```python
import functools

import jax
import jax.numpy as jnp
from jax import lax
from jax.experimental import pallas as pl
from jax.experimental.pallas import tpu as pltpu
from jax.sharding import PartitionSpec as P

PX = 16
PY = 16
FACES = 6
LANES = 128
HALF = PX // 2
PITCH = PX + 8
F32 = jnp.float32
BF16 = jnp.bfloat16
VMEM_LIMIT = 28 * 1024 * 1024
PACK_LIMIT = 60 * 1024 * 1024


def dot(a, b):
    return jnp.dot(a, b, preferred_element_type=F32)


def dot_first(a, b):
    return lax.dot_general(a, b, (((0,), (0,)), ((), ())), preferred_element_type=F32)


def iota(shape, dim):
    return lax.broadcasted_iota(jnp.int32, shape, dim)


def ones_where(mask):
    return jnp.where(mask, 1.0, 0.0).astype(BF16)


def pack_kernel(
    groups, capacity, dest_hbm, lists_hbm, state_hbm, coef_hbm, send_hbm, lists_out,
    dest_ref, lists_ref, state_ref, coef_ref, send, in_sems, out_sems,
):
    species, slots, cells = state_ref.shape
    copies = [
        pltpu.make_async_copy(source, target, in_sems.at[i])
        for i, (source, target) in enumerate(
            (
                (dest_hbm, dest_ref),
                (coef_hbm, coef_ref),
                (state_hbm, state_ref),
                (lists_hbm, lists_ref),
            )
        )
    ]
    for copy in copies:
        copy.start()
    copies[0].wait()
    dest = dest_ref[...]
    onehot = iota((groups, slots), 0) == dest
    earlier = dot(
        ones_where(onehot), ones_where(iota((slots, slots), 0) < iota((slots, slots), 1))
    )
    running = jnp.sum(jnp.where(onehot, earlier, 0.0), axis=0, keepdims=True).astype(jnp.int32)
    position = jnp.where(dest >= 0, dest * capacity + running, -1)
    place = ones_where(iota((slots, slots), 0) == position)
    copies[1].wait()
    send[:, :cells] = dot(place, coef_ref[...]).astype(BF16)
    copies[2].wait()
    out_copies = []
    middle = cells + species // 2 * cells
    for k in range(species):
        at = slice((k + 1) * cells, (k + 2) * cells)
        send[:, at] = dot(place, state_ref[k]).astype(BF16)
        if at.stop in (middle, send.shape[1]):
            at = slice(0 if at.stop == middle else middle, at.stop)
            i = len(out_copies)
            out_copies.append(
                pltpu.make_async_copy(send.at[:, at], send_hbm.at[:, at], out_sems.at[i])
            )
            out_copies[-1].start()
    copies[3].wait()
    none = jnp.zeros((1, slots), jnp.int32)
    rows = [lists_ref[f] + 1 for f in range(FACES)] + [none] * (8 - FACES)
    lists_out[...] = jnp.concatenate(rows, 0)
    for copy in out_copies:
        copy.wait()


def sorting(coef_rows):
    slots = coef_rows.shape[0]
    lead = coef_rows[:, :slots].astype(F32)[:, :1]
    valid = jnp.broadcast_to(lead, (slots, slots)) > 0.0
    slot = dot(
        ones_where(iota((slots, slots), 1) < iota((slots, slots), 0)), ones_where(valid)
    ).astype(jnp.int32)
    return ones_where(valid & (slot == iota((slots, slots), 1)))


def picking(entry):
    slots = entry.shape[1]
    return ones_where(iota((slots, slots), 0) == entry)


def twice(matrix):
    return jnp.concatenate([matrix, matrix], 0)


def split(field):
    high = field.astype(BF16)
    low = (field - high.astype(F32)).astype(BF16)
    return jnp.concatenate([high, low], 1)


PADDED = (PY + 2) * PITCH


def row(y):
    return (y + 1) * PITCH + PITCH - PX


def step(start):
    return pl.ds(start, HALF, stride=2)


def natural(y, odd):
    return step(y * PX + odd)


def halves(y, odd):
    return slice(y * PX + odd * HALF, y * PX + (odd + 1) * HALF)


def put(padded, field):
    for y in range(PY):
        padded[row(y) : row(y) + PX] = field[y * PX : (y + 1) * PX]


def beside_xy(padded, y, odd):
    at = row(y) + odd
    return [padded[step(at + shift)] for shift in (-1, 1, -PITCH, PITCH)]


def weighted(weights, values):
    flow = weights[0] * values[0]
    for w, v in zip(weights[1:], values[1:]):
        flow = flow + w * v
    return flow


def fill_edges(picks, fields, exact):
    x_first, x_last = row(0), row(0) + PX - 1
    places = (
        (pl.ds(x_last, PY, stride=PITCH), pl.ds(x_first - 1, PY, stride=PITCH)),
        (pl.ds(x_first, PY, stride=PITCH), pl.ds(x_last + 1, PY, stride=PITCH)),
        (pl.ds(row(PY - 1), PX), pl.ds(row(-1), PX)),
        (pl.ds(row(0), PX), pl.ds(row(PY), PX)),
    )
    for pick, (source, target) in zip(picks, places):
        taken = jnp.concatenate([field[source] for field in fields], 0)
        got = dot(taken.astype(BF16), pick) if exact else dot(split(taken), twice(pick))
        for i, field in enumerate(fields):
            field[target] = got[i * PX : (i + 1) * PX]


def pick_kernel(members, lists0, all_lists, pick_ref, xy_pick, z_pick):
    slots = lists0.shape[1]
    member = lax.axis_index("member")
    lists_lo = jnp.where(member > 0, all_lists[jnp.maximum(member - 1, 0)], 0)
    lists_hi = jnp.where(member < members - 1, all_lists[jnp.minimum(member + 1, members - 1)], 0)

    def picking(lists, face):
        return ones_where(iota((slots, slots), 0) == lists[face : face + 1] - 1)

    for face in range(FACES):
        pick_ref[face] = picking(lists0, face)
    for d, lists in enumerate((lists_lo, lists_hi)):
        for face in range(4):
            xy_pick[d, face] = picking(lists, face)
    z_pick[0] = jnp.concatenate([picking(lists_lo, 5), picking(lists_hi, 4)], 1)
    z_pick[1] = jnp.concatenate([picking(lists_lo, 4), picking(lists_hi, 5)], 1)


def own_kernel(
    lewis_ref, got, pick_ref,
    later_ref, coef_ref, weights_ref, flat_ref, base_ref, rhs_ref, coef_pad, field_ref,
):
    species, cells, slots = base_ref.shape
    later_ref[...] = got[:, got.shape[1] - later_ref.shape[1] :]
    sort = sorting(got[:, :cells])
    coef = dot_first(got[:, :cells], sort)
    coef_ref[...] = coef
    put(coef_pad, coef)
    picks = [pick_ref[face] for face in range(4)]
    fill_edges(picks, [coef_pad], True)
    for k in range(species):
        field = dot_first(got[:, (k + 1) * cells : (k + 2) * cells], sort)
        put(field_ref.at[k], field)
        flat_ref[k] = field.astype(BF16)
    fill_edges(picks, [field_ref.at[k] for k in range(species)], True)
    factor = [lewis_ref[k] for k in range(species)]
    for y in range(PY):
        for odd in range(2):
            at = halves(y, odd)
            own = coef_pad[step(row(y) + odd)]
            weights = [0.5 * (own + near) for near in beside_xy(coef_pad, y, odd)]
            for f in range(4):
                weights_ref[f, at] = weights[f]
            for k in range(species):
                field = field_ref[k, step(row(y) + odd)]
                flow = weighted(weights, beside_xy(field_ref.at[k], y, odd))
                base_ref[k, at] = field + factor[k] * flow
                rhs_ref[k, at] = field


def prepare_kernel(
    head_lo, head_hi, coef0, pick0, weights0, xy_pick, z_pick,
    sort_ref, z_natural, z_halves, total0, beside_ref, total_ref, coef_ref, padded, z_ref,
):
    cells, slots = coef0.shape
    for d, head in enumerate((head_lo, head_hi)):
        rows = head[...]
        sort = sorting(rows)
        both = jnp.concatenate([sort, dot(sort, pick0[4 + d]).astype(BF16)], 1)
        sort_ref[d] = both
        coef = dot_first(rows, both)
        coef_ref[d] = coef[:, :slots]
        put(padded.at[d], coef[:, :slots])
        z_natural[d] = 0.5 * (coef0[...] + coef[:, slots:])
        fill_edges([xy_pick[d, f] for f in range(4)], [padded.at[d]], True)
    near = dot(coef0[...].astype(BF16), z_pick[0])
    z_ref[0] = near[:, :slots]
    z_ref[1] = near[:, slots:]
    for y in range(PY):
        for odd in range(2):
            at = halves(y, odd)
            total = None
            for i in range(2):
                w = z_natural[i, natural(y, odd)]
                z_halves[i, at] = w
                total = w if total is None else total + w
            for f in range(4):
                total = total + weights0[f, at]
            total0[at] = total
            for d in range(2):
                own = padded[d, step(row(y) + odd)]
                near = [*beside_xy(padded.at[d], y, odd), z_ref[d, natural(y, odd)]]
                total = None
                for f in range(5):
                    w = 0.5 * (own + near[f])
                    beside_ref[d, f, at] = w
                    total = w if total is None else total + w
                total_ref[d, natural(y, odd)] = total


def inner_kernel(
    first, lewis_ref, sort_ref, xy_pick, z_pick, z_halves, total0, beside_ref,
    pick0, weights0, flat_ref, base_ref, rhs_ref, got_lo, got_hi,
    num0, scale0, num_lo, num_hi, field_ref, z_ref, phi_ref,
):
    species, cells, slots = num0.shape
    start = got_lo.shape[1] - species * cells
    gots, numbers = (got_lo, got_hi), (num_lo, num_hi)
    factor = [lewis_ref[first + k] for k in range(species)]
    for k in range(species):
        at = slice(start + k * cells, start + (k + 1) * cells)
        near = dot(flat_ref[first + k], z_pick[0])
        for d in range(2):
            both = dot_first(gots[d][:, at], sort_ref[d])
            put(field_ref.at[d, k], both[:, :slots])
            z_ref[d, k] = both[:, slots:]
            z_ref[2 + d, k] = near[:, d * slots : (d + 1) * slots]
    for y in range(PY):
        for odd in range(2):
            at = halves(y, odd)
            weights = [z_halves[i, at] for i in range(2)]
            total = total0[at]
            for k in range(species):
                near = [z_ref[i, k, natural(y, odd)] for i in range(2)]
                number = base_ref[first + k, at] + factor[k] * weighted(weights, near)
                inverse = 1.0 / (1.0 + factor[k] * total)
                phi_ref[k, step(row(y) + odd)] = number * inverse
                scale0[k, natural(y, odd)] = inverse
    fill_edges([pick0[f] for f in range(4)], [phi_ref.at[k] for k in range(species)], False)
    for d in range(2):
        fill_edges(
            [xy_pick[d, f] for f in range(4)], [field_ref.at[d, k] for k in range(species)], True
        )
    for d in range(2):
        for y in range(PY):
            for odd in range(2):
                at = halves(y, odd)
                weights = [beside_ref[d, f, at] for f in range(5)]
                for k in range(species):
                    near = beside_xy(field_ref.at[d, k], y, odd)
                    near.append(z_ref[2 + d, k, natural(y, odd)])
                    numbers[d][k, natural(y, odd)] = (
                        field_ref[d, k, step(row(y) + odd)] + factor[k] * weighted(weights, near)
                    )
    for y in range(PY):
        for odd in range(2):
            at = halves(y, odd)
            weights = [weights0[f, at] for f in range(4)]
            for k in range(species):
                near = beside_xy(phi_ref.at[k], y, odd)
                inverse = scale0[k, natural(y, odd)]
                number = rhs_ref[first + k, at] + factor[k] * weighted(weights, near)
                num0[k, natural(y, odd)] = number * inverse
                scale0[k, natural(y, odd)] = factor[k] * inverse


def far_kernel(pick0, z_pick, total_ref, coef_ref, head_lo2, head_hi2, far_ref, w_ref, t_ref, two_ref):
    cells = coef_ref.shape[1]
    slots = coef_ref.shape[2]
    none = jnp.zeros((slots, slots), BF16)
    rows = [head_lo2[...], head_hi2[...]]
    fars = []
    for i in range(2):
        fars.append(dot(sorting(rows[i]), z_pick[1, :, i * slots : (i + 1) * slots]).astype(BF16))
        two_ref[i] = twice(pick0[4 + i])
    far = jnp.concatenate(
        [jnp.concatenate([fars[0], none], 1), jnp.concatenate([none, fars[1]], 1)], 0
    )
    far_ref[...] = far
    near = dot_first(jnp.concatenate(rows, 0), far)
    for i in range(2):
        w = 0.5 * (coef_ref[i] + near[:, i * slots : (i + 1) * slots])
        w_ref[i] = w
        t_ref[i] = total_ref[i] + w


def outer_kernel(
    first, lewis_ref, far_ref, w_ref, t_ref, two_ref, z_natural,
    num0, scale0, num_lo, num_hi, got_lo2, got_hi2, *rest,
):
    species, cells, slots = num0.shape
    start = got_lo2.shape[1] - species * cells
    numbers = (num_lo, num_hi)
    copies = []
    if first:
        early, out_hbm, out_ref, sems = rest
        copies.append(
            pltpu.make_async_copy(early, out_hbm.at[:first], sems.at[species])
        )
        copies[-1].start()
    else:
        (out_ref,) = rest
    for k in range(species):
        at = slice(start + k * cells, start + (k + 1) * cells)
        factor = lewis_ref[first + k]
        ghosts = dot_first(jnp.concatenate([got_lo2[:, at], got_hi2[:, at]], 0), far_ref[...])
        flow = None
        for i in range(2):
            ghost = ghosts[:, i * slots : (i + 1) * slots]
            phi = (numbers[i][k] + factor * (w_ref[i] * ghost)) * (1.0 / (1.0 + factor * t_ref[i]))
            term = z_natural[i] * dot(split(phi), two_ref[i])
            flow = term if flow is None else flow + term
        out_ref[k] = jnp.transpose(num0[k] + scale0[k] * flow, (1, 0))
        if first:
            copies.append(pltpu.make_async_copy(out_ref.at[k], out_hbm.at[first + k], sems.at[k]))
            copies[-1].start()
    for copy in copies:
        copy.wait()


def call(
    kernel, out_shape, scratch, operands, specs=None, outs=None, flops=0, limit=0,
    grid=(1,),
):
    whole = pl.BlockSpec(memory_space=pltpu.VMEM)
    specs = specs or {}
    moved = sum(o.size * o.dtype.itemsize for o in operands)
    moved += sum(o.size * o.dtype.itemsize for o in out_shape)
    return pl.pallas_call(
        kernel,
        out_shape=out_shape,
        grid=grid,
        in_specs=[specs.get(i, whole) for i in range(len(operands))],
        out_specs=outs or [whole] * len(out_shape),
        scratch_shapes=scratch,
        compiler_params=pltpu.CompilerParams(vmem_limit_bytes=limit or VMEM_LIMIT),
        cost_estimate=pl.CostEstimate(flops=flops, bytes_accessed=moved, transcendentals=0),
    )(*operands)


def per_device(state, coef, new_group, face_lists, lewis):
    groups = lax.axis_size("group")
    members = lax.axis_size("member")
    up = [(i, i + 1) for i in range(members - 1)]
    down = [(i + 1, i) for i in range(members - 1)]
    slots, species, cells = state.shape[2:]
    capacity = slots // groups
    cuts = (species - species // 2, species // 2)
    firsts = (0, cuts[0])
    width = (1 + species) * cells
    middle = (1 + cuts[0]) * cells
    smem = pl.BlockSpec(memory_space=pltpu.SMEM)
    anywhere = pl.BlockSpec(memory_space=pl.ANY)
    head = pl.BlockSpec((slots, cells), lambda i: (0, 0))

    def shape(*dims, dtype=F32):
        return jax.ShapeDtypeStruct(dims, dtype)

    send, lists = call(
        functools.partial(pack_kernel, groups, capacity),
        [shape(slots, width, dtype=BF16), shape(8, slots, dtype=jnp.int32)],
        [
            pltpu.VMEM((1, slots), jnp.int32),
            pltpu.VMEM((FACES, 1, slots), jnp.int32),
            pltpu.VMEM((species, slots, cells), BF16),
            pltpu.VMEM((slots, cells), BF16),
            pltpu.VMEM((slots, width), BF16),
            pltpu.SemaphoreType.DMA((4,)),
            pltpu.SemaphoreType.DMA((2,)),
        ],
        (
            new_group[0],
            jnp.transpose(face_lists[0], (1, 0, 2)),
            jnp.transpose(state[0, 0], (1, 0, 2)),
            coef[0, 0],
        ),
        specs={i: anywhere for i in range(4)},
        outs=[anywhere, pl.BlockSpec(memory_space=pltpu.VMEM)],
        limit=PACK_LIMIT,
        grid=(),
    )
    rows = lax.all_to_all(send, "group", split_axis=0, concat_axis=0, tiled=True)
    all_lists = lax.all_gather(lists, "member")
    rows, all_lists = lax.optimization_barrier((rows, all_lists))
    pick0, xy_pick, z_pick = call(
        functools.partial(pick_kernel, members),
        [
            shape(FACES, slots, slots, dtype=BF16),
            shape(2, 4, slots, slots, dtype=BF16),
            shape(2, slots, 2 * slots, dtype=BF16),
        ],
        [],
        (lists, all_lists),
    )
    later, coef0, weights0, flat, base, rhs = call(
        own_kernel,
        [
            shape(slots, width - middle, dtype=BF16),
            shape(cells, slots),
            shape(4, cells, slots),
            shape(species, cells, slots, dtype=BF16),
            shape(species, cells, slots),
            shape(species, cells, slots),
        ],
        [pltpu.VMEM((PADDED, slots), F32), pltpu.VMEM((species, PADDED, slots), F32)],
        (lewis, rows, pick0),
        specs={0: smem},
        flops=500_000_000,
    )
    got = [rows[:, :middle], later]
    got_lo = [lax.ppermute(part, "member", up) for part in got]
    got_hi = [lax.ppermute(part, "member", down) for part in got]
    got_lo2 = [lax.ppermute(part, "member", up) for part in got_lo]
    got_hi2 = [lax.ppermute(part, "member", down) for part in got_hi]
    sort, z_natural, z_halves, total0, beside, total, coefs = call(
        prepare_kernel,
        [
            shape(2, slots, 2 * slots, dtype=BF16),
            shape(2, cells, slots),
            shape(2, cells, slots),
            shape(cells, slots),
            shape(2, 5, cells, slots),
            shape(2, cells, slots),
            shape(2, cells, slots),
        ],
        [pltpu.VMEM((2, PADDED, slots), F32), pltpu.VMEM((2, cells, slots), F32)],
        (got_lo[0], got_hi[0], coef0, pick0, weights0, xy_pick, z_pick),
        specs={0: head, 1: head},
        flops=100_000_000,
    )
    inner = [
        call(
            functools.partial(inner_kernel, first),
            [shape(count, cells, slots)] * 4,
            [
                pltpu.VMEM((2, count, PADDED, slots), F32),
                pltpu.VMEM((4, count, cells, slots), F32),
                pltpu.VMEM((count, PADDED, slots), F32),
            ],
            (
                lewis, sort, xy_pick, z_pick, z_halves, total0, beside,
                pick0, weights0, flat, base, rhs, got_lo[c], got_hi[c],
            ),
            specs={0: smem},
            flops=200_000_000 * count,
        )
        for c, (first, count) in enumerate(zip(firsts, cuts))
    ]
    far = call(
        far_kernel,
        [
            shape(2 * slots, 2 * slots, dtype=BF16),
            shape(2, cells, slots),
            shape(2, cells, slots),
            shape(2, 2 * slots, slots, dtype=BF16),
        ],
        [],
        (pick0, z_pick, total, coefs, got_lo2[0], got_hi2[0]),
        specs={4: head, 5: head},
        flops=50_000_000,
    )
    (early,) = call(
        functools.partial(outer_kernel, 0),
        [shape(cuts[0], slots, cells)],
        [],
        (lewis, *far, z_natural, *inner[0], got_lo2[0], got_hi2[0]),
        specs={0: smem},
        flops=100_000_000 * cuts[0],
    )
    (out,) = call(
        functools.partial(outer_kernel, firsts[1]),
        [shape(species, slots, cells)],
        [pltpu.VMEM((cuts[1], slots, cells), F32), pltpu.SemaphoreType.DMA((cuts[1] + 1,))],
        (lewis, *far, z_natural, *inner[1], got_lo2[1], got_hi2[1], early),
        specs={0: smem},
        outs=[anywhere],
        flops=100_000_000 * cuts[1],
    )
    return jnp.transpose(out, (1, 0, 2))[None, None]


def solution(mesh):
    return jax.shard_map(
        per_device,
        mesh=mesh,
        in_specs=(
            P("group", "member", None, None, None),
            P("group", "member", None, None),
            P("group", "member", None),
            P("group", "member", None, None),
            P(),
        ),
        out_specs=P("group", "member", None, None, None),
        check_vma=False,
    )
```

```python
import functools

import jax
import jax.numpy as jnp
from jax import lax
from jax.experimental import pallas as pl
from jax.experimental.pallas import tpu as pltpu
from jax.sharding import PartitionSpec as P

PX = 16
PY = 16
FACES = 6
LANES = 128
HALF = PX // 2
PITCH = PX + 8
F32 = jnp.float32
BF16 = jnp.bfloat16
VMEM_LIMIT = 28 * 1024 * 1024
PACK_LIMIT = 60 * 1024 * 1024


def dot(a, b):
    return jnp.dot(a, b, preferred_element_type=F32)


def dot_first(a, b):
    return lax.dot_general(a, b, (((0,), (0,)), ((), ())), preferred_element_type=F32)


def iota(shape, dim):
    return lax.broadcasted_iota(jnp.int32, shape, dim)


def ones_where(mask):
    return jnp.where(mask, 1.0, 0.0).astype(BF16)


def pack_kernel(
    groups, capacity, dest_hbm, lists_hbm, state_hbm, coef_hbm, send_hbm, lists_out,
    dest_ref, lists_ref, state_ref, coef_ref, send, in_sems, out_sems,
):
    species, slots, cells = state_ref.shape
    copies = [
        pltpu.make_async_copy(source, target, in_sems.at[i])
        for i, (source, target) in enumerate(
            (
                (dest_hbm, dest_ref),
                (coef_hbm, coef_ref),
                (state_hbm, state_ref),
                (lists_hbm, lists_ref),
            )
        )
    ]
    for copy in copies:
        copy.start()
    copies[0].wait()
    dest = dest_ref[...]
    onehot = iota((groups, slots), 0) == dest
    earlier = dot(
        ones_where(onehot), ones_where(iota((slots, slots), 0) < iota((slots, slots), 1))
    )
    running = jnp.sum(jnp.where(onehot, earlier, 0.0), axis=0, keepdims=True).astype(jnp.int32)
    position = jnp.where(dest >= 0, dest * capacity + running, -1)
    place = ones_where(iota((slots, slots), 0) == position)
    copies[1].wait()
    send[:, :cells] = dot(place, coef_ref[...]).astype(BF16)
    copies[2].wait()
    out_copies = []
    middle = cells + species // 2 * cells
    for k in range(species):
        at = slice((k + 1) * cells, (k + 2) * cells)
        send[:, at] = dot(place, state_ref[k]).astype(BF16)
        if at.stop in (middle, send.shape[1]):
            at = slice(0 if at.stop == middle else middle, at.stop)
            i = len(out_copies)
            out_copies.append(
                pltpu.make_async_copy(send.at[:, at], send_hbm.at[:, at], out_sems.at[i])
            )
            out_copies[-1].start()
    copies[3].wait()
    none = jnp.zeros((1, slots), jnp.int32)
    rows = [lists_ref[f] + 1 for f in range(FACES)] + [none] * (8 - FACES)
    lists_out[...] = jnp.concatenate(rows, 0)
    for copy in out_copies:
        copy.wait()


def sorting(coef_rows):
    slots = coef_rows.shape[0]
    lead = coef_rows[:, :slots].astype(F32)[:, :1]
    valid = jnp.broadcast_to(lead, (slots, slots)) > 0.0
    slot = dot(
        ones_where(iota((slots, slots), 1) < iota((slots, slots), 0)), ones_where(valid)
    ).astype(jnp.int32)
    return ones_where(valid & (slot == iota((slots, slots), 1)))


def picking(entry):
    slots = entry.shape[1]
    return ones_where(iota((slots, slots), 0) == entry)


def twice(matrix):
    return jnp.concatenate([matrix, matrix], 0)


def split(field):
    high = field.astype(BF16)
    low = (field - high.astype(F32)).astype(BF16)
    return jnp.concatenate([high, low], 1)


PADDED = (PY + 2) * PITCH


def row(y):
    return (y + 1) * PITCH + PITCH - PX


def step(start):
    return pl.ds(start, HALF, stride=2)


def natural(y, odd):
    return step(y * PX + odd)


def halves(y, odd):
    return slice(y * PX + odd * HALF, y * PX + (odd + 1) * HALF)


def put(padded, field):
    for y in range(PY):
        padded[row(y) : row(y) + PX] = field[y * PX : (y + 1) * PX]


def beside_xy(padded, y, odd):
    at = row(y) + odd
    return [padded[step(at + shift)] for shift in (-1, 1, -PITCH, PITCH)]


def weighted(weights, values):
    flow = weights[0] * values[0]
    for w, v in zip(weights[1:], values[1:]):
        flow = flow + w * v
    return flow


def fill_edges(picks, fields, exact):
    x_first, x_last = row(0), row(0) + PX - 1
    places = (
        (pl.ds(x_last, PY, stride=PITCH), pl.ds(x_first - 1, PY, stride=PITCH)),
        (pl.ds(x_first, PY, stride=PITCH), pl.ds(x_last + 1, PY, stride=PITCH)),
        (pl.ds(row(PY - 1), PX), pl.ds(row(-1), PX)),
        (pl.ds(row(0), PX), pl.ds(row(PY), PX)),
    )
    for pick, (source, target) in zip(picks, places):
        taken = jnp.concatenate([field[source] for field in fields], 0)
        got = dot(taken.astype(BF16), pick) if exact else dot(split(taken), twice(pick))
        for i, field in enumerate(fields):
            field[target] = got[i * PX : (i + 1) * PX]


def pick_kernel(lists0, lists_lo, lists_hi, pick_ref, xy_pick, z_pick):
    slots = lists0.shape[1]

    def picking(lists, face):
        return ones_where(iota((slots, slots), 0) == lists[face : face + 1] - 1)

    for face in range(FACES):
        pick_ref[face] = picking(lists0, face)
    for d, lists in enumerate((lists_lo, lists_hi)):
        for face in range(4):
            xy_pick[d, face] = picking(lists, face)
    z_pick[0] = jnp.concatenate([picking(lists_lo, 5), picking(lists_hi, 4)], 1)
    z_pick[1] = jnp.concatenate([picking(lists_lo, 4), picking(lists_hi, 5)], 1)


def own_kernel(
    lewis_ref, got, pick_ref,
    coef_ref, weights_ref, flat_ref, base_ref, rhs_ref, coef_pad, field_ref,
):
    species, cells, slots = base_ref.shape
    sort = sorting(got[:, :cells])
    coef = dot_first(got[:, :cells], sort)
    coef_ref[...] = coef
    put(coef_pad, coef)
    picks = [pick_ref[face] for face in range(4)]
    fill_edges(picks, [coef_pad], True)
    for k in range(species):
        field = dot_first(got[:, (k + 1) * cells : (k + 2) * cells], sort)
        put(field_ref.at[k], field)
        flat_ref[k] = field.astype(BF16)
    fill_edges(picks, [field_ref.at[k] for k in range(species)], True)
    factor = [lewis_ref[k] for k in range(species)]
    for y in range(PY):
        for odd in range(2):
            at = halves(y, odd)
            own = coef_pad[step(row(y) + odd)]
            weights = [0.5 * (own + near) for near in beside_xy(coef_pad, y, odd)]
            for f in range(4):
                weights_ref[f, at] = weights[f]
            for k in range(species):
                field = field_ref[k, step(row(y) + odd)]
                flow = weighted(weights, beside_xy(field_ref.at[k], y, odd))
                base_ref[k, at] = field + factor[k] * flow
                rhs_ref[k, at] = field


def prepare_kernel(
    head_lo, head_hi, coef0, pick0, weights0, xy_pick, z_pick,
    sort_ref, z_natural, z_halves, total0, beside_ref, total_ref, coef_ref, padded, z_ref,
):
    cells, slots = coef0.shape
    for d, head in enumerate((head_lo, head_hi)):
        rows = head[...]
        sort = sorting(rows)
        both = jnp.concatenate([sort, dot(sort, pick0[4 + d]).astype(BF16)], 1)
        sort_ref[d] = both
        coef = dot_first(rows, both)
        coef_ref[d] = coef[:, :slots]
        put(padded.at[d], coef[:, :slots])
        z_natural[d] = 0.5 * (coef0[...] + coef[:, slots:])
        fill_edges([xy_pick[d, f] for f in range(4)], [padded.at[d]], True)
    near = dot(coef0[...].astype(BF16), z_pick[0])
    z_ref[0] = near[:, :slots]
    z_ref[1] = near[:, slots:]
    for y in range(PY):
        for odd in range(2):
            at = halves(y, odd)
            total = None
            for i in range(2):
                w = z_natural[i, natural(y, odd)]
                z_halves[i, at] = w
                total = w if total is None else total + w
            for f in range(4):
                total = total + weights0[f, at]
            total0[at] = total
            for d in range(2):
                own = padded[d, step(row(y) + odd)]
                near = [*beside_xy(padded.at[d], y, odd), z_ref[d, natural(y, odd)]]
                total = None
                for f in range(5):
                    w = 0.5 * (own + near[f])
                    beside_ref[d, f, at] = w
                    total = w if total is None else total + w
                total_ref[d, natural(y, odd)] = total


def inner_kernel(
    first, lewis_ref, sort_ref, xy_pick, z_pick, z_halves, total0, beside_ref,
    pick0, weights0, flat_ref, base_ref, rhs_ref, got_lo, got_hi,
    num0, scale0, num_lo, num_hi, field_ref, z_ref, phi_ref,
):
    species, cells, slots = num0.shape
    start = got_lo.shape[1] - species * cells
    gots, numbers = (got_lo, got_hi), (num_lo, num_hi)
    factor = [lewis_ref[first + k] for k in range(species)]
    for k in range(species):
        at = slice(start + k * cells, start + (k + 1) * cells)
        near = dot(flat_ref[first + k], z_pick[0])
        for d in range(2):
            both = dot_first(gots[d][:, at], sort_ref[d])
            put(field_ref.at[d, k], both[:, :slots])
            z_ref[d, k] = both[:, slots:]
            z_ref[2 + d, k] = near[:, d * slots : (d + 1) * slots]
    for y in range(PY):
        for odd in range(2):
            at = halves(y, odd)
            weights = [z_halves[i, at] for i in range(2)]
            total = total0[at]
            for k in range(species):
                near = [z_ref[i, k, natural(y, odd)] for i in range(2)]
                number = base_ref[first + k, at] + factor[k] * weighted(weights, near)
                inverse = 1.0 / (1.0 + factor[k] * total)
                phi_ref[k, step(row(y) + odd)] = number * inverse
                scale0[k, natural(y, odd)] = inverse
    fill_edges([pick0[f] for f in range(4)], [phi_ref.at[k] for k in range(species)], False)
    for d in range(2):
        fill_edges(
            [xy_pick[d, f] for f in range(4)], [field_ref.at[d, k] for k in range(species)], True
        )
    for d in range(2):
        for y in range(PY):
            for odd in range(2):
                at = halves(y, odd)
                weights = [beside_ref[d, f, at] for f in range(5)]
                for k in range(species):
                    near = beside_xy(field_ref.at[d, k], y, odd)
                    near.append(z_ref[2 + d, k, natural(y, odd)])
                    numbers[d][k, natural(y, odd)] = (
                        field_ref[d, k, step(row(y) + odd)] + factor[k] * weighted(weights, near)
                    )
    for y in range(PY):
        for odd in range(2):
            at = halves(y, odd)
            weights = [weights0[f, at] for f in range(4)]
            for k in range(species):
                near = beside_xy(phi_ref.at[k], y, odd)
                inverse = scale0[k, natural(y, odd)]
                number = rhs_ref[first + k, at] + factor[k] * weighted(weights, near)
                num0[k, natural(y, odd)] = number * inverse
                scale0[k, natural(y, odd)] = factor[k] * inverse


def far_kernel(pick0, z_pick, total_ref, coef_ref, head_lo2, head_hi2, far_ref, w_ref, t_ref, two_ref):
    cells = coef_ref.shape[1]
    slots = coef_ref.shape[2]
    none = jnp.zeros((slots, slots), BF16)
    rows = [head_lo2[...], head_hi2[...]]
    fars = []
    for i in range(2):
        fars.append(dot(sorting(rows[i]), z_pick[1, :, i * slots : (i + 1) * slots]).astype(BF16))
        two_ref[i] = twice(pick0[4 + i])
    far = jnp.concatenate(
        [jnp.concatenate([fars[0], none], 1), jnp.concatenate([none, fars[1]], 1)], 0
    )
    far_ref[...] = far
    near = dot_first(jnp.concatenate(rows, 0), far)
    for i in range(2):
        w = 0.5 * (coef_ref[i] + near[:, i * slots : (i + 1) * slots])
        w_ref[i] = w
        t_ref[i] = total_ref[i] + w


def outer_kernel(
    first, lewis_ref, far_ref, w_ref, t_ref, two_ref, z_natural,
    num0, scale0, num_lo, num_hi, got_lo2, got_hi2, *rest,
):
    species, cells, slots = num0.shape
    start = got_lo2.shape[1] - species * cells
    numbers = (num_lo, num_hi)
    copies = []
    if first:
        early, out_hbm, out_ref, sems = rest
        copies.append(
            pltpu.make_async_copy(early, out_hbm.at[:first], sems.at[species])
        )
        copies[-1].start()
    else:
        (out_ref,) = rest
    for k in range(species):
        at = slice(start + k * cells, start + (k + 1) * cells)
        factor = lewis_ref[first + k]
        ghosts = dot_first(jnp.concatenate([got_lo2[:, at], got_hi2[:, at]], 0), far_ref[...])
        flow = None
        for i in range(2):
            ghost = ghosts[:, i * slots : (i + 1) * slots]
            phi = (numbers[i][k] + factor * (w_ref[i] * ghost)) * (1.0 / (1.0 + factor * t_ref[i]))
            term = z_natural[i] * dot(split(phi), two_ref[i])
            flow = term if flow is None else flow + term
        out_ref[k] = jnp.transpose(num0[k] + scale0[k] * flow, (1, 0))
        if first:
            copies.append(pltpu.make_async_copy(out_ref.at[k], out_hbm.at[first + k], sems.at[k]))
            copies[-1].start()
    for copy in copies:
        copy.wait()


def call(
    kernel, out_shape, scratch, operands, specs=None, outs=None, flops=0, limit=0,
    grid=(1,),
):
    whole = pl.BlockSpec(memory_space=pltpu.VMEM)
    specs = specs or {}
    moved = sum(o.size * o.dtype.itemsize for o in operands)
    moved += sum(o.size * o.dtype.itemsize for o in out_shape)
    return pl.pallas_call(
        kernel,
        out_shape=out_shape,
        grid=grid,
        in_specs=[specs.get(i, whole) for i in range(len(operands))],
        out_specs=outs or [whole] * len(out_shape),
        scratch_shapes=scratch,
        compiler_params=pltpu.CompilerParams(vmem_limit_bytes=limit or VMEM_LIMIT),
        cost_estimate=pl.CostEstimate(flops=flops, bytes_accessed=moved, transcendentals=0),
    )(*operands)


def per_device(state, coef, new_group, face_lists, lewis):
    groups = lax.axis_size("group")
    members = lax.axis_size("member")
    up = [(i, i + 1) for i in range(members - 1)]
    down = [(i + 1, i) for i in range(members - 1)]
    slots, species, cells = state.shape[2:]
    capacity = slots // groups
    cuts = (species - species // 2, species // 2)
    firsts = (0, cuts[0])
    width = (1 + species) * cells
    middle = (1 + cuts[0]) * cells
    smem = pl.BlockSpec(memory_space=pltpu.SMEM)
    anywhere = pl.BlockSpec(memory_space=pl.ANY)
    head = pl.BlockSpec((slots, cells), lambda i: (0, 0))

    def shape(*dims, dtype=F32):
        return jax.ShapeDtypeStruct(dims, dtype)

    send, lists = call(
        functools.partial(pack_kernel, groups, capacity),
        [shape(slots, width, dtype=BF16), shape(8, slots, dtype=jnp.int32)],
        [
            pltpu.VMEM((1, slots), jnp.int32),
            pltpu.VMEM((FACES, 1, slots), jnp.int32),
            pltpu.VMEM((species, slots, cells), BF16),
            pltpu.VMEM((slots, cells), BF16),
            pltpu.VMEM((slots, width), BF16),
            pltpu.SemaphoreType.DMA((4,)),
            pltpu.SemaphoreType.DMA((2,)),
        ],
        (
            new_group[0],
            jnp.transpose(face_lists[0], (1, 0, 2)),
            jnp.transpose(state[0, 0], (1, 0, 2)),
            coef[0, 0],
        ),
        specs={i: anywhere for i in range(4)},
        outs=[anywhere, pl.BlockSpec(memory_space=pltpu.VMEM)],
        limit=PACK_LIMIT,
        grid=(),
    )
    rows = lax.all_to_all(send, "group", split_axis=0, concat_axis=0, tiled=True)
    lists_lo = lax.ppermute(lists, "member", up)
    lists_hi = lax.ppermute(lists, "member", down)
    pick0, xy_pick, z_pick = call(
        pick_kernel,
        [
            shape(FACES, slots, slots, dtype=BF16),
            shape(2, 4, slots, slots, dtype=BF16),
            shape(2, slots, 2 * slots, dtype=BF16),
        ],
        [],
        (lists, lists_lo, lists_hi),
    )
    rows, pick0, xy_pick, z_pick = lax.optimization_barrier((rows, pick0, xy_pick, z_pick))
    got = [rows[:, :middle], rows[:, middle:]]
    got_lo = [lax.ppermute(part, "member", up) for part in got]
    got_hi = [lax.ppermute(part, "member", down) for part in got]
    coef0, weights0, flat, base, rhs = call(
        own_kernel,
        [
            shape(cells, slots),
            shape(4, cells, slots),
            shape(species, cells, slots, dtype=BF16),
            shape(species, cells, slots),
            shape(species, cells, slots),
        ],
        [pltpu.VMEM((PADDED, slots), F32), pltpu.VMEM((species, PADDED, slots), F32)],
        (lewis, rows, pick0),
        specs={0: smem},
        flops=500_000_000,
    )
    got_lo[0], got_hi[0], coef0, weights0, flat, base, rhs = lax.optimization_barrier(
        (got_lo[0], got_hi[0], coef0, weights0, flat, base, rhs)
    )
    got_lo2 = [lax.ppermute(part, "member", up) for part in got_lo]
    got_hi2 = [lax.ppermute(part, "member", down) for part in got_hi]
    sort, z_natural, z_halves, total0, beside, total, coefs = call(
        prepare_kernel,
        [
            shape(2, slots, 2 * slots, dtype=BF16),
            shape(2, cells, slots),
            shape(2, cells, slots),
            shape(cells, slots),
            shape(2, 5, cells, slots),
            shape(2, cells, slots),
            shape(2, cells, slots),
        ],
        [pltpu.VMEM((2, PADDED, slots), F32), pltpu.VMEM((2, cells, slots), F32)],
        (got_lo[0], got_hi[0], coef0, pick0, weights0, xy_pick, z_pick),
        specs={0: head, 1: head},
        flops=100_000_000,
    )
    inner = [
        call(
            functools.partial(inner_kernel, first),
            [shape(count, cells, slots)] * 4,
            [
                pltpu.VMEM((2, count, PADDED, slots), F32),
                pltpu.VMEM((4, count, cells, slots), F32),
                pltpu.VMEM((count, PADDED, slots), F32),
            ],
            (
                lewis, sort, xy_pick, z_pick, z_halves, total0, beside,
                pick0, weights0, flat, base, rhs, got_lo[c], got_hi[c],
            ),
            specs={0: smem},
            flops=200_000_000 * count,
        )
        for c, (first, count) in enumerate(zip(firsts, cuts))
    ]
    far = call(
        far_kernel,
        [
            shape(2 * slots, 2 * slots, dtype=BF16),
            shape(2, cells, slots),
            shape(2, cells, slots),
            shape(2, 2 * slots, slots, dtype=BF16),
        ],
        [],
        (pick0, z_pick, total, coefs, got_lo2[0], got_hi2[0]),
        specs={4: head, 5: head},
        flops=50_000_000,
    )
    (early,) = call(
        functools.partial(outer_kernel, 0),
        [shape(cuts[0], slots, cells)],
        [],
        (lewis, *far, z_natural, *inner[0], got_lo2[0], got_hi2[0]),
        specs={0: smem},
        flops=100_000_000 * cuts[0],
    )
    (out,) = call(
        functools.partial(outer_kernel, firsts[1]),
        [shape(species, slots, cells)],
        [pltpu.VMEM((cuts[1], slots, cells), F32), pltpu.SemaphoreType.DMA((cuts[1] + 1,))],
        (lewis, *far, z_natural, *inner[1], got_lo2[1], got_hi2[1], early),
        specs={0: smem},
        outs=[anywhere],
        flops=100_000_000 * cuts[1],
    )
    return jnp.transpose(out, (1, 0, 2))[None, None]


def solution(mesh):
    return jax.shard_map(
        per_device,
        mesh=mesh,
        in_specs=(
            P("group", "member", None, None, None),
            P("group", "member", None, None),
            P("group", "member", None),
            P("group", "member", None, None),
            P(),
        ),
        out_specs=P("group", "member", None, None, None),
        check_vma=False,
    )
```

```python
import functools

import jax
import jax.numpy as jnp
from jax import lax
from jax.experimental import pallas as pl
from jax.experimental.pallas import tpu as pltpu
from jax.sharding import PartitionSpec as P

PX = 16
PY = 16
FACES = 6
LANES = 128
HALF = PX // 2
PITCH = PX + 8
F32 = jnp.float32
BF16 = jnp.bfloat16
VMEM_LIMIT = 28 * 1024 * 1024
PACK_LIMIT = 60 * 1024 * 1024


def dot(a, b):
    return jnp.dot(a, b, preferred_element_type=F32)


def dot_first(a, b):
    return lax.dot_general(a, b, (((0,), (0,)), ((), ())), preferred_element_type=F32)


def iota(shape, dim):
    return lax.broadcasted_iota(jnp.int32, shape, dim)


def ones_where(mask):
    return jnp.where(mask, 1.0, 0.0).astype(BF16)


def pack_kernel(groups, capacity, dest_ref, lists_ref, state_ref, coef_ref, send_ref, lists_out):
    species, slots, cells = state_ref.shape
    dest = dest_ref[...]
    onehot = iota((groups, slots), 0) == dest
    earlier = dot(
        ones_where(onehot), ones_where(iota((slots, slots), 0) < iota((slots, slots), 1))
    )
    running = jnp.sum(jnp.where(onehot, earlier, 0.0), axis=0, keepdims=True).astype(jnp.int32)
    position = jnp.where(dest >= 0, dest * capacity + running, -1)
    place = ones_where(iota((slots, slots), 0) == position)
    send_ref[:, :cells] = dot(place, coef_ref[...]).astype(BF16)
    for k in range(species):
        at = slice((k + 1) * cells, (k + 2) * cells)
        send_ref[:, at] = dot(place, state_ref[k]).astype(BF16)
    none = jnp.zeros((1, slots), jnp.int32)
    rows = [lists_ref[f] + 1 for f in range(FACES)] + [none] * (8 - FACES)
    lists_out[...] = jnp.concatenate(rows, 0)


def sorting(coef_rows):
    slots = coef_rows.shape[0]
    lead = coef_rows[:, :slots].astype(F32)[:, :1]
    valid = jnp.broadcast_to(lead, (slots, slots)) > 0.0
    slot = dot(
        ones_where(iota((slots, slots), 1) < iota((slots, slots), 0)), ones_where(valid)
    ).astype(jnp.int32)
    return ones_where(valid & (slot == iota((slots, slots), 1)))


def picking(entry):
    slots = entry.shape[1]
    return ones_where(iota((slots, slots), 0) == entry)


def diagonal(a, b):
    none = jnp.zeros_like(a)
    return jnp.concatenate(
        [jnp.concatenate([a, none], 1), jnp.concatenate([none, b], 1)], 0
    )


def twice(matrix):
    return jnp.concatenate([matrix, matrix], 0)


def split(field):
    high = field.astype(BF16)
    low = (field - high.astype(F32)).astype(BF16)
    return jnp.concatenate([high, low], 1)


PADDED = (PY + 2) * PITCH


def row(y):
    return (y + 1) * PITCH + PITCH - PX


def step(start):
    return pl.ds(start, HALF, stride=2)


def natural(y, odd):
    return step(y * PX + odd)


def halves(y, odd):
    return slice(y * PX + odd * HALF, y * PX + (odd + 1) * HALF)


def put(padded, field):
    for y in range(PY):
        padded[row(y) : row(y) + PX] = field[y * PX : (y + 1) * PX]


def beside_xy(padded, y, odd):
    at = row(y) + odd
    return [padded[step(at + shift)] for shift in (-1, 1, -PITCH, PITCH)]


def weighted(weights, values):
    flow = weights[0] * values[0]
    for w, v in zip(weights[1:], values[1:]):
        flow = flow + w * v
    return flow


def fill_edges(picks, fields, exact):
    x_first, x_last = row(0), row(0) + PX - 1
    places = (
        (pl.ds(x_last, PY, stride=PITCH), pl.ds(x_first - 1, PY, stride=PITCH)),
        (pl.ds(x_first, PY, stride=PITCH), pl.ds(x_last + 1, PY, stride=PITCH)),
        (pl.ds(row(PY - 1), PX), pl.ds(row(-1), PX)),
        (pl.ds(row(0), PX), pl.ds(row(PY), PX)),
    )
    for pick, (source, target) in zip(picks, places):
        taken = jnp.concatenate([field[source] for field in fields], 0)
        got = dot(taken.astype(BF16), pick) if exact else dot(split(taken), twice(pick))
        for i, field in enumerate(fields):
            field[target] = got[i * PX : (i + 1) * PX]


def pick_kernel(lists0, lists_lo, lists_hi, pick_ref, xy_pick, z_pick):
    slots = lists0.shape[1]

    def picking(lists, face):
        return ones_where(iota((slots, slots), 0) == lists[face : face + 1] - 1)

    for face in range(FACES):
        pick_ref[face] = picking(lists0, face)
    for d, lists in enumerate((lists_lo, lists_hi)):
        for face in range(4):
            xy_pick[d, face] = picking(lists, face)
    z_pick[0] = jnp.concatenate([picking(lists_lo, 5), picking(lists_hi, 4)], 1)
    z_pick[1] = jnp.concatenate([picking(lists_lo, 4), picking(lists_hi, 5)], 1)


def own_kernel(
    lewis_ref, got, pick_ref,
    coef_ref, weights_ref, flat_ref, base_ref, rhs_ref, coef_pad, field_ref,
):
    species, cells, slots = base_ref.shape
    sort = diagonal(*[sorting(got[:, :cells])] * 2)
    fields = []
    for i in range(0, species + 1, 2):
        j = min(i + 1, species)
        pair = [got[:, k * cells : (k + 1) * cells] for k in (i, j)]
        both = dot_first(jnp.concatenate(pair, 0), sort)
        fields += [both[:, :slots], both[:, slots:]][: j - i + 1]
    coef_ref[...] = fields[0]
    put(coef_pad, fields[0])
    picks = [pick_ref[face] for face in range(4)]
    fill_edges(picks, [coef_pad], True)
    for k in range(species):
        put(field_ref.at[k], fields[k + 1])
        flat_ref[k] = fields[k + 1].astype(BF16)
    fill_edges(picks, [field_ref.at[k] for k in range(species)], True)
    factor = [lewis_ref[k] for k in range(species)]
    for y in range(PY):
        for odd in range(2):
            at = halves(y, odd)
            own = coef_pad[step(row(y) + odd)]
            weights = [0.5 * (own + near) for near in beside_xy(coef_pad, y, odd)]
            for f in range(4):
                weights_ref[f, at] = weights[f]
            for k in range(species):
                field = field_ref[k, step(row(y) + odd)]
                flow = weighted(weights, beside_xy(field_ref.at[k], y, odd))
                base_ref[k, at] = field + factor[k] * flow
                rhs_ref[k, at] = field


def prepare_kernel(
    head_lo, head_hi, coef0, pick0, weights0, xy_pick, z_pick,
    sort_ref, z_natural, z_halves, total0, beside_ref, total_ref, coef_ref, padded, z_ref,
):
    cells, slots = coef0.shape
    for d, head in enumerate((head_lo, head_hi)):
        rows = head[:, :cells]
        sort = sorting(rows)
        both = jnp.concatenate([sort, dot(sort, pick0[4 + d]).astype(BF16)], 1)
        sort_ref[d] = both
        coef = dot_first(rows, both)
        coef_ref[d] = coef[:, :slots]
        put(padded.at[d], coef[:, :slots])
        z_natural[d] = 0.5 * (coef0[...] + coef[:, slots:])
        fill_edges([xy_pick[d, f] for f in range(4)], [padded.at[d]], True)
    near = dot(coef0[...].astype(BF16), z_pick[0])
    z_ref[0] = near[:, :slots]
    z_ref[1] = near[:, slots:]
    for y in range(PY):
        for odd in range(2):
            at = halves(y, odd)
            total = None
            for i in range(2):
                w = z_natural[i, natural(y, odd)]
                z_halves[i, at] = w
                total = w if total is None else total + w
            for f in range(4):
                total = total + weights0[f, at]
            total0[at] = total
            for d in range(2):
                own = padded[d, step(row(y) + odd)]
                near = [*beside_xy(padded.at[d], y, odd), z_ref[d, natural(y, odd)]]
                total = None
                for f in range(5):
                    w = 0.5 * (own + near[f])
                    beside_ref[d, f, at] = w
                    total = w if total is None else total + w
                total_ref[d, natural(y, odd)] = total


def inner_kernel(
    cuts, lewis_ref, sort_ref, xy_pick, z_pick, z_halves, total0, beside_ref,
    pick0, weights0, flat_ref, base_ref, rhs_ref, parts,
    num0, scale0, num_lo, num_hi, field_ref, z_ref, phi_ref,
):
    species, cells, slots = num0.shape
    numbers = (num_lo, num_hi)
    factor = [lewis_ref[k] for k in range(species)]
    for k in range(species):
        gots, first = (parts[0], -1) if k < cuts[0] else (parts[1], cuts[0])
        at = slice((k - first) * cells, (k - first + 1) * cells)
        near = dot(flat_ref[k], z_pick[0])
        for d in range(2):
            both = dot_first(gots[d][:, at], sort_ref[d])
            put(field_ref.at[d, k], both[:, :slots])
            z_ref[d, k] = both[:, slots:]
            z_ref[2 + d, k] = near[:, d * slots : (d + 1) * slots]
    for y in range(PY):
        for odd in range(2):
            at = halves(y, odd)
            weights = [z_halves[i, at] for i in range(2)]
            total = total0[at]
            for k in range(species):
                near = [z_ref[i, k, natural(y, odd)] for i in range(2)]
                number = base_ref[k, at] + factor[k] * weighted(weights, near)
                inverse = 1.0 / (1.0 + factor[k] * total)
                phi_ref[k, step(row(y) + odd)] = number * inverse
                scale0[k, natural(y, odd)] = inverse
    fill_edges([pick0[f] for f in range(4)], [phi_ref.at[k] for k in range(species)], False)
    for d in range(2):
        fill_edges(
            [xy_pick[d, f] for f in range(4)], [field_ref.at[d, k] for k in range(species)], True
        )
    for d in range(2):
        for y in range(PY):
            for odd in range(2):
                at = halves(y, odd)
                weights = [beside_ref[d, f, at] for f in range(5)]
                for k in range(species):
                    near = beside_xy(field_ref.at[d, k], y, odd)
                    near.append(z_ref[2 + d, k, natural(y, odd)])
                    numbers[d][k, natural(y, odd)] = (
                        field_ref[d, k, step(row(y) + odd)] + factor[k] * weighted(weights, near)
                    )
    for y in range(PY):
        for odd in range(2):
            at = halves(y, odd)
            weights = [weights0[f, at] for f in range(4)]
            for k in range(species):
                near = beside_xy(phi_ref.at[k], y, odd)
                inverse = scale0[k, natural(y, odd)]
                number = rhs_ref[k, at] + factor[k] * weighted(weights, near)
                num0[k, natural(y, odd)] = number * inverse
                scale0[k, natural(y, odd)] = factor[k] * inverse


def both_kernel(
    cuts, lewis_ref, got_lo, got_hi, later_lo, later_hi,
    coef0, pick0, weights0, xy_pick, z_pick, flat_ref, base_ref, rhs_ref,
    z_natural, total_ref, coef_ref, num0, scale0, num_lo, num_hi,
    sort_ref, z_halves, total0, beside_ref, padded, near_ref, field_ref, z_ref, phi_ref,
):
    prepare_kernel(
        got_lo, got_hi, coef0, pick0, weights0, xy_pick, z_pick,
        sort_ref, z_natural, z_halves, total0, beside_ref, total_ref, coef_ref, padded, near_ref,
    )
    inner_kernel(
        cuts, lewis_ref, sort_ref, xy_pick, z_pick, z_halves, total0, beside_ref,
        pick0, weights0, flat_ref, base_ref, rhs_ref, ((got_lo, got_hi), (later_lo, later_hi)),
        num0, scale0, num_lo, num_hi, field_ref, z_ref, phi_ref,
    )


def far_kernel(pick0, z_pick, total_ref, coef_ref, head_lo2, head_hi2, far_ref, w_ref, t_ref, two_ref):
    cells = coef_ref.shape[1]
    slots = coef_ref.shape[2]
    rows = [head_lo2[:, :cells], head_hi2[:, :cells]]
    fars = []
    for i in range(2):
        fars.append(dot(sorting(rows[i]), z_pick[1, :, i * slots : (i + 1) * slots]).astype(BF16))
        two_ref[i] = twice(pick0[4 + i])
    far = diagonal(*fars)
    far_ref[...] = far
    near = dot_first(jnp.concatenate(rows, 0), far)
    for i in range(2):
        w = 0.5 * (coef_ref[i] + near[:, i * slots : (i + 1) * slots])
        w_ref[i] = w
        t_ref[i] = total_ref[i] + w


def outer_kernel(
    first, lewis_ref, far_ref, w_ref, t_ref, two_ref, z_natural,
    num0, scale0, num_lo, num_hi, got_lo2, got_hi2, *rest,
):
    if first:
        early, out_hbm, out_ref, sems = rest
    else:
        (out_ref,) = rest
    species, slots, cells = out_ref.shape
    start = got_lo2.shape[1] - species * cells
    numbers = (num_lo, num_hi)
    copies = []
    if first:
        copies.append(
            pltpu.make_async_copy(early, out_hbm.at[:first], sems.at[species])
        )
        copies[-1].start()
    for k in range(species):
        at = slice(start + k * cells, start + (k + 1) * cells)
        factor = lewis_ref[first + k]
        ghosts = dot_first(jnp.concatenate([got_lo2[:, at], got_hi2[:, at]], 0), far_ref[...])
        flow = None
        for i in range(2):
            ghost = ghosts[:, i * slots : (i + 1) * slots]
            phi = (numbers[i][first + k] + factor * (w_ref[i] * ghost)) * (1.0 / (1.0 + factor * t_ref[i]))
            term = z_natural[i] * dot(split(phi), two_ref[i])
            flow = term if flow is None else flow + term
        out_ref[k] = jnp.transpose(num0[first + k] + scale0[first + k] * flow, (1, 0))
        if first:
            copies.append(pltpu.make_async_copy(out_ref.at[k], out_hbm.at[first + k], sems.at[k]))
            copies[-1].start()
    for copy in copies:
        copy.wait()


def first_outer_kernel(
    lewis_ref, pick0, z_pick, total_ref, coef_ref, z_natural, num0, scale0, num_lo, num_hi,
    got_lo2, got_hi2, far_ref, w_ref, t_ref, two_ref, out_ref,
):
    far_kernel(
        pick0, z_pick, total_ref, coef_ref, got_lo2, got_hi2, far_ref, w_ref, t_ref, two_ref
    )
    outer_kernel(
        0, lewis_ref, far_ref, w_ref, t_ref, two_ref, z_natural,
        num0, scale0, num_lo, num_hi, got_lo2, got_hi2, out_ref,
    )


def call(
    kernel, out_shape, scratch, operands, specs=None, outs=None, flops=0, limit=0,
    grid=(1,),
):
    whole = pl.BlockSpec(memory_space=pltpu.VMEM)
    specs = specs or {}
    moved = sum(o.size * o.dtype.itemsize for o in operands)
    moved += sum(o.size * o.dtype.itemsize for o in out_shape)
    return pl.pallas_call(
        kernel,
        out_shape=out_shape,
        grid=grid,
        in_specs=[specs.get(i, whole) for i in range(len(operands))],
        out_specs=outs or [whole] * len(out_shape),
        scratch_shapes=scratch,
        compiler_params=pltpu.CompilerParams(vmem_limit_bytes=limit or VMEM_LIMIT),
        cost_estimate=pl.CostEstimate(flops=flops, bytes_accessed=moved, transcendentals=0),
    )(*operands)


def per_device(state, coef, new_group, face_lists, lewis):
    groups = lax.axis_size("group")
    members = lax.axis_size("member")
    up = [(i, i + 1) for i in range(members - 1)]
    down = [(i + 1, i) for i in range(members - 1)]
    slots, species, cells = state.shape[2:]
    capacity = slots // groups
    cuts = (species - species // 2, species // 2)
    width = (1 + species) * cells
    middle = (1 + cuts[0]) * cells
    smem = pl.BlockSpec(memory_space=pltpu.SMEM)
    anywhere = pl.BlockSpec(memory_space=pl.ANY)

    def shape(*dims, dtype=F32):
        return jax.ShapeDtypeStruct(dims, dtype)

    send, lists = call(
        functools.partial(pack_kernel, groups, capacity),
        [shape(slots, width, dtype=BF16), shape(8, slots, dtype=jnp.int32)],
        [],
        (
            new_group[0],
            jnp.transpose(face_lists[0], (1, 0, 2)),
            jnp.transpose(state[0, 0], (1, 0, 2)),
            coef[0, 0],
        ),
        limit=PACK_LIMIT,
        grid=(),
    )
    rows = lax.all_to_all(send, "group", split_axis=0, concat_axis=0, tiled=True)
    lists_lo = lax.ppermute(lists, "member", up)
    lists_hi = lax.ppermute(lists, "member", down)
    pick0, xy_pick, z_pick = call(
        pick_kernel,
        [
            shape(FACES, slots, slots, dtype=BF16),
            shape(2, 4, slots, slots, dtype=BF16),
            shape(2, slots, 2 * slots, dtype=BF16),
        ],
        [],
        (lists, lists_lo, lists_hi),
    )
    rows, pick0, xy_pick, z_pick = lax.optimization_barrier((rows, pick0, xy_pick, z_pick))
    soon = rows[:, :middle]
    got_lo = [lax.ppermute(soon, "member", up)]
    got_hi = [lax.ppermute(soon, "member", down)]
    coef0, weights0, flat, base, rhs = call(
        own_kernel,
        [
            shape(cells, slots),
            shape(4, cells, slots),
            shape(species, cells, slots, dtype=BF16),
            shape(species, cells, slots),
            shape(species, cells, slots),
        ],
        [pltpu.VMEM((PADDED, slots), F32), pltpu.VMEM((species, PADDED, slots), F32)],
        (lewis, rows, pick0),
        specs={0: smem},
        flops=500_000_000,
    )
    later, coef0, weights0, flat, base, rhs = lax.optimization_barrier(
        (rows[:, middle:], coef0, weights0, flat, base, rhs)
    )
    got_lo.append(lax.ppermute(later, "member", up))
    got_hi.append(lax.ppermute(later, "member", down))
    got_lo2 = [lax.ppermute(part, "member", up) for part in got_lo]
    got_hi2 = [lax.ppermute(part, "member", down) for part in got_hi]

    z_natural, total, coefs, *numbers = call(
        functools.partial(both_kernel, cuts),
        [shape(2, cells, slots)] * 3 + [shape(species, cells, slots)] * 4,
        [
            pltpu.VMEM((2, slots, 2 * slots), BF16),
            pltpu.VMEM((2, cells, slots), F32),
            pltpu.VMEM((cells, slots), F32),
            pltpu.VMEM((2, 5, cells, slots), F32),
            pltpu.VMEM((2, PADDED, slots), F32),
            pltpu.VMEM((2, cells, slots), F32),
            pltpu.VMEM((2, species, PADDED, slots), F32),
            pltpu.VMEM((4, species, cells, slots), F32),
            pltpu.VMEM((species, PADDED, slots), F32),
        ],
        (
            lewis, got_lo[0], got_hi[0], got_lo[1], got_hi[1],
            coef0, pick0, weights0, xy_pick, z_pick, flat, base, rhs,
        ),
        specs={0: smem},
        flops=200_000_000 * species,
    )
    *far, early = call(
        first_outer_kernel,
        [
            shape(2 * slots, 2 * slots, dtype=BF16),
            shape(2, cells, slots),
            shape(2, cells, slots),
            shape(2, 2 * slots, slots, dtype=BF16),
            shape(cuts[0], slots, cells),
        ],
        [],
        (lewis, pick0, z_pick, total, coefs, z_natural, *numbers, got_lo2[0], got_hi2[0]),
        specs={0: smem},
        flops=100_000_000 * cuts[0],
    )
    (out,) = call(
        functools.partial(outer_kernel, cuts[0]),
        [shape(species, slots, cells)],
        [pltpu.VMEM((cuts[1], slots, cells), F32), pltpu.SemaphoreType.DMA((cuts[1] + 1,))],
        (lewis, *far, z_natural, *numbers, got_lo2[1], got_hi2[1], early),
        specs={0: smem},
        outs=[anywhere],
        flops=100_000_000 * cuts[1],
    )
    return jnp.transpose(out, (1, 0, 2))[None, None]


def solution(mesh):
    return jax.shard_map(
        per_device,
        mesh=mesh,
        in_specs=(
            P("group", "member", None, None, None),
            P("group", "member", None, None),
            P("group", "member", None),
            P("group", "member", None, None),
            P(),
        ),
        out_specs=P("group", "member", None, None, None),
        check_vma=False,
    )
```

```python
import functools

import jax
import jax.numpy as jnp
from jax import lax
from jax.experimental import pallas as pl
from jax.experimental.pallas import tpu as pltpu
from jax.sharding import PartitionSpec as P

PX = 16
PY = 16
FACES = 6
LANES = 128
HALF = PX // 2
PITCH = PX + 8
F32 = jnp.float32
BF16 = jnp.bfloat16
VMEM_LIMIT = 28 * 1024 * 1024
PACK_LIMIT = 60 * 1024 * 1024


def dot(a, b):
    return jnp.dot(a, b, preferred_element_type=F32)


def dot_first(a, b):
    return lax.dot_general(a, b, (((0,), (0,)), ((), ())), preferred_element_type=F32)


def iota(shape, dim):
    return lax.broadcasted_iota(jnp.int32, shape, dim)


def ones_where(mask):
    return jnp.where(mask, 1.0, 0.0).astype(BF16)


def pack_kernel(groups, capacity, dest_ref, lists_ref, state_ref, coef_ref, send_ref, lists_out):
    species, slots, cells = state_ref.shape
    dest = dest_ref[...]
    onehot = iota((groups, slots), 0) == dest
    earlier = dot(
        ones_where(onehot), ones_where(iota((slots, slots), 0) < iota((slots, slots), 1))
    )
    running = jnp.sum(jnp.where(onehot, earlier, 0.0), axis=0, keepdims=True).astype(jnp.int32)
    position = jnp.where(dest >= 0, dest * capacity + running, -1)
    place = ones_where(iota((slots, slots), 0) == position)
    send_ref[:, :cells] = dot(place, coef_ref[...]).astype(BF16)
    for k in range(species):
        at = slice((k + 1) * cells, (k + 2) * cells)
        send_ref[:, at] = dot(place, state_ref[k]).astype(BF16)
    none = jnp.zeros((1, slots), jnp.int32)
    rows = [lists_ref[f] + 1 for f in range(FACES)] + [none] * (8 - FACES)
    odd = lax.rem(lax.axis_index("group"), 2) == 1
    rows[4], rows[5] = jnp.where(odd, rows[5], rows[4]), jnp.where(odd, rows[4], rows[5])
    lists_out[...] = jnp.concatenate(rows, 0)


def sorting(coef_rows):
    slots = coef_rows.shape[0]
    lead = coef_rows[:, :slots].astype(F32)[:, :1]
    valid = jnp.broadcast_to(lead, (slots, slots)) > 0.0
    slot = dot(
        ones_where(iota((slots, slots), 1) < iota((slots, slots), 0)), ones_where(valid)
    ).astype(jnp.int32)
    return ones_where(valid & (slot == iota((slots, slots), 1)))


def picking(entry):
    slots = entry.shape[1]
    return ones_where(iota((slots, slots), 0) == entry)


def diagonal(a, b):
    none = jnp.zeros_like(a)
    return jnp.concatenate(
        [jnp.concatenate([a, none], 1), jnp.concatenate([none, b], 1)], 0
    )


def twice(matrix):
    return jnp.concatenate([matrix, matrix], 0)


def split(field):
    high = field.astype(BF16)
    low = (field - high.astype(F32)).astype(BF16)
    return jnp.concatenate([high, low], 1)


PADDED = (PY + 2) * PITCH


def row(y):
    return (y + 1) * PITCH + PITCH - PX


def step(start):
    return pl.ds(start, HALF, stride=2)


def natural(y, odd):
    return step(y * PX + odd)


def halves(y, odd):
    return slice(y * PX + odd * HALF, y * PX + (odd + 1) * HALF)


def put(padded, field):
    for y in range(PY):
        padded[row(y) : row(y) + PX] = field[y * PX : (y + 1) * PX]


def beside_xy(padded, y, odd):
    at = row(y) + odd
    return [padded[step(at + shift)] for shift in (-1, 1, -PITCH, PITCH)]


def weighted(weights, values):
    flow = weights[0] * values[0]
    for w, v in zip(weights[1:], values[1:]):
        flow = flow + w * v
    return flow


def fill_edges(picks, fields, exact):
    x_first, x_last = row(0), row(0) + PX - 1
    places = (
        (pl.ds(x_last, PY, stride=PITCH), pl.ds(x_first - 1, PY, stride=PITCH)),
        (pl.ds(x_first, PY, stride=PITCH), pl.ds(x_last + 1, PY, stride=PITCH)),
        (pl.ds(row(PY - 1), PX), pl.ds(row(-1), PX)),
        (pl.ds(row(0), PX), pl.ds(row(PY), PX)),
    )
    for pick, (source, target) in zip(picks, places):
        taken = jnp.concatenate([field[source] for field in fields], 0)
        got = dot(taken.astype(BF16), pick) if exact else dot(split(taken), twice(pick))
        for i, field in enumerate(fields):
            field[target] = got[i * PX : (i + 1) * PX]


def pick_kernel(lists0, lists_lo, lists_hi, pick_ref, xy_pick, z_pick):
    slots = lists0.shape[1]

    def picking(lists, face):
        return ones_where(iota((slots, slots), 0) == lists[face : face + 1] - 1)

    for face in range(FACES):
        pick_ref[face] = picking(lists0, face)
    for d, lists in enumerate((lists_lo, lists_hi)):
        for face in range(4):
            xy_pick[d, face] = picking(lists, face)
    z_pick[0] = jnp.concatenate([picking(lists_lo, 5), picking(lists_hi, 4)], 1)
    z_pick[1] = jnp.concatenate([picking(lists_lo, 4), picking(lists_hi, 5)], 1)


def own_kernel(
    lewis_ref, got, pick_ref,
    coef_ref, weights_ref, flat_ref, base_ref, rhs_ref, coef_pad, field_ref,
):
    species, cells, slots = base_ref.shape
    sort = diagonal(*[sorting(got[:, :cells])] * 2)
    fields = []
    for i in range(0, species + 1, 2):
        j = min(i + 1, species)
        pair = [got[:, k * cells : (k + 1) * cells] for k in (i, j)]
        both = dot_first(jnp.concatenate(pair, 0), sort)
        fields += [both[:, :slots], both[:, slots:]][: j - i + 1]
    coef_ref[...] = fields[0]
    put(coef_pad, fields[0])
    picks = [pick_ref[face] for face in range(4)]
    fill_edges(picks, [coef_pad], True)
    for k in range(species):
        put(field_ref.at[k], fields[k + 1])
        flat_ref[k] = fields[k + 1].astype(BF16)
    fill_edges(picks, [field_ref.at[k] for k in range(species)], True)
    factor = [lewis_ref[k] for k in range(species)]
    for y in range(PY):
        for odd in range(2):
            at = halves(y, odd)
            own = coef_pad[step(row(y) + odd)]
            weights = [0.5 * (own + near) for near in beside_xy(coef_pad, y, odd)]
            for f in range(4):
                weights_ref[f, at] = weights[f]
            for k in range(species):
                field = field_ref[k, step(row(y) + odd)]
                flow = weighted(weights, beside_xy(field_ref.at[k], y, odd))
                base_ref[k, at] = field + factor[k] * flow
                rhs_ref[k, at] = field


def prepare_kernel(
    head_lo, head_hi, coef0, pick0, weights0, xy_pick, z_pick,
    sort_ref, z_natural, z_halves, total0, beside_ref, total_ref, coef_ref, padded, z_ref,
):
    cells, slots = coef0.shape
    for d, head in enumerate((head_lo, head_hi)):
        rows = head[:, :cells]
        sort = sorting(rows)
        both = jnp.concatenate([sort, dot(sort, pick0[4 + d]).astype(BF16)], 1)
        sort_ref[d] = both
        coef = dot_first(rows, both)
        coef_ref[d] = coef[:, :slots]
        put(padded.at[d], coef[:, :slots])
        z_natural[d] = 0.5 * (coef0[...] + coef[:, slots:])
        fill_edges([xy_pick[d, f] for f in range(4)], [padded.at[d]], True)
    near = dot(coef0[...].astype(BF16), z_pick[0])
    z_ref[0] = near[:, :slots]
    z_ref[1] = near[:, slots:]
    for y in range(PY):
        for odd in range(2):
            at = halves(y, odd)
            total = None
            for i in range(2):
                w = z_natural[i, natural(y, odd)]
                z_halves[i, at] = w
                total = w if total is None else total + w
            for f in range(4):
                total = total + weights0[f, at]
            total0[at] = total
            for d in range(2):
                own = padded[d, step(row(y) + odd)]
                near = [*beside_xy(padded.at[d], y, odd), z_ref[d, natural(y, odd)]]
                total = None
                for f in range(5):
                    w = 0.5 * (own + near[f])
                    beside_ref[d, f, at] = w
                    total = w if total is None else total + w
                total_ref[d, natural(y, odd)] = total


def inner_kernel(
    cuts, lewis_ref, sort_ref, xy_pick, z_pick, z_halves, total0, beside_ref,
    pick0, weights0, flat_ref, base_ref, rhs_ref, parts,
    num0, scale0, num_lo, num_hi, field_ref, z_ref, phi_ref,
):
    species, cells, slots = num0.shape
    numbers = (num_lo, num_hi)
    factor = [lewis_ref[k] for k in range(species)]
    for k in range(species):
        gots, first = (parts[0], -1) if k < cuts[0] else (parts[1], cuts[0])
        at = slice((k - first) * cells, (k - first + 1) * cells)
        near = dot(flat_ref[k], z_pick[0])
        for d in range(2):
            both = dot_first(gots[d][:, at], sort_ref[d])
            put(field_ref.at[d, k], both[:, :slots])
            z_ref[d, k] = both[:, slots:]
            z_ref[2 + d, k] = near[:, d * slots : (d + 1) * slots]
    for y in range(PY):
        for odd in range(2):
            at = halves(y, odd)
            weights = [z_halves[i, at] for i in range(2)]
            total = total0[at]
            for k in range(species):
                near = [z_ref[i, k, natural(y, odd)] for i in range(2)]
                number = base_ref[k, at] + factor[k] * weighted(weights, near)
                inverse = 1.0 / (1.0 + factor[k] * total)
                phi_ref[k, step(row(y) + odd)] = number * inverse
                scale0[k, natural(y, odd)] = inverse
    fill_edges([pick0[f] for f in range(4)], [phi_ref.at[k] for k in range(species)], False)
    for d in range(2):
        fill_edges(
            [xy_pick[d, f] for f in range(4)], [field_ref.at[d, k] for k in range(species)], True
        )
    for d in range(2):
        for y in range(PY):
            for odd in range(2):
                at = halves(y, odd)
                weights = [beside_ref[d, f, at] for f in range(5)]
                for k in range(species):
                    near = beside_xy(field_ref.at[d, k], y, odd)
                    near.append(z_ref[2 + d, k, natural(y, odd)])
                    numbers[d][k, natural(y, odd)] = (
                        field_ref[d, k, step(row(y) + odd)] + factor[k] * weighted(weights, near)
                    )
    for y in range(PY):
        for odd in range(2):
            at = halves(y, odd)
            weights = [weights0[f, at] for f in range(4)]
            for k in range(species):
                near = beside_xy(phi_ref.at[k], y, odd)
                inverse = scale0[k, natural(y, odd)]
                number = rhs_ref[k, at] + factor[k] * weighted(weights, near)
                num0[k, natural(y, odd)] = number * inverse
                scale0[k, natural(y, odd)] = factor[k] * inverse


def both_kernel(
    cuts, lewis_ref, got_lo, got_hi, later_lo, later_hi,
    coef0, pick0, weights0, xy_pick, z_pick, flat_ref, base_ref, rhs_ref,
    z_natural, total_ref, coef_ref, num0, scale0, num_lo, num_hi,
    sort_ref, z_halves, total0, beside_ref, padded, near_ref, field_ref, z_ref, phi_ref,
):
    prepare_kernel(
        got_lo, got_hi, coef0, pick0, weights0, xy_pick, z_pick,
        sort_ref, z_natural, z_halves, total0, beside_ref, total_ref, coef_ref, padded, near_ref,
    )
    inner_kernel(
        cuts, lewis_ref, sort_ref, xy_pick, z_pick, z_halves, total0, beside_ref,
        pick0, weights0, flat_ref, base_ref, rhs_ref, ((got_lo, got_hi), (later_lo, later_hi)),
        num0, scale0, num_lo, num_hi, field_ref, z_ref, phi_ref,
    )


def far_kernel(pick0, z_pick, total_ref, coef_ref, head_lo2, head_hi2, far_ref, w_ref, t_ref, two_ref):
    cells = coef_ref.shape[1]
    slots = coef_ref.shape[2]
    rows = [head_lo2[:, :cells], head_hi2[:, :cells]]
    fars = []
    for i in range(2):
        fars.append(dot(sorting(rows[i]), z_pick[1, :, i * slots : (i + 1) * slots]).astype(BF16))
        two_ref[i] = twice(pick0[4 + i])
    far = diagonal(*fars)
    far_ref[...] = far
    near = dot_first(jnp.concatenate(rows, 0), far)
    for i in range(2):
        w = 0.5 * (coef_ref[i] + near[:, i * slots : (i + 1) * slots])
        w_ref[i] = w
        t_ref[i] = total_ref[i] + w


def finish(ghosts, phi_of, two_ref, z_natural, num0, scale0):
    slots = num0.shape[1]
    flow = None
    for i in range(2):
        phi = phi_of(i, ghosts[:, i * slots : (i + 1) * slots])
        term = z_natural[i] * dot(split(phi), two_ref[i])
        flow = term if flow is None else flow + term
    return jnp.transpose(num0 + scale0 * flow, (1, 0))


def first_outer_kernel(
    lewis_ref, pick0, z_pick, total_ref, coef_ref, z_natural, num0, scale0, num_lo, num_hi,
    got_lo2, got_hi2, far_ref, two_ref, offset_ref, slope_ref, out_hbm,
    w_ref, t_ref, out_ref, sems,
):
    far_kernel(
        pick0, z_pick, total_ref, coef_ref, got_lo2, got_hi2, far_ref, w_ref, t_ref, two_ref
    )
    cut, slots, cells = out_ref.shape
    numbers = (num_lo, num_hi)
    copies = []
    for k in range(cut):
        at = slice((1 + k) * cells, (2 + k) * cells)
        factor = lewis_ref[k]
        ghosts = dot_first(jnp.concatenate([got_lo2[:, at], got_hi2[:, at]], 0), far_ref[...])

        def phi_of(i, ghost):
            number = numbers[i][k] + factor * (w_ref[i] * ghost)
            return number * (1.0 / (1.0 + factor * t_ref[i]))

        out_ref[k] = finish(ghosts, phi_of, two_ref, z_natural, num0[k], scale0[k])
        copies.append(pltpu.make_async_copy(out_ref.at[k], out_hbm.at[k], sems.at[k]))
        copies[-1].start()
    for k in range(cut, num0.shape[0]):
        factor = lewis_ref[k]
        for i in range(2):
            inverse = 1.0 / (1.0 + factor * t_ref[i])
            offset_ref[i, k - cut] = numbers[i][k] * inverse
            slope_ref[i, k - cut] = factor * (w_ref[i] * inverse)
    for copy in copies:
        copy.wait()


def second_outer_kernel(
    far_ref, two_ref, offset_ref, slope_ref, z_natural, num0, scale0, later_lo2, later_hi2, early,
    out_hbm, out_ref, sems,
):
    count, slots, cells = out_ref.shape
    cut = num0.shape[0] - count
    copies = []
    for k in range(count):
        at = slice(k * cells, (k + 1) * cells)
        ghosts = dot_first(jnp.concatenate([later_lo2[:, at], later_hi2[:, at]], 0), far_ref[...])

        def phi_of(i, ghost):
            return offset_ref[i, k] + slope_ref[i, k] * ghost

        out_ref[k] = finish(ghosts, phi_of, two_ref, z_natural, num0[cut + k], scale0[cut + k])
        copies.append(pltpu.make_async_copy(out_ref.at[k], out_hbm.at[cut + k], sems.at[k]))
        copies[-1].start()
    for copy in copies:
        copy.wait()


def call(
    kernel, out_shape, scratch, operands, specs=None, outs=None, flops=0, limit=0,
    grid=(1,), aliases=None,
):
    whole = pl.BlockSpec(memory_space=pltpu.VMEM)
    specs = specs or {}
    moved = sum(o.size * o.dtype.itemsize for o in operands)
    moved += sum(o.size * o.dtype.itemsize for o in out_shape)
    return pl.pallas_call(
        kernel,
        out_shape=out_shape,
        grid=grid,
        in_specs=[specs.get(i, whole) for i in range(len(operands))],
        out_specs=outs or [whole] * len(out_shape),
        scratch_shapes=scratch,
        input_output_aliases=aliases or {},
        compiler_params=pltpu.CompilerParams(vmem_limit_bytes=limit or VMEM_LIMIT),
        cost_estimate=pl.CostEstimate(flops=flops, bytes_accessed=moved, transcendentals=0),
    )(*operands)


def per_device(state, coef, new_group, face_lists, lewis):
    groups = lax.axis_size("group")
    members = lax.axis_size("member")
    along = ("group", "member")
    up = [[(g * members + i, g * members + i + 1) for i in range(members - 1)] for g in range(groups)]
    down = [[(target, source) for source, target in pairs] for pairs in up]
    one = [pair for g in range(groups) for pair in (down if g % 2 else up)[g]]
    two = [pair for g in range(groups) for pair in (up if g % 2 else down)[g]]
    slots, species, cells = state.shape[2:]
    capacity = slots // groups
    cuts = (species - species // 2, species // 2)
    width = (1 + species) * cells
    middle = (1 + cuts[0]) * cells
    smem = pl.BlockSpec(memory_space=pltpu.SMEM)
    anywhere = pl.BlockSpec(memory_space=pl.ANY)

    def shape(*dims, dtype=F32):
        return jax.ShapeDtypeStruct(dims, dtype)

    send, lists = call(
        functools.partial(pack_kernel, groups, capacity),
        [shape(slots, width, dtype=BF16), shape(8, slots, dtype=jnp.int32)],
        [],
        (
            new_group[0],
            jnp.transpose(face_lists[0], (1, 0, 2)),
            jnp.transpose(state[0, 0], (1, 0, 2)),
            coef[0, 0],
        ),
        limit=PACK_LIMIT,
        grid=(),
    )
    rows = lax.all_to_all(send, "group", split_axis=0, concat_axis=0, tiled=True)
    lists_lo = lax.ppermute(lists, along, one)
    lists_hi = lax.ppermute(lists, along, two)
    pick0, xy_pick, z_pick = call(
        pick_kernel,
        [
            shape(FACES, slots, slots, dtype=BF16),
            shape(2, 4, slots, slots, dtype=BF16),
            shape(2, slots, 2 * slots, dtype=BF16),
        ],
        [],
        (lists, lists_lo, lists_hi),
    )
    rows, pick0, xy_pick, z_pick = lax.optimization_barrier((rows, pick0, xy_pick, z_pick))
    soon = rows[:, :middle]
    got_lo = [lax.ppermute(soon, along, one)]
    got_hi = [lax.ppermute(soon, along, two)]
    coef0, weights0, flat, base, rhs = call(
        own_kernel,
        [
            shape(cells, slots),
            shape(4, cells, slots),
            shape(species, cells, slots, dtype=BF16),
            shape(species, cells, slots),
            shape(species, cells, slots),
        ],
        [pltpu.VMEM((PADDED, slots), F32), pltpu.VMEM((species, PADDED, slots), F32)],
        (lewis, rows, pick0),
        specs={0: smem},
        flops=500_000_000,
    )
    later, coef0, weights0, flat, base, rhs = lax.optimization_barrier(
        (rows[:, middle:], coef0, weights0, flat, base, rhs)
    )
    got_lo.append(lax.ppermute(later, along, one))
    got_hi.append(lax.ppermute(later, along, two))
    got_lo2 = [lax.ppermute(part, along, one) for part in got_lo]
    got_hi2 = [lax.ppermute(part, along, two) for part in got_hi]

    z_natural, total, coefs, *numbers = call(
        functools.partial(both_kernel, cuts),
        [shape(2, cells, slots)] * 3 + [shape(species, cells, slots)] * 4,
        [
            pltpu.VMEM((2, slots, 2 * slots), BF16),
            pltpu.VMEM((2, cells, slots), F32),
            pltpu.VMEM((cells, slots), F32),
            pltpu.VMEM((2, 5, cells, slots), F32),
            pltpu.VMEM((2, PADDED, slots), F32),
            pltpu.VMEM((2, cells, slots), F32),
            pltpu.VMEM((2, species, PADDED, slots), F32),
            pltpu.VMEM((4, species, cells, slots), F32),
            pltpu.VMEM((species, PADDED, slots), F32),
        ],
        (
            lewis, got_lo[0], got_hi[0], got_lo[1], got_hi[1],
            coef0, pick0, weights0, xy_pick, z_pick, flat, base, rhs,
        ),
        specs={0: smem},
        flops=200_000_000 * species,
    )
    far, twos, offset, slope, early = call(
        first_outer_kernel,
        [
            shape(2 * slots, 2 * slots, dtype=BF16),
            shape(2, 2 * slots, slots, dtype=BF16),
            shape(2, cuts[1], cells, slots),
            shape(2, cuts[1], cells, slots),
            shape(species, slots, cells),
        ],
        [
            pltpu.VMEM((2, cells, slots), F32),
            pltpu.VMEM((2, cells, slots), F32),
            pltpu.VMEM((cuts[0], slots, cells), F32),
            pltpu.SemaphoreType.DMA((cuts[0],)),
        ],
        (lewis, pick0, z_pick, total, coefs, z_natural, *numbers, got_lo2[0], got_hi2[0]),
        specs={0: smem},
        outs=[pl.BlockSpec(memory_space=pltpu.VMEM)] * 4 + [anywhere],
        flops=100_000_000 * cuts[0],
    )
    (out,) = call(
        second_outer_kernel,
        [shape(species, slots, cells)],
        [pltpu.VMEM((cuts[1], slots, cells), F32), pltpu.SemaphoreType.DMA((cuts[1],))],
        (
            far, twos, offset, slope, z_natural, numbers[0], numbers[1],
            got_lo2[1], got_hi2[1], early,
        ),
        specs={9: anywhere},
        outs=[anywhere],
        aliases={9: 0},
        flops=100_000_000 * cuts[1],
    )
    return jnp.transpose(out, (1, 0, 2))[None, None]


def solution(mesh):
    return jax.shard_map(
        per_device,
        mesh=mesh,
        in_specs=(
            P("group", "member", None, None, None),
            P("group", "member", None, None),
            P("group", "member", None),
            P("group", "member", None, None),
            P(),
        ),
        out_specs=P("group", "member", None, None, None),
        check_vma=False,
    )
```

```python
import functools

import jax
import jax.numpy as jnp
from jax import lax
from jax.experimental import pallas as pl
from jax.experimental.pallas import tpu as pltpu
from jax.sharding import PartitionSpec as P

PX = 16
PY = 16
FACES = 6
LANES = 128
HALF = PX // 2
PITCH = PX + 8
F32 = jnp.float32
BF16 = jnp.bfloat16
VMEM_LIMIT = 28 * 1024 * 1024
PACK_LIMIT = 60 * 1024 * 1024


def dot(a, b):
    return jnp.dot(a, b, preferred_element_type=F32)


def dot_first(a, b):
    return lax.dot_general(a, b, (((0,), (0,)), ((), ())), preferred_element_type=F32)


def iota(shape, dim):
    return lax.broadcasted_iota(jnp.int32, shape, dim)


def ones_where(mask):
    return jnp.where(mask, 1.0, 0.0).astype(BF16)


def pack_kernel(groups, capacity, dest_ref, lists_ref, state_ref, coef_ref, send_ref, lists_out):
    species, slots, cells = state_ref.shape
    dest = dest_ref[...]
    onehot = iota((groups, slots), 0) == dest
    earlier = dot(
        ones_where(onehot), ones_where(iota((slots, slots), 0) < iota((slots, slots), 1))
    )
    running = jnp.sum(jnp.where(onehot, earlier, 0.0), axis=0, keepdims=True).astype(jnp.int32)
    position = jnp.where(dest >= 0, dest * capacity + running, -1)
    place = ones_where(iota((slots, slots), 0) == position)
    send_ref[:, :cells] = dot(place, coef_ref[...]).astype(BF16)
    for k in range(species):
        at = slice((k + 1) * cells, (k + 2) * cells)
        send_ref[:, at] = dot(place, state_ref[k]).astype(BF16)
    none = jnp.zeros((1, slots), jnp.int32)
    rows = [lists_ref[f] + 1 for f in range(FACES)] + [none] * (8 - FACES)
    odd = lax.rem(lax.axis_index("group"), 2) == 1
    rows[4], rows[5] = jnp.where(odd, rows[5], rows[4]), jnp.where(odd, rows[4], rows[5])
    lists_out[...] = jnp.concatenate(rows, 0)


def sorting(coef_rows):
    slots = coef_rows.shape[0]
    lead = coef_rows[:, :slots].astype(F32)[:, :1]
    valid = jnp.broadcast_to(lead, (slots, slots)) > 0.0
    slot = dot(
        ones_where(iota((slots, slots), 1) < iota((slots, slots), 0)), ones_where(valid)
    ).astype(jnp.int32)
    return ones_where(valid & (slot == iota((slots, slots), 1)))


def picking(entry):
    slots = entry.shape[1]
    return ones_where(iota((slots, slots), 0) == entry)


def diagonal(a, b):
    none = jnp.zeros_like(a)
    return jnp.concatenate(
        [jnp.concatenate([a, none], 1), jnp.concatenate([none, b], 1)], 0
    )


def twice(matrix):
    return jnp.concatenate([matrix, matrix], 0)


def split(field):
    high = field.astype(BF16)
    low = (field - high.astype(F32)).astype(BF16)
    return jnp.concatenate([high, low], 1)


PADDED = (PY + 2) * PITCH


def row(y):
    return (y + 1) * PITCH + PITCH - PX


def step(start):
    return pl.ds(start, HALF, stride=2)


def natural(y, odd):
    return step(y * PX + odd)


def halves(y, odd):
    return slice(y * PX + odd * HALF, y * PX + (odd + 1) * HALF)


def put(padded, field):
    for y in range(PY):
        padded[row(y) : row(y) + PX] = field[y * PX : (y + 1) * PX]


def beside_xy(padded, y, odd):
    at = row(y) + odd
    return [padded[step(at + shift)] for shift in (-1, 1, -PITCH, PITCH)]


def weighted(weights, values):
    flow = weights[0] * values[0]
    for w, v in zip(weights[1:], values[1:]):
        flow = flow + w * v
    return flow


def fill_edges(picks, fields, exact):
    x_first, x_last = row(0), row(0) + PX - 1
    places = (
        (pl.ds(x_last, PY, stride=PITCH), pl.ds(x_first - 1, PY, stride=PITCH)),
        (pl.ds(x_first, PY, stride=PITCH), pl.ds(x_last + 1, PY, stride=PITCH)),
        (pl.ds(row(PY - 1), PX), pl.ds(row(-1), PX)),
        (pl.ds(row(0), PX), pl.ds(row(PY), PX)),
    )
    for pick, (source, target) in zip(picks, places):
        taken = jnp.concatenate([field[source] for field in fields], 0)
        got = dot(taken.astype(BF16), pick) if exact else dot(split(taken), twice(pick))
        for i, field in enumerate(fields):
            field[target] = got[i * PX : (i + 1) * PX]


def pick_kernel(lists0, lists_lo, lists_hi, pick_ref, xy_pick, z_pick):
    slots = lists0.shape[1]

    def picking(lists, face):
        return ones_where(iota((slots, slots), 0) == lists[face : face + 1] - 1)

    for face in range(FACES):
        pick_ref[face] = picking(lists0, face)
    for d, lists in enumerate((lists_lo, lists_hi)):
        for face in range(4):
            xy_pick[d, face] = picking(lists, face)
    z_pick[0] = jnp.concatenate([picking(lists_lo, 5), picking(lists_hi, 4)], 1)
    z_pick[1] = jnp.concatenate([picking(lists_lo, 4), picking(lists_hi, 5)], 1)


def own_kernel(
    lewis_ref, got, pick_ref,
    coef_ref, weights_ref, flat_ref, base_ref, rhs_ref, coef_pad, field_ref,
):
    species, cells, slots = base_ref.shape
    sort = diagonal(*[sorting(got[:, :cells])] * 2)
    count = (species + 2) // 2
    pair = [got[:, : count * cells], got[:, (species + 1 - count) * cells :]]
    both = dot_first(jnp.concatenate(pair, 0), sort)
    fields = [both[k * cells : (k + 1) * cells, :slots] for k in range(count)]
    fields += [
        both[k * cells : (k + 1) * cells, slots:] for k in range(2 * count - species - 1, count)
    ]
    coef_ref[...] = fields[0]
    put(coef_pad, fields[0])
    picks = [pick_ref[face] for face in range(4)]
    fill_edges(picks, [coef_pad], True)
    for k in range(species):
        put(field_ref.at[k], fields[k + 1])
        flat_ref[k] = fields[k + 1].astype(BF16)
    fill_edges(picks, [field_ref.at[k] for k in range(species)], True)
    factor = [lewis_ref[k] for k in range(species)]
    for y in range(PY):
        for odd in range(2):
            at = halves(y, odd)
            own = coef_pad[step(row(y) + odd)]
            weights = [0.5 * (own + near) for near in beside_xy(coef_pad, y, odd)]
            for f in range(4):
                weights_ref[f, at] = weights[f]
            for k in range(species):
                field = field_ref[k, step(row(y) + odd)]
                flow = weighted(weights, beside_xy(field_ref.at[k], y, odd))
                base_ref[k, at] = field + factor[k] * flow
                rhs_ref[k, at] = field


def prepare_kernel(
    head_lo, head_hi, coef0, pick0, weights0, xy_pick, z_pick,
    sort_ref, z_natural, z_halves, total0, beside_ref, total_ref, coef_ref, padded, z_ref,
):
    cells, slots = coef0.shape
    for d, head in enumerate((head_lo, head_hi)):
        rows = head[:, :cells]
        sort = sorting(rows)
        both = jnp.concatenate([sort, dot(sort, pick0[4 + d]).astype(BF16)], 1)
        sort_ref[d] = both
        coef = dot_first(rows, both)
        coef_ref[d] = coef[:, :slots]
        put(padded.at[d], coef[:, :slots])
        z_natural[d] = 0.5 * (coef0[...] + coef[:, slots:])
        fill_edges([xy_pick[d, f] for f in range(4)], [padded.at[d]], True)
    near = dot(coef0[...].astype(BF16), z_pick[0])
    z_ref[0] = near[:, :slots]
    z_ref[1] = near[:, slots:]
    for y in range(PY):
        for odd in range(2):
            at = halves(y, odd)
            total = None
            for i in range(2):
                w = z_natural[i, natural(y, odd)]
                z_halves[i, at] = w
                total = w if total is None else total + w
            for f in range(4):
                total = total + weights0[f, at]
            total0[at] = total
            for d in range(2):
                own = padded[d, step(row(y) + odd)]
                near = [*beside_xy(padded.at[d], y, odd), z_ref[d, natural(y, odd)]]
                total = None
                for f in range(5):
                    w = 0.5 * (own + near[f])
                    beside_ref[d, f, at] = w
                    total = w if total is None else total + w
                total_ref[d, natural(y, odd)] = total


def inner_kernel(
    cuts, lewis_ref, sort_ref, xy_pick, z_pick, z_halves, total0, beside_ref,
    pick0, weights0, flat_ref, base_ref, rhs_ref, parts,
    num0, scale0, num_lo, num_hi, field_ref, z_ref, phi_ref,
):
    species, cells, slots = num0.shape
    numbers = (num_lo, num_hi)
    factor = [lewis_ref[k] for k in range(species)]
    for d in range(2):
        k = 0
        for gots, skip, count in zip(parts, (cells, 0), cuts):
            both = dot_first(gots[d][:, skip:], sort_ref[d])
            for i in range(count):
                rows = slice(i * cells, (i + 1) * cells)
                put(field_ref.at[d, k], both[rows, :slots])
                z_ref[d, k] = both[rows, slots:]
                k += 1
    near = dot(flat_ref[...].reshape(species * cells, slots), z_pick[0])
    for k in range(species):
        for d in range(2):
            z_ref[2 + d, k] = near[k * cells : (k + 1) * cells, d * slots : (d + 1) * slots]
    for d in range(2):
        fill_edges(
            [xy_pick[d, f] for f in range(4)], [field_ref.at[d, k] for k in range(species)], True
        )
    for y in range(PY):
        for odd in range(2):
            at = halves(y, odd)
            weights = [z_halves[i, at] for i in range(2)]
            total = total0[at]
            for k in range(species):
                near = [z_ref[i, k, natural(y, odd)] for i in range(2)]
                number = base_ref[k, at] + factor[k] * weighted(weights, near)
                inverse = 1.0 / (1.0 + factor[k] * total)
                phi_ref[k, step(row(y) + odd)] = number * inverse
                scale0[k, natural(y, odd)] = inverse
    fill_edges([pick0[f] for f in range(4)], [phi_ref.at[k] for k in range(species)], False)
    for d in range(2):
        for y in range(PY):
            for odd in range(2):
                at = halves(y, odd)
                weights = [beside_ref[d, f, at] for f in range(5)]
                for k in range(species):
                    near = beside_xy(field_ref.at[d, k], y, odd)
                    near.append(z_ref[2 + d, k, natural(y, odd)])
                    numbers[d][k, natural(y, odd)] = (
                        field_ref[d, k, step(row(y) + odd)] + factor[k] * weighted(weights, near)
                    )
    for y in range(PY):
        for odd in range(2):
            at = halves(y, odd)
            weights = [weights0[f, at] for f in range(4)]
            for k in range(species):
                near = beside_xy(phi_ref.at[k], y, odd)
                inverse = scale0[k, natural(y, odd)]
                number = rhs_ref[k, at] + factor[k] * weighted(weights, near)
                num0[k, natural(y, odd)] = number * inverse
                scale0[k, natural(y, odd)] = factor[k] * inverse


def both_kernel(
    cuts, lewis_ref, got_lo, got_hi, later_lo, later_hi,
    coef0, pick0, weights0, xy_pick, z_pick, flat_ref, base_ref, rhs_ref,
    z_natural, total_ref, coef_ref, num0, scale0, num_lo, num_hi,
    sort_ref, z_halves, total0, beside_ref, padded, near_ref, field_ref, z_ref, phi_ref,
):
    prepare_kernel(
        got_lo, got_hi, coef0, pick0, weights0, xy_pick, z_pick,
        sort_ref, z_natural, z_halves, total0, beside_ref, total_ref, coef_ref, padded, near_ref,
    )
    inner_kernel(
        cuts, lewis_ref, sort_ref, xy_pick, z_pick, z_halves, total0, beside_ref,
        pick0, weights0, flat_ref, base_ref, rhs_ref, ((got_lo, got_hi), (later_lo, later_hi)),
        num0, scale0, num_lo, num_hi, field_ref, z_ref, phi_ref,
    )


def far_kernel(pick0, z_pick, total_ref, coef_ref, head_lo2, head_hi2, far_ref, w_ref, t_ref, two_ref):
    cells = coef_ref.shape[1]
    slots = coef_ref.shape[2]
    rows = [head_lo2[:, :cells], head_hi2[:, :cells]]
    fars = []
    for i in range(2):
        fars.append(dot(sorting(rows[i]), z_pick[1, :, i * slots : (i + 1) * slots]).astype(BF16))
        two_ref[i] = twice(pick0[4 + i])
    far = diagonal(*fars)
    far_ref[...] = far
    near = dot_first(jnp.concatenate(rows, 0), far)
    for i in range(2):
        w = 0.5 * (coef_ref[i] + near[:, i * slots : (i + 1) * slots])
        w_ref[i] = w
        t_ref[i] = total_ref[i] + w


def finish(ghosts, phi_of, two_ref, z_natural, num0, scale0, first, out_ref):
    count, slots, cells = out_ref.shape
    terms = []
    for i in range(2):
        phis = [
            split(phi_of(k, i, ghosts[k * cells : (k + 1) * cells, i * slots : (i + 1) * slots]))
            for k in range(count)
        ]
        terms.append(dot(jnp.concatenate(phis, 0), two_ref[i]))
    for k in range(count):
        rows = slice(k * cells, (k + 1) * cells)
        flow = z_natural[0] * terms[0][rows] + z_natural[1] * terms[1][rows]
        out_ref[k] = jnp.transpose(num0[first + k] + scale0[first + k] * flow, (1, 0))
        yield k


def first_outer_kernel(
    lewis_ref, pick0, z_pick, total_ref, coef_ref, z_natural, num0, scale0, num_lo, num_hi,
    got_lo2, got_hi2, far_ref, two_ref, offset_ref, slope_ref, out_ref, w_ref, t_ref,
):
    far_kernel(
        pick0, z_pick, total_ref, coef_ref, got_lo2, got_hi2, far_ref, w_ref, t_ref, two_ref
    )
    cut, slots, cells = out_ref.shape
    numbers = (num_lo, num_hi)
    factor = [lewis_ref[k] for k in range(num0.shape[0])]
    ghosts = dot_first(
        jnp.concatenate([got_lo2[:, cells:], got_hi2[:, cells:]], 0), far_ref[...]
    )

    def phi_of(k, i, ghost):
        number = numbers[i][k] + factor[k] * (w_ref[i] * ghost)
        return number * (1.0 / (1.0 + factor[k] * t_ref[i]))

    for k in finish(ghosts, phi_of, two_ref, z_natural, num0, scale0, 0, out_ref):
        pass
    for k in range(cut, num0.shape[0]):
        for i in range(2):
            inverse = 1.0 / (1.0 + factor[k] * t_ref[i])
            offset_ref[i, k - cut] = numbers[i][k] * inverse
            slope_ref[i, k - cut] = factor[k] * (w_ref[i] * inverse)


def second_outer_kernel(
    far_ref, two_ref, offset_ref, slope_ref, z_natural, num0, scale0, later_lo2, later_hi2, early,
    out_hbm, out_ref, sems,
):
    count, slots, cells = out_ref.shape
    cut = num0.shape[0] - count
    copies = [pltpu.make_async_copy(early, out_hbm.at[:cut], sems.at[count])]
    copies[-1].start()
    ghosts = dot_first(jnp.concatenate([later_lo2[...], later_hi2[...]], 0), far_ref[...])

    def phi_of(k, i, ghost):
        return offset_ref[i, k] + slope_ref[i, k] * ghost

    for k in finish(ghosts, phi_of, two_ref, z_natural, num0, scale0, cut, out_ref):
        copies.append(pltpu.make_async_copy(out_ref.at[k], out_hbm.at[cut + k], sems.at[k]))
        copies[-1].start()
    for copy in copies:
        copy.wait()


def call(
    kernel, out_shape, scratch, operands, specs=None, outs=None, flops=0, limit=0,
    grid=(1,),
):
    whole = pl.BlockSpec(memory_space=pltpu.VMEM)
    specs = specs or {}
    moved = sum(o.size * o.dtype.itemsize for o in operands)
    moved += sum(o.size * o.dtype.itemsize for o in out_shape)
    return pl.pallas_call(
        kernel,
        out_shape=out_shape,
        grid=grid,
        in_specs=[specs.get(i, whole) for i in range(len(operands))],
        out_specs=outs or [whole] * len(out_shape),
        scratch_shapes=scratch,
        compiler_params=pltpu.CompilerParams(vmem_limit_bytes=limit or VMEM_LIMIT),
        cost_estimate=pl.CostEstimate(flops=flops, bytes_accessed=moved, transcendentals=0),
    )(*operands)


def per_device(state, coef, new_group, face_lists, lewis):
    groups = lax.axis_size("group")
    members = lax.axis_size("member")
    along = ("group", "member")
    up = [[(g * members + i, g * members + i + 1) for i in range(members - 1)] for g in range(groups)]
    down = [[(target, source) for source, target in pairs] for pairs in up]
    one = [pair for g in range(groups) for pair in (down if g % 2 else up)[g]]
    two = [pair for g in range(groups) for pair in (up if g % 2 else down)[g]]
    slots, species, cells = state.shape[2:]
    capacity = slots // groups
    cuts = (species - species // 2, species // 2)
    width = (1 + species) * cells
    middle = (1 + cuts[0]) * cells
    smem = pl.BlockSpec(memory_space=pltpu.SMEM)
    anywhere = pl.BlockSpec(memory_space=pl.ANY)

    def shape(*dims, dtype=F32):
        return jax.ShapeDtypeStruct(dims, dtype)

    send, lists = call(
        functools.partial(pack_kernel, groups, capacity),
        [shape(slots, width, dtype=BF16), shape(8, slots, dtype=jnp.int32)],
        [],
        (
            new_group[0],
            jnp.transpose(face_lists[0], (1, 0, 2)),
            jnp.transpose(state[0, 0], (1, 0, 2)),
            coef[0, 0],
        ),
        limit=PACK_LIMIT,
        grid=(),
    )
    rows = lax.all_to_all(send, "group", split_axis=0, concat_axis=0, tiled=True)
    lists_lo = lax.ppermute(lists, along, one)
    lists_hi = lax.ppermute(lists, along, two)
    pick0, xy_pick, z_pick = call(
        pick_kernel,
        [
            shape(FACES, slots, slots, dtype=BF16),
            shape(2, 4, slots, slots, dtype=BF16),
            shape(2, slots, 2 * slots, dtype=BF16),
        ],
        [],
        (lists, lists_lo, lists_hi),
    )
    rows, pick0, xy_pick, z_pick = lax.optimization_barrier((rows, pick0, xy_pick, z_pick))
    soon = rows[:, :middle]
    got_lo = [lax.ppermute(soon, along, one)]
    got_hi = [lax.ppermute(soon, along, two)]
    coef0, weights0, flat, base, rhs = call(
        own_kernel,
        [
            shape(cells, slots),
            shape(4, cells, slots),
            shape(species, cells, slots, dtype=BF16),
            shape(species, cells, slots),
            shape(species, cells, slots),
        ],
        [pltpu.VMEM((PADDED, slots), F32), pltpu.VMEM((species, PADDED, slots), F32)],
        (lewis, rows, pick0),
        specs={0: smem},
        flops=500_000_000,
    )
    later, coef0, weights0, flat, base, rhs = lax.optimization_barrier(
        (rows[:, middle:], coef0, weights0, flat, base, rhs)
    )
    got_lo.append(lax.ppermute(later, along, one))
    got_hi.append(lax.ppermute(later, along, two))
    got_lo2 = [lax.ppermute(part, along, one) for part in got_lo]
    got_hi2 = [lax.ppermute(part, along, two) for part in got_hi]

    z_natural, total, coefs, *numbers = call(
        functools.partial(both_kernel, cuts),
        [shape(2, cells, slots)] * 3 + [shape(species, cells, slots)] * 4,
        [
            pltpu.VMEM((2, slots, 2 * slots), BF16),
            pltpu.VMEM((2, cells, slots), F32),
            pltpu.VMEM((cells, slots), F32),
            pltpu.VMEM((2, 5, cells, slots), F32),
            pltpu.VMEM((2, PADDED, slots), F32),
            pltpu.VMEM((2, cells, slots), F32),
            pltpu.VMEM((2, species, PADDED, slots), F32),
            pltpu.VMEM((4, species, cells, slots), F32),
            pltpu.VMEM((species, PADDED, slots), F32),
        ],
        (
            lewis, got_lo[0], got_hi[0], got_lo[1], got_hi[1],
            coef0, pick0, weights0, xy_pick, z_pick, flat, base, rhs,
        ),
        specs={0: smem},
        flops=200_000_000 * species,
    )
    far, twos, offset, slope, early = call(
        first_outer_kernel,
        [
            shape(2 * slots, 2 * slots, dtype=BF16),
            shape(2, 2 * slots, slots, dtype=BF16),
            shape(2, cuts[1], cells, slots),
            shape(2, cuts[1], cells, slots),
            shape(cuts[0], slots, cells),
        ],
        [pltpu.VMEM((2, cells, slots), F32), pltpu.VMEM((2, cells, slots), F32)],
        (lewis, pick0, z_pick, total, coefs, z_natural, *numbers, got_lo2[0], got_hi2[0]),
        specs={0: smem},
        flops=100_000_000 * cuts[0],
    )
    (out,) = call(
        second_outer_kernel,
        [shape(species, slots, cells)],
        [pltpu.VMEM((cuts[1], slots, cells), F32), pltpu.SemaphoreType.DMA((cuts[1] + 1,))],
        (
            far, twos, offset, slope, z_natural, numbers[0], numbers[1],
            got_lo2[1], got_hi2[1], early,
        ),
        outs=[anywhere],
        flops=100_000_000 * cuts[1],
    )
    return jnp.transpose(out, (1, 0, 2))[None, None]


def solution(mesh):
    return jax.shard_map(
        per_device,
        mesh=mesh,
        in_specs=(
            P("group", "member", None, None, None),
            P("group", "member", None, None),
            P("group", "member", None),
            P("group", "member", None, None),
            P(),
        ),
        out_specs=P("group", "member", None, None, None),
        check_vma=False,
    )
```

```python
import functools

import jax
import jax.numpy as jnp
from jax import lax
from jax.experimental import pallas as pl
from jax.experimental.pallas import tpu as pltpu
from jax.sharding import PartitionSpec as P

PX = 16
PY = 16
FACES = 6
LANES = 128
HALF = PX // 2
PITCH = PX + 8
F32 = jnp.float32
BF16 = jnp.bfloat16
VMEM_LIMIT = 28 * 1024 * 1024
PACK_LIMIT = 60 * 1024 * 1024


def dot(a, b):
    return jnp.dot(a, b, preferred_element_type=F32)


def dot_first(a, b):
    return lax.dot_general(a, b, (((0,), (0,)), ((), ())), preferred_element_type=F32)


def iota(shape, dim):
    return lax.broadcasted_iota(jnp.int32, shape, dim)


def ones_where(mask):
    return jnp.where(mask, 1.0, 0.0).astype(BF16)


def pack_kernel(groups, capacity, dest_ref, lists_ref, state_ref, coef_ref, send_ref, lists_out):
    species, slots, cells = state_ref.shape
    dest = dest_ref[...]
    onehot = iota((groups, slots), 0) == dest
    earlier = dot(
        ones_where(onehot), ones_where(iota((slots, slots), 0) < iota((slots, slots), 1))
    )
    running = jnp.sum(jnp.where(onehot, earlier, 0.0), axis=0, keepdims=True).astype(jnp.int32)
    position = jnp.where(dest >= 0, dest * capacity + running, -1)
    place = ones_where(iota((slots, slots), 0) == position)
    send_ref[:, :cells] = dot(place, coef_ref[...]).astype(BF16)
    for k in range(species):
        at = slice((k + 1) * cells, (k + 2) * cells)
        send_ref[:, at] = dot(place, state_ref[k]).astype(BF16)
    none = jnp.zeros((1, slots), jnp.int32)
    rows = [lists_ref[f] + 1 for f in range(FACES)] + [none] * (8 - FACES)
    odd = lax.rem(lax.axis_index("group"), 2) == 1
    rows[4], rows[5] = jnp.where(odd, rows[5], rows[4]), jnp.where(odd, rows[4], rows[5])
    lists_out[...] = jnp.concatenate(rows, 0)


def sorting(coef_rows):
    slots = coef_rows.shape[0]
    lead = coef_rows[:, :slots].astype(F32)[:, :1]
    valid = jnp.broadcast_to(lead, (slots, slots)) > 0.0
    slot = dot(
        ones_where(iota((slots, slots), 1) < iota((slots, slots), 0)), ones_where(valid)
    ).astype(jnp.int32)
    return ones_where(valid & (slot == iota((slots, slots), 1)))


def picking(entry):
    slots = entry.shape[1]
    return ones_where(iota((slots, slots), 0) == entry)


def diagonal(a, b):
    none = jnp.zeros_like(a)
    return jnp.concatenate(
        [jnp.concatenate([a, none], 1), jnp.concatenate([none, b], 1)], 0
    )


def twice(matrix):
    return jnp.concatenate([matrix, matrix], 0)


def split(field):
    high = field.astype(BF16)
    low = (field - high.astype(F32)).astype(BF16)
    return jnp.concatenate([high, low], 1)


PADDED = (PY + 2) * PITCH


def row(y):
    return (y + 1) * PITCH + PITCH - PX


def step(start):
    return pl.ds(start, HALF, stride=2)


def natural(y, odd):
    return step(y * PX + odd)


def halves(y, odd):
    return slice(y * PX + odd * HALF, y * PX + (odd + 1) * HALF)


def put(padded, field):
    for y in range(PY):
        padded[row(y) : row(y) + PX] = field[y * PX : (y + 1) * PX]


def beside_xy(padded, y, odd):
    at = row(y) + odd
    return [padded[step(at + shift)] for shift in (-1, 1, -PITCH, PITCH)]


def weighted(weights, values):
    flow = weights[0] * values[0]
    for w, v in zip(weights[1:], values[1:]):
        flow = flow + w * v
    return flow


def fill_edges(picks, fields, exact):
    x_first, x_last = row(0), row(0) + PX - 1
    places = (
        (pl.ds(x_last, PY, stride=PITCH), pl.ds(x_first - 1, PY, stride=PITCH)),
        (pl.ds(x_first, PY, stride=PITCH), pl.ds(x_last + 1, PY, stride=PITCH)),
        (pl.ds(row(PY - 1), PX), pl.ds(row(-1), PX)),
        (pl.ds(row(0), PX), pl.ds(row(PY), PX)),
    )
    for pick, (source, target) in zip(picks, places):
        taken = jnp.concatenate([field[source] for field in fields], 0)
        got = dot(taken.astype(BF16), pick) if exact else dot(split(taken), twice(pick))
        for i, field in enumerate(fields):
            field[target] = got[i * PX : (i + 1) * PX]


def pick_kernel(lists0, lists_lo, lists_hi, pick_ref, xy_pick, z_pick):
    slots = lists0.shape[1]

    def picking(lists, face):
        return ones_where(iota((slots, slots), 0) == lists[face : face + 1] - 1)

    for face in range(FACES):
        pick_ref[face] = picking(lists0, face)
    for d, lists in enumerate((lists_lo, lists_hi)):
        for face in range(4):
            xy_pick[d, face] = picking(lists, face)
    z_pick[0] = jnp.concatenate([picking(lists_lo, 5), picking(lists_hi, 4)], 1)
    z_pick[1] = jnp.concatenate([picking(lists_lo, 4), picking(lists_hi, 5)], 1)


def own_kernel(
    lewis_ref, got, pick_ref,
    coef_ref, weights_ref, flat_ref, base_ref, rhs_ref, coef_pad, field_ref,
):
    species, cells, slots = base_ref.shape
    sort = diagonal(*[sorting(got[:, :cells])] * 2)
    count = (species + 2) // 2
    pair = [got[:, : count * cells], got[:, (species + 1 - count) * cells :]]
    both = dot_first(jnp.concatenate(pair, 0), sort)
    fields = [both[k * cells : (k + 1) * cells, :slots] for k in range(count)]
    fields += [
        both[k * cells : (k + 1) * cells, slots:] for k in range(2 * count - species - 1, count)
    ]
    coef_ref[...] = fields[0]
    put(coef_pad, fields[0])
    picks = [pick_ref[face] for face in range(4)]
    fill_edges(picks, [coef_pad], True)
    for k in range(species):
        put(field_ref.at[k], fields[k + 1])
        flat_ref[k] = fields[k + 1].astype(BF16)
    fill_edges(picks, [field_ref.at[k] for k in range(species)], True)
    factor = [lewis_ref[k] for k in range(species)]
    for y in range(PY):
        for odd in range(2):
            at = halves(y, odd)
            own = coef_pad[step(row(y) + odd)]
            weights = [0.5 * (own + near) for near in beside_xy(coef_pad, y, odd)]
            for f in range(4):
                weights_ref[f, at] = weights[f]
            for k in range(species):
                field = field_ref[k, step(row(y) + odd)]
                flow = weighted(weights, beside_xy(field_ref.at[k], y, odd))
                base_ref[k, at] = field + factor[k] * flow
                rhs_ref[k, at] = field


def prepare_kernel(
    head_lo, head_hi, coef0, pick0, weights0, xy_pick, z_pick,
    sort_ref, z_natural, z_halves, total0, beside_ref, total_ref, coef_ref, padded, z_ref,
):
    cells, slots = coef0.shape
    for d, head in enumerate((head_lo, head_hi)):
        rows = head[:, :cells]
        sort = sorting(rows)
        both = jnp.concatenate([sort, dot(sort, pick0[4 + d]).astype(BF16)], 1)
        sort_ref[d] = both
        coef = dot_first(rows, both)
        coef_ref[d] = coef[:, :slots]
        put(padded.at[d], coef[:, :slots])
        z_natural[d] = 0.5 * (coef0[...] + coef[:, slots:])
        fill_edges([xy_pick[d, f] for f in range(4)], [padded.at[d]], True)
    near = dot(coef0[...].astype(BF16), z_pick[0])
    z_ref[0] = near[:, :slots]
    z_ref[1] = near[:, slots:]
    for y in range(PY):
        for odd in range(2):
            at = halves(y, odd)
            total = None
            for i in range(2):
                w = z_natural[i, natural(y, odd)]
                z_halves[i, at] = w
                total = w if total is None else total + w
            for f in range(4):
                total = total + weights0[f, at]
            total0[at] = total
            for d in range(2):
                own = padded[d, step(row(y) + odd)]
                near = [*beside_xy(padded.at[d], y, odd), z_ref[d, natural(y, odd)]]
                total = None
                for f in range(5):
                    w = 0.5 * (own + near[f])
                    beside_ref[d, f, at] = w
                    total = w if total is None else total + w
                total_ref[d, natural(y, odd)] = total


def inner_kernel(
    cuts, lewis_ref, sort_ref, xy_pick, z_pick, z_halves, total0, beside_ref,
    pick0, weights0, flat_ref, base_ref, rhs_ref, parts,
    num0, scale0, num_lo, num_hi, field_ref, z_ref, phi_ref,
):
    species, cells, slots = num0.shape
    numbers = (num_lo, num_hi)
    factor = [lewis_ref[k] for k in range(species)]
    for d in range(2):
        k = 0
        for gots, skip, count in zip(parts, (cells, 0), cuts):
            both = dot_first(gots[d][:, skip:], sort_ref[d])
            for i in range(count):
                rows = slice(i * cells, (i + 1) * cells)
                put(field_ref.at[d, k], both[rows, :slots])
                z_ref[d, k] = both[rows, slots:]
                k += 1
    near = dot(flat_ref[...].reshape(species * cells, slots), z_pick[0])
    for k in range(species):
        for d in range(2):
            z_ref[2 + d, k] = near[k * cells : (k + 1) * cells, d * slots : (d + 1) * slots]
    for d in range(2):
        fill_edges(
            [xy_pick[d, f] for f in range(4)], [field_ref.at[d, k] for k in range(species)], True
        )
    for y in range(PY):
        for odd in range(2):
            at = halves(y, odd)
            weights = [z_halves[i, at] for i in range(2)]
            total = total0[at]
            for k in range(species):
                near = [z_ref[i, k, natural(y, odd)] for i in range(2)]
                number = base_ref[k, at] + factor[k] * weighted(weights, near)
                inverse = 1.0 / (1.0 + factor[k] * total)
                phi_ref[k, step(row(y) + odd)] = number * inverse
                scale0[k, natural(y, odd)] = inverse
    fill_edges([pick0[f] for f in range(4)], [phi_ref.at[k] for k in range(species)], False)
    for d in range(2):
        for y in range(PY):
            for odd in range(2):
                at = halves(y, odd)
                weights = [beside_ref[d, f, at] for f in range(5)]
                for k in range(species):
                    near = beside_xy(field_ref.at[d, k], y, odd)
                    near.append(z_ref[2 + d, k, natural(y, odd)])
                    numbers[d][k, natural(y, odd)] = (
                        field_ref[d, k, step(row(y) + odd)] + factor[k] * weighted(weights, near)
                    )
    for y in range(PY):
        for odd in range(2):
            at = halves(y, odd)
            weights = [weights0[f, at] for f in range(4)]
            for k in range(species):
                near = beside_xy(phi_ref.at[k], y, odd)
                inverse = scale0[k, natural(y, odd)]
                number = rhs_ref[k, at] + factor[k] * weighted(weights, near)
                num0[k, natural(y, odd)] = number * inverse
                scale0[k, natural(y, odd)] = factor[k] * inverse


def both_kernel(
    cuts, lewis_ref, got_lo, got_hi, later_lo, later_hi,
    coef0, pick0, weights0, xy_pick, z_pick, flat_ref, base_ref, rhs_ref,
    z_natural, total_ref, coef_ref, num0, scale0, num_lo, num_hi,
    sort_ref, z_halves, total0, beside_ref, padded, near_ref, field_ref, z_ref, phi_ref,
):
    prepare_kernel(
        got_lo, got_hi, coef0, pick0, weights0, xy_pick, z_pick,
        sort_ref, z_natural, z_halves, total0, beside_ref, total_ref, coef_ref, padded, near_ref,
    )
    inner_kernel(
        cuts, lewis_ref, sort_ref, xy_pick, z_pick, z_halves, total0, beside_ref,
        pick0, weights0, flat_ref, base_ref, rhs_ref, ((got_lo, got_hi), (later_lo, later_hi)),
        num0, scale0, num_lo, num_hi, field_ref, z_ref, phi_ref,
    )


def far_kernel(pick0, z_pick, total_ref, coef_ref, head_lo2, head_hi2, far_ref, w_ref, t_ref, two_ref):
    cells = coef_ref.shape[1]
    slots = coef_ref.shape[2]
    rows = [head_lo2[:, :cells], head_hi2[:, :cells]]
    fars = []
    for i in range(2):
        fars.append(dot(sorting(rows[i]), z_pick[1, :, i * slots : (i + 1) * slots]).astype(BF16))
        two_ref[i] = twice(pick0[4 + i])
    far = diagonal(*fars)
    far_ref[...] = far
    near = dot_first(jnp.concatenate(rows, 0), far)
    for i in range(2):
        w = 0.5 * (coef_ref[i] + near[:, i * slots : (i + 1) * slots])
        w_ref[i] = w
        t_ref[i] = total_ref[i] + w


def finish(ghosts, phi_of, two_ref, z_natural, num0, scale0, first, out_ref):
    count, slots, cells = out_ref.shape
    terms = []
    for i in range(2):
        phis = [
            split(phi_of(k, i, ghosts[k * cells : (k + 1) * cells, i * slots : (i + 1) * slots]))
            for k in range(count)
        ]
        terms.append(dot(jnp.concatenate(phis, 0), two_ref[i]))
    for k in range(count):
        rows = slice(k * cells, (k + 1) * cells)
        flow = z_natural[0] * terms[0][rows] + z_natural[1] * terms[1][rows]
        out_ref[k] = jnp.transpose(num0[first + k] + scale0[first + k] * flow, (1, 0))
        yield k


def first_outer_kernel(
    lewis_ref, pick0, z_pick, total_ref, coef_ref, z_natural, num0, scale0, num_lo, num_hi,
    got_lo2, got_hi2, far_ref, two_ref, offset_ref, slope_ref, out_ref, w_ref, t_ref,
):
    far_kernel(
        pick0, z_pick, total_ref, coef_ref, got_lo2, got_hi2, far_ref, w_ref, t_ref, two_ref
    )
    cut, slots, cells = out_ref.shape
    numbers = (num_lo, num_hi)
    factor = [lewis_ref[k] for k in range(num0.shape[0])]
    ghosts = dot_first(
        jnp.concatenate([got_lo2[:, cells:], got_hi2[:, cells:]], 0), far_ref[...]
    )

    def phi_of(k, i, ghost):
        number = numbers[i][k] + factor[k] * (w_ref[i] * ghost)
        return number * (1.0 / (1.0 + factor[k] * t_ref[i]))

    for k in finish(ghosts, phi_of, two_ref, z_natural, num0, scale0, 0, out_ref):
        pass
    for k in range(cut, num0.shape[0]):
        for i in range(2):
            inverse = 1.0 / (1.0 + factor[k] * t_ref[i])
            offset_ref[i, k - cut] = numbers[i][k] * inverse
            slope_ref[i, k - cut] = factor[k] * (w_ref[i] * inverse)


def second_outer_kernel(
    far_ref, two_ref, offset_ref, slope_ref, z_natural, num0, scale0, later_lo2, later_hi2, early,
    out_hbm, out_ref, sems,
):
    count, slots, cells = out_ref.shape
    cut = num0.shape[0] - count
    copies = [pltpu.make_async_copy(early, out_hbm.at[:cut], sems.at[count])]
    copies[-1].start()
    ghosts = dot_first(jnp.concatenate([later_lo2[...], later_hi2[...]], 0), far_ref[...])

    def phi_of(k, i, ghost):
        return offset_ref[i, k] + slope_ref[i, k] * ghost

    for k in finish(ghosts, phi_of, two_ref, z_natural, num0, scale0, cut, out_ref):
        copies.append(pltpu.make_async_copy(out_ref.at[k], out_hbm.at[cut + k], sems.at[k]))
        copies[-1].start()
    for copy in copies:
        copy.wait()


def call(
    kernel, out_shape, scratch, operands, specs=None, outs=None, flops=0, limit=0,
    grid=(1,),
):
    whole = pl.BlockSpec(memory_space=pltpu.VMEM)
    specs = specs or {}
    moved = sum(o.size * o.dtype.itemsize for o in operands)
    moved += sum(o.size * o.dtype.itemsize for o in out_shape)
    return pl.pallas_call(
        kernel,
        out_shape=out_shape,
        grid=grid,
        in_specs=[specs.get(i, whole) for i in range(len(operands))],
        out_specs=outs or [whole] * len(out_shape),
        scratch_shapes=scratch,
        compiler_params=pltpu.CompilerParams(vmem_limit_bytes=limit or VMEM_LIMIT),
        cost_estimate=pl.CostEstimate(flops=flops, bytes_accessed=moved, transcendentals=0),
    )(*operands)


def per_device(state, coef, new_group, face_lists, lewis):
    groups = lax.axis_size("group")
    members = lax.axis_size("member")
    along = ("group", "member")

    def pairs(upward, ends):
        steps = []
        for g in range(groups):
            for i in range(0 if ends else 1, members if ends else members - 1):
                target = i + 1 if upward == (g % 2 == 0) else i - 1
                if 0 <= target < members:
                    steps.append((g * members + i, g * members + target))
        return steps

    one, two = pairs(True, True), pairs(False, True)
    one_on, two_on = pairs(True, False), pairs(False, False)
    slots, species, cells = state.shape[2:]
    capacity = slots // groups
    cuts = (species - species // 2, species // 2)
    width = (1 + species) * cells
    middle = (1 + cuts[0]) * cells
    smem = pl.BlockSpec(memory_space=pltpu.SMEM)
    anywhere = pl.BlockSpec(memory_space=pl.ANY)

    def shape(*dims, dtype=F32):
        return jax.ShapeDtypeStruct(dims, dtype)

    send, lists = call(
        functools.partial(pack_kernel, groups, capacity),
        [shape(slots, width, dtype=BF16), shape(8, slots, dtype=jnp.int32)],
        [],
        (
            new_group[0],
            jnp.transpose(face_lists[0], (1, 0, 2)),
            jnp.transpose(state[0, 0], (1, 0, 2)),
            coef[0, 0],
        ),
        limit=PACK_LIMIT,
        grid=(),
    )
    rows = lax.all_to_all(send, "group", split_axis=0, concat_axis=0, tiled=True)
    lists_lo = lax.ppermute(lists, along, one)
    lists_hi = lax.ppermute(lists, along, two)
    pick0, xy_pick, z_pick = call(
        pick_kernel,
        [
            shape(FACES, slots, slots, dtype=BF16),
            shape(2, 4, slots, slots, dtype=BF16),
            shape(2, slots, 2 * slots, dtype=BF16),
        ],
        [],
        (lists, lists_lo, lists_hi),
    )
    rows, pick0, xy_pick, z_pick = lax.optimization_barrier((rows, pick0, xy_pick, z_pick))
    soon = rows[:, :middle]
    got_lo = [lax.ppermute(soon, along, one)]
    got_hi = [lax.ppermute(soon, along, two)]
    coef0, weights0, flat, base, rhs = call(
        own_kernel,
        [
            shape(cells, slots),
            shape(4, cells, slots),
            shape(species, cells, slots, dtype=BF16),
            shape(species, cells, slots),
            shape(species, cells, slots),
        ],
        [pltpu.VMEM((PADDED, slots), F32), pltpu.VMEM((species, PADDED, slots), F32)],
        (lewis, rows, pick0),
        specs={0: smem},
        flops=500_000_000,
    )
    later, coef0, weights0, flat, base, rhs = lax.optimization_barrier(
        (rows[:, middle:], coef0, weights0, flat, base, rhs)
    )
    got_lo.append(lax.ppermute(later, along, one))
    got_hi.append(lax.ppermute(later, along, two))
    got_lo2 = [lax.ppermute(part, along, one_on) for part in got_lo]
    got_hi2 = [lax.ppermute(part, along, two_on) for part in got_hi]

    z_natural, total, coefs, *numbers = call(
        functools.partial(both_kernel, cuts),
        [shape(2, cells, slots)] * 3 + [shape(species, cells, slots)] * 4,
        [
            pltpu.VMEM((2, slots, 2 * slots), BF16),
            pltpu.VMEM((2, cells, slots), F32),
            pltpu.VMEM((cells, slots), F32),
            pltpu.VMEM((2, 5, cells, slots), F32),
            pltpu.VMEM((2, PADDED, slots), F32),
            pltpu.VMEM((2, cells, slots), F32),
            pltpu.VMEM((2, species, PADDED, slots), F32),
            pltpu.VMEM((4, species, cells, slots), F32),
            pltpu.VMEM((species, PADDED, slots), F32),
        ],
        (
            lewis, got_lo[0], got_hi[0], got_lo[1], got_hi[1],
            coef0, pick0, weights0, xy_pick, z_pick, flat, base, rhs,
        ),
        specs={0: smem},
        flops=200_000_000 * species,
    )
    far, twos, offset, slope, early = call(
        first_outer_kernel,
        [
            shape(2 * slots, 2 * slots, dtype=BF16),
            shape(2, 2 * slots, slots, dtype=BF16),
            shape(2, cuts[1], cells, slots),
            shape(2, cuts[1], cells, slots),
            shape(cuts[0], slots, cells),
        ],
        [pltpu.VMEM((2, cells, slots), F32), pltpu.VMEM((2, cells, slots), F32)],
        (lewis, pick0, z_pick, total, coefs, z_natural, *numbers, got_lo2[0], got_hi2[0]),
        specs={0: smem},
        flops=100_000_000 * cuts[0],
    )
    (out,) = call(
        second_outer_kernel,
        [shape(species, slots, cells)],
        [pltpu.VMEM((cuts[1], slots, cells), F32), pltpu.SemaphoreType.DMA((cuts[1] + 1,))],
        (
            far, twos, offset, slope, z_natural, numbers[0], numbers[1],
            got_lo2[1], got_hi2[1], early,
        ),
        outs=[anywhere],
        flops=100_000_000 * cuts[1],
    )
    return jnp.transpose(out, (1, 0, 2))[None, None]


def solution(mesh):
    return jax.shard_map(
        per_device,
        mesh=mesh,
        in_specs=(
            P("group", "member", None, None, None),
            P("group", "member", None, None),
            P("group", "member", None),
            P("group", "member", None, None),
            P(),
        ),
        out_specs=P("group", "member", None, None, None),
        check_vma=False,
    )
```

```python
import functools

import jax
import jax.numpy as jnp
from jax import lax
from jax.experimental import pallas as pl
from jax.experimental.pallas import tpu as pltpu
from jax.sharding import PartitionSpec as P

PX = 16
PY = 16
FACES = 6
LANES = 128
HALF = PX // 2
PITCH = PX + 8
F32 = jnp.float32
BF16 = jnp.bfloat16
VMEM_LIMIT = 28 * 1024 * 1024
PACK_LIMIT = 60 * 1024 * 1024


def dot(a, b):
    return jnp.dot(a, b, preferred_element_type=F32)


def dot_first(a, b):
    return lax.dot_general(a, b, (((0,), (0,)), ((), ())), preferred_element_type=F32)


def iota(shape, dim):
    return lax.broadcasted_iota(jnp.int32, shape, dim)


def ones_where(mask):
    return jnp.where(mask, 1.0, 0.0).astype(BF16)


def pack_kernel(groups, capacity, dest_ref, lists_ref, state_ref, coef_ref, send_ref, lists_out):
    species, slots, cells = state_ref.shape
    dest = dest_ref[...]
    onehot = iota((groups, slots), 0) == dest
    earlier = dot(
        ones_where(onehot), ones_where(iota((slots, slots), 0) < iota((slots, slots), 1))
    )
    running = jnp.sum(jnp.where(onehot, earlier, 0.0), axis=0, keepdims=True).astype(jnp.int32)
    position = jnp.where(dest >= 0, dest * capacity + running, -1)
    place = ones_where(iota((slots, slots), 0) == position)
    send_ref[:, :cells] = dot(place, coef_ref[...]).astype(BF16)
    for k in range(species):
        at = slice((k + 1) * cells, (k + 2) * cells)
        send_ref[:, at] = dot(place, state_ref[k]).astype(BF16)
    none = jnp.zeros((1, slots), jnp.int32)
    rows = [lists_ref[f] + 1 for f in range(FACES)] + [none] * (8 - FACES)
    even = lax.rem(lax.axis_index("group"), 2) == 0
    rows[4], rows[5] = jnp.where(even, rows[5], rows[4]), jnp.where(even, rows[4], rows[5])
    lists_out[...] = jnp.concatenate(rows, 0)


def sorting(coef_rows):
    slots = coef_rows.shape[0]
    lead = coef_rows[:, :slots].astype(F32)[:, :1]
    valid = jnp.broadcast_to(lead, (slots, slots)) > 0.0
    slot = dot(
        ones_where(iota((slots, slots), 1) < iota((slots, slots), 0)), ones_where(valid)
    ).astype(jnp.int32)
    return ones_where(valid & (slot == iota((slots, slots), 1)))


def picking(entry):
    slots = entry.shape[1]
    return ones_where(iota((slots, slots), 0) == entry)


def diagonal(a, b):
    none = jnp.zeros_like(a)
    return jnp.concatenate(
        [jnp.concatenate([a, none], 1), jnp.concatenate([none, b], 1)], 0
    )


def twice(matrix):
    return jnp.concatenate([matrix, matrix], 0)


def split(field):
    high = field.astype(BF16)
    low = (field - high.astype(F32)).astype(BF16)
    return jnp.concatenate([high, low], 1)


PADDED = (PY + 2) * PITCH


def row(y):
    return (y + 1) * PITCH + PITCH - PX


def step(start):
    return pl.ds(start, HALF, stride=2)


def natural(y, odd):
    return step(y * PX + odd)


def halves(y, odd):
    return slice(y * PX + odd * HALF, y * PX + (odd + 1) * HALF)


def put(padded, field):
    for y in range(PY):
        padded[row(y) : row(y) + PX] = field[y * PX : (y + 1) * PX]


def beside_xy(padded, y, odd):
    at = row(y) + odd
    return [padded[step(at + shift)] for shift in (-1, 1, -PITCH, PITCH)]


def weighted(weights, values):
    flow = weights[0] * values[0]
    for w, v in zip(weights[1:], values[1:]):
        flow = flow + w * v
    return flow


def fill_edges(picks, fields, exact):
    x_first, x_last = row(0), row(0) + PX - 1
    places = (
        (pl.ds(x_last, PY, stride=PITCH), pl.ds(x_first - 1, PY, stride=PITCH)),
        (pl.ds(x_first, PY, stride=PITCH), pl.ds(x_last + 1, PY, stride=PITCH)),
        (pl.ds(row(PY - 1), PX), pl.ds(row(-1), PX)),
        (pl.ds(row(0), PX), pl.ds(row(PY), PX)),
    )
    for pick, (source, target) in zip(picks, places):
        taken = jnp.concatenate([field[source] for field in fields], 0)
        got = dot(taken.astype(BF16), pick) if exact else dot(split(taken), twice(pick))
        for i, field in enumerate(fields):
            field[target] = got[i * PX : (i + 1) * PX]


def pick_kernel(lists0, lists_lo, lists_hi, pick_ref, xy_pick, z_pick):
    slots = lists0.shape[1]

    def picking(lists, face):
        return ones_where(iota((slots, slots), 0) == lists[face : face + 1] - 1)

    for face in range(FACES):
        pick_ref[face] = picking(lists0, face)
    for d, lists in enumerate((lists_lo, lists_hi)):
        for face in range(4):
            xy_pick[d, face] = picking(lists, face)
    z_pick[0] = jnp.concatenate([picking(lists_lo, 5), picking(lists_hi, 4)], 1)
    z_pick[1] = jnp.concatenate([picking(lists_lo, 4), picking(lists_hi, 5)], 1)


def own_kernel(
    lewis_ref, got, pick_ref,
    coef_ref, weights_ref, flat_ref, base_ref, rhs_ref, coef_pad, field_ref,
):
    species, cells, slots = base_ref.shape
    sort = diagonal(*[sorting(got[:, :cells])] * 2)
    count = (species + 2) // 2
    pair = [got[:, : count * cells], got[:, (species + 1 - count) * cells :]]
    both = dot_first(jnp.concatenate(pair, 0), sort)
    fields = [both[k * cells : (k + 1) * cells, :slots] for k in range(count)]
    fields += [
        both[k * cells : (k + 1) * cells, slots:] for k in range(2 * count - species - 1, count)
    ]
    coef_ref[...] = fields[0]
    put(coef_pad, fields[0])
    picks = [pick_ref[face] for face in range(4)]
    fill_edges(picks, [coef_pad], True)
    for k in range(species):
        put(field_ref.at[k], fields[k + 1])
        flat_ref[k] = fields[k + 1].astype(BF16)
    fill_edges(picks, [field_ref.at[k] for k in range(species)], True)
    factor = [lewis_ref[k] for k in range(species)]
    for y in range(PY):
        for odd in range(2):
            at = halves(y, odd)
            own = coef_pad[step(row(y) + odd)]
            weights = [0.5 * (own + near) for near in beside_xy(coef_pad, y, odd)]
            for f in range(4):
                weights_ref[f, at] = weights[f]
            for k in range(species):
                field = field_ref[k, step(row(y) + odd)]
                flow = weighted(weights, beside_xy(field_ref.at[k], y, odd))
                base_ref[k, at] = field + factor[k] * flow
                rhs_ref[k, at] = field


def prepare_kernel(
    head_lo, head_hi, coef0, pick0, weights0, xy_pick, z_pick,
    sort_ref, z_natural, z_halves, total0, beside_ref, total_ref, coef_ref, padded, z_ref,
):
    cells, slots = coef0.shape
    for d, head in enumerate((head_lo, head_hi)):
        rows = head[:, :cells]
        sort = sorting(rows)
        both = jnp.concatenate([sort, dot(sort, pick0[4 + d]).astype(BF16)], 1)
        sort_ref[d] = both
        coef = dot_first(rows, both)
        coef_ref[d] = coef[:, :slots]
        put(padded.at[d], coef[:, :slots])
        z_natural[d] = 0.5 * (coef0[...] + coef[:, slots:])
        fill_edges([xy_pick[d, f] for f in range(4)], [padded.at[d]], True)
    near = dot(coef0[...].astype(BF16), z_pick[0])
    z_ref[0] = near[:, :slots]
    z_ref[1] = near[:, slots:]
    for y in range(PY):
        for odd in range(2):
            at = halves(y, odd)
            total = None
            for i in range(2):
                w = z_natural[i, natural(y, odd)]
                z_halves[i, at] = w
                total = w if total is None else total + w
            for f in range(4):
                total = total + weights0[f, at]
            total0[at] = total
            for d in range(2):
                own = padded[d, step(row(y) + odd)]
                near = [*beside_xy(padded.at[d], y, odd), z_ref[d, natural(y, odd)]]
                total = None
                for f in range(5):
                    w = 0.5 * (own + near[f])
                    beside_ref[d, f, at] = w
                    total = w if total is None else total + w
                total_ref[d, natural(y, odd)] = total


def inner_kernel(
    cuts, lewis_ref, sort_ref, xy_pick, z_pick, z_halves, total0, beside_ref,
    pick0, weights0, flat_ref, base_ref, rhs_ref, parts,
    num0, scale0, num_lo, num_hi, field_ref, z_ref, phi_ref,
):
    species, cells, slots = num0.shape
    numbers = (num_lo, num_hi)
    factor = [lewis_ref[k] for k in range(species)]
    for d in range(2):
        k = 0
        for gots, skip, count in zip(parts, (cells, 0), cuts):
            both = dot_first(gots[d][:, skip:], sort_ref[d])
            for i in range(count):
                rows = slice(i * cells, (i + 1) * cells)
                put(field_ref.at[d, k], both[rows, :slots])
                z_ref[d, k] = both[rows, slots:]
                k += 1
    near = dot(flat_ref[...].reshape(species * cells, slots), z_pick[0])
    for k in range(species):
        for d in range(2):
            z_ref[2 + d, k] = near[k * cells : (k + 1) * cells, d * slots : (d + 1) * slots]
    for d in range(2):
        fill_edges(
            [xy_pick[d, f] for f in range(4)], [field_ref.at[d, k] for k in range(species)], True
        )
    for y in range(PY):
        for odd in range(2):
            at = halves(y, odd)
            weights = [z_halves[i, at] for i in range(2)]
            total = total0[at]
            for k in range(species):
                near = [z_ref[i, k, natural(y, odd)] for i in range(2)]
                number = base_ref[k, at] + factor[k] * weighted(weights, near)
                inverse = 1.0 / (1.0 + factor[k] * total)
                phi_ref[k, step(row(y) + odd)] = number * inverse
                scale0[k, natural(y, odd)] = inverse
    fill_edges([pick0[f] for f in range(4)], [phi_ref.at[k] for k in range(species)], False)
    for d in range(2):
        for y in range(PY):
            for odd in range(2):
                at = halves(y, odd)
                weights = [beside_ref[d, f, at] for f in range(5)]
                for k in range(species):
                    near = beside_xy(field_ref.at[d, k], y, odd)
                    near.append(z_ref[2 + d, k, natural(y, odd)])
                    numbers[d][k, natural(y, odd)] = (
                        field_ref[d, k, step(row(y) + odd)] + factor[k] * weighted(weights, near)
                    )
    for y in range(PY):
        for odd in range(2):
            at = halves(y, odd)
            weights = [weights0[f, at] for f in range(4)]
            for k in range(species):
                near = beside_xy(phi_ref.at[k], y, odd)
                inverse = scale0[k, natural(y, odd)]
                number = rhs_ref[k, at] + factor[k] * weighted(weights, near)
                num0[k, natural(y, odd)] = number * inverse
                scale0[k, natural(y, odd)] = factor[k] * inverse


def both_kernel(
    cuts, lewis_ref, got_lo, got_hi, later_lo, later_hi,
    coef0, pick0, weights0, xy_pick, z_pick, flat_ref, base_ref, rhs_ref,
    z_natural, total_ref, coef_ref, num0, scale0, num_lo, num_hi,
    sort_ref, z_halves, total0, beside_ref, padded, near_ref, field_ref, z_ref, phi_ref,
):
    prepare_kernel(
        got_lo, got_hi, coef0, pick0, weights0, xy_pick, z_pick,
        sort_ref, z_natural, z_halves, total0, beside_ref, total_ref, coef_ref, padded, near_ref,
    )
    inner_kernel(
        cuts, lewis_ref, sort_ref, xy_pick, z_pick, z_halves, total0, beside_ref,
        pick0, weights0, flat_ref, base_ref, rhs_ref, ((got_lo, got_hi), (later_lo, later_hi)),
        num0, scale0, num_lo, num_hi, field_ref, z_ref, phi_ref,
    )


def far_kernel(pick0, z_pick, total_ref, coef_ref, head_lo2, head_hi2, far_ref, w_ref, t_ref, two_ref):
    cells = coef_ref.shape[1]
    slots = coef_ref.shape[2]
    rows = [head_lo2[:, :cells], head_hi2[:, :cells]]
    fars = []
    for i in range(2):
        fars.append(dot(sorting(rows[i]), z_pick[1, :, i * slots : (i + 1) * slots]).astype(BF16))
        two_ref[i] = twice(pick0[4 + i])
    far = diagonal(*fars)
    far_ref[...] = far
    near = dot_first(jnp.concatenate(rows, 0), far)
    for i in range(2):
        w = 0.5 * (coef_ref[i] + near[:, i * slots : (i + 1) * slots])
        w_ref[i] = w
        t_ref[i] = total_ref[i] + w


def finish(ghosts, phi_of, two_ref, z_natural, num0, scale0, first, out_ref):
    count, slots, cells = out_ref.shape
    terms = []
    for i in range(2):
        phis = [
            split(phi_of(k, i, ghosts[k * cells : (k + 1) * cells, i * slots : (i + 1) * slots]))
            for k in range(count)
        ]
        terms.append(dot(jnp.concatenate(phis, 0), two_ref[i]))
    for k in range(count):
        rows = slice(k * cells, (k + 1) * cells)
        flow = z_natural[0] * terms[0][rows] + z_natural[1] * terms[1][rows]
        out_ref[k] = jnp.transpose(num0[first + k] + scale0[first + k] * flow, (1, 0))
        yield k


def first_outer_kernel(
    lewis_ref, pick0, z_pick, total_ref, coef_ref, z_natural, num0, scale0, num_lo, num_hi,
    got_lo2, got_hi2, far_ref, two_ref, offset_ref, slope_ref, out_ref, w_ref, t_ref,
):
    far_kernel(
        pick0, z_pick, total_ref, coef_ref, got_lo2, got_hi2, far_ref, w_ref, t_ref, two_ref
    )
    cut, slots, cells = out_ref.shape
    numbers = (num_lo, num_hi)
    factor = [lewis_ref[k] for k in range(num0.shape[0])]
    ghosts = dot_first(
        jnp.concatenate([got_lo2[:, cells:], got_hi2[:, cells:]], 0), far_ref[...]
    )

    def phi_of(k, i, ghost):
        number = numbers[i][k] + factor[k] * (w_ref[i] * ghost)
        return number * (1.0 / (1.0 + factor[k] * t_ref[i]))

    for k in finish(ghosts, phi_of, two_ref, z_natural, num0, scale0, 0, out_ref):
        pass
    for k in range(cut, num0.shape[0]):
        for i in range(2):
            inverse = 1.0 / (1.0 + factor[k] * t_ref[i])
            offset_ref[i, k - cut] = numbers[i][k] * inverse
            slope_ref[i, k - cut] = factor[k] * (w_ref[i] * inverse)


def second_outer_kernel(
    far_ref, two_ref, offset_ref, slope_ref, z_natural, num0, scale0, later_lo2, later_hi2, early,
    out_hbm, out_ref, sems,
):
    count, slots, cells = out_ref.shape
    cut = num0.shape[0] - count
    copies = [pltpu.make_async_copy(early, out_hbm.at[:cut], sems.at[count])]
    copies[-1].start()
    ghosts = dot_first(jnp.concatenate([later_lo2[...], later_hi2[...]], 0), far_ref[...])

    def phi_of(k, i, ghost):
        return offset_ref[i, k] + slope_ref[i, k] * ghost

    for k in finish(ghosts, phi_of, two_ref, z_natural, num0, scale0, cut, out_ref):
        copies.append(pltpu.make_async_copy(out_ref.at[k], out_hbm.at[cut + k], sems.at[k]))
        copies[-1].start()
    for copy in copies:
        copy.wait()


def call(
    kernel, out_shape, scratch, operands, specs=None, outs=None, flops=0, limit=0,
    grid=(1,),
):
    whole = pl.BlockSpec(memory_space=pltpu.VMEM)
    specs = specs or {}
    moved = sum(o.size * o.dtype.itemsize for o in operands)
    moved += sum(o.size * o.dtype.itemsize for o in out_shape)
    return pl.pallas_call(
        kernel,
        out_shape=out_shape,
        grid=grid,
        in_specs=[specs.get(i, whole) for i in range(len(operands))],
        out_specs=outs or [whole] * len(out_shape),
        scratch_shapes=scratch,
        compiler_params=pltpu.CompilerParams(vmem_limit_bytes=limit or VMEM_LIMIT),
        cost_estimate=pl.CostEstimate(flops=flops, bytes_accessed=moved, transcendentals=0),
    )(*operands)


def per_device(state, coef, new_group, face_lists, lewis):
    groups = lax.axis_size("group")
    members = lax.axis_size("member")
    along = ("group", "member")

    def pairs(upward, ends):
        steps = []
        for g in range(groups):
            for i in range(0 if ends else 1, members if ends else members - 1):
                target = i + 1 if upward == (g % 2 == 1) else i - 1
                if 0 <= target < members:
                    steps.append((g * members + i, g * members + target))
        return steps

    one, two = pairs(True, True), pairs(False, True)
    one_on, two_on = pairs(True, False), pairs(False, False)
    slots, species, cells = state.shape[2:]
    capacity = slots // groups
    cuts = (species - species // 2, species // 2)
    width = (1 + species) * cells
    middle = (1 + cuts[0]) * cells
    smem = pl.BlockSpec(memory_space=pltpu.SMEM)
    anywhere = pl.BlockSpec(memory_space=pl.ANY)

    def shape(*dims, dtype=F32):
        return jax.ShapeDtypeStruct(dims, dtype)

    send, lists = call(
        functools.partial(pack_kernel, groups, capacity),
        [shape(slots, width, dtype=BF16), shape(8, slots, dtype=jnp.int32)],
        [],
        (
            new_group[0],
            jnp.transpose(face_lists[0], (1, 0, 2)),
            jnp.transpose(state[0, 0], (1, 0, 2)),
            coef[0, 0],
        ),
        limit=PACK_LIMIT,
        grid=(),
    )
    rows = lax.all_to_all(send, "group", split_axis=0, concat_axis=0, tiled=True)
    lists_lo = lax.ppermute(lists, along, one)
    lists_hi = lax.ppermute(lists, along, two)
    pick0, xy_pick, z_pick = call(
        pick_kernel,
        [
            shape(FACES, slots, slots, dtype=BF16),
            shape(2, 4, slots, slots, dtype=BF16),
            shape(2, slots, 2 * slots, dtype=BF16),
        ],
        [],
        (lists, lists_lo, lists_hi),
    )
    rows, pick0, xy_pick, z_pick = lax.optimization_barrier((rows, pick0, xy_pick, z_pick))
    soon = rows[:, :middle]
    got_lo = [lax.ppermute(soon, along, one)]
    got_hi = [lax.ppermute(soon, along, two)]
    coef0, weights0, flat, base, rhs = call(
        own_kernel,
        [
            shape(cells, slots),
            shape(4, cells, slots),
            shape(species, cells, slots, dtype=BF16),
            shape(species, cells, slots),
            shape(species, cells, slots),
        ],
        [pltpu.VMEM((PADDED, slots), F32), pltpu.VMEM((species, PADDED, slots), F32)],
        (lewis, rows, pick0),
        specs={0: smem},
        flops=500_000_000,
    )
    later, coef0, weights0, flat, base, rhs = lax.optimization_barrier(
        (rows[:, middle:], coef0, weights0, flat, base, rhs)
    )
    got_lo.append(lax.ppermute(later, along, one))
    got_hi.append(lax.ppermute(later, along, two))
    got_lo2 = [lax.ppermute(part, along, one_on) for part in got_lo]
    got_hi2 = [lax.ppermute(part, along, two_on) for part in got_hi]

    z_natural, total, coefs, *numbers = call(
        functools.partial(both_kernel, cuts),
        [shape(2, cells, slots)] * 3 + [shape(species, cells, slots)] * 4,
        [
            pltpu.VMEM((2, slots, 2 * slots), BF16),
            pltpu.VMEM((2, cells, slots), F32),
            pltpu.VMEM((cells, slots), F32),
            pltpu.VMEM((2, 5, cells, slots), F32),
            pltpu.VMEM((2, PADDED, slots), F32),
            pltpu.VMEM((2, cells, slots), F32),
            pltpu.VMEM((2, species, PADDED, slots), F32),
            pltpu.VMEM((4, species, cells, slots), F32),
            pltpu.VMEM((species, PADDED, slots), F32),
        ],
        (
            lewis, got_lo[0], got_hi[0], got_lo[1], got_hi[1],
            coef0, pick0, weights0, xy_pick, z_pick, flat, base, rhs,
        ),
        specs={0: smem},
        flops=200_000_000 * species,
    )
    far, twos, offset, slope, early = call(
        first_outer_kernel,
        [
            shape(2 * slots, 2 * slots, dtype=BF16),
            shape(2, 2 * slots, slots, dtype=BF16),
            shape(2, cuts[1], cells, slots),
            shape(2, cuts[1], cells, slots),
            shape(cuts[0], slots, cells),
        ],
        [pltpu.VMEM((2, cells, slots), F32), pltpu.VMEM((2, cells, slots), F32)],
        (lewis, pick0, z_pick, total, coefs, z_natural, *numbers, got_lo2[0], got_hi2[0]),
        specs={0: smem},
        flops=100_000_000 * cuts[0],
    )
    (out,) = call(
        second_outer_kernel,
        [shape(species, slots, cells)],
        [pltpu.VMEM((cuts[1], slots, cells), F32), pltpu.SemaphoreType.DMA((cuts[1] + 1,))],
        (
            far, twos, offset, slope, z_natural, numbers[0], numbers[1],
            got_lo2[1], got_hi2[1], early,
        ),
        outs=[anywhere],
        flops=100_000_000 * cuts[1],
    )
    return jnp.transpose(out, (1, 0, 2))[None, None]


def solution(mesh):
    return jax.shard_map(
        per_device,
        mesh=mesh,
        in_specs=(
            P("group", "member", None, None, None),
            P("group", "member", None, None),
            P("group", "member", None),
            P("group", "member", None, None),
            P(),
        ),
        out_specs=P("group", "member", None, None, None),
        check_vma=False,
    )
```

```python
import functools

import jax
import jax.numpy as jnp
from jax import lax
from jax.experimental import pallas as pl
from jax.experimental.pallas import tpu as pltpu
from jax.sharding import PartitionSpec as P

PX = 16
PY = 16
FACES = 6
LANES = 128
HALF = PX // 2
PITCH = PX + 8
F32 = jnp.float32
BF16 = jnp.bfloat16
VMEM_LIMIT = 28 * 1024 * 1024
PACK_LIMIT = 60 * 1024 * 1024


def dot(a, b):
    return jnp.dot(a, b, preferred_element_type=F32)


def dot_first(a, b):
    return lax.dot_general(a, b, (((0,), (0,)), ((), ())), preferred_element_type=F32)


def iota(shape, dim):
    return lax.broadcasted_iota(jnp.int32, shape, dim)


def ones_where(mask):
    return jnp.where(mask, 1.0, 0.0).astype(BF16)


def pack_kernel(groups, capacity, dest_ref, lists_ref, state_ref, coef_ref, send_ref, lists_out):
    species, slots, cells = state_ref.shape
    dest = dest_ref[...]
    onehot = iota((groups, slots), 0) == dest
    earlier = dot(
        ones_where(onehot), ones_where(iota((slots, slots), 0) < iota((slots, slots), 1))
    )
    running = jnp.sum(jnp.where(onehot, earlier, 0.0), axis=0, keepdims=True).astype(jnp.int32)
    position = jnp.where(dest >= 0, dest * capacity + running, -1)
    place = ones_where(iota((slots, slots), 0) == position)
    send_ref[:, :cells] = dot(place, coef_ref[...]).astype(BF16)
    for k in range(species):
        at = slice((k + 1) * cells, (k + 2) * cells)
        send_ref[:, at] = dot(place, state_ref[k]).astype(BF16)
    none = jnp.zeros((1, slots), jnp.int32)
    rows = [lists_ref[f] + 1 for f in (0, 1, 2, 3, 5, 4)] + [none] * (8 - FACES)
    lists_out[...] = jnp.concatenate(rows, 0)


def sorting(coef_rows):
    slots = coef_rows.shape[0]
    lead = coef_rows[:, :slots].astype(F32)[:, :1]
    valid = jnp.broadcast_to(lead, (slots, slots)) > 0.0
    slot = dot(
        ones_where(iota((slots, slots), 1) < iota((slots, slots), 0)), ones_where(valid)
    ).astype(jnp.int32)
    return ones_where(valid & (slot == iota((slots, slots), 1)))


def picking(entry):
    slots = entry.shape[1]
    return ones_where(iota((slots, slots), 0) == entry)


def diagonal(a, b):
    none = jnp.zeros_like(a)
    return jnp.concatenate(
        [jnp.concatenate([a, none], 1), jnp.concatenate([none, b], 1)], 0
    )


def twice(matrix):
    return jnp.concatenate([matrix, matrix], 0)


def split(field):
    high = field.astype(BF16)
    low = (field - high.astype(F32)).astype(BF16)
    return jnp.concatenate([high, low], 1)


PADDED = (PY + 2) * PITCH


def row(y):
    return (y + 1) * PITCH + PITCH - PX


def step(start):
    return pl.ds(start, HALF, stride=2)


def natural(y, odd):
    return step(y * PX + odd)


def halves(y, odd):
    return slice(y * PX + odd * HALF, y * PX + (odd + 1) * HALF)


def put(padded, field):
    for y in range(PY):
        padded[row(y) : row(y) + PX] = field[y * PX : (y + 1) * PX]


def beside_xy(padded, y, odd):
    at = row(y) + odd
    return [padded[step(at + shift)] for shift in (-1, 1, -PITCH, PITCH)]


def weighted(weights, values):
    flow = weights[0] * values[0]
    for w, v in zip(weights[1:], values[1:]):
        flow = flow + w * v
    return flow


def fill_edges(picks, fields, exact):
    x_first, x_last = row(0), row(0) + PX - 1
    places = (
        (pl.ds(x_last, PY, stride=PITCH), pl.ds(x_first - 1, PY, stride=PITCH)),
        (pl.ds(x_first, PY, stride=PITCH), pl.ds(x_last + 1, PY, stride=PITCH)),
        (pl.ds(row(PY - 1), PX), pl.ds(row(-1), PX)),
        (pl.ds(row(0), PX), pl.ds(row(PY), PX)),
    )
    for pick, (source, target) in zip(picks, places):
        taken = jnp.concatenate([field[source] for field in fields], 0)
        got = dot(taken.astype(BF16), pick) if exact else dot(split(taken), twice(pick))
        for i, field in enumerate(fields):
            field[target] = got[i * PX : (i + 1) * PX]


def pick_kernel(lists0, lists_lo, lists_hi, pick_ref, xy_pick, z_pick):
    slots = lists0.shape[1]

    def picking(lists, face):
        return ones_where(iota((slots, slots), 0) == lists[face : face + 1] - 1)

    for face in range(FACES):
        pick_ref[face] = picking(lists0, face)
    for d, lists in enumerate((lists_lo, lists_hi)):
        for face in range(4):
            xy_pick[d, face] = picking(lists, face)
    z_pick[0] = jnp.concatenate([picking(lists_lo, 5), picking(lists_hi, 4)], 1)
    z_pick[1] = jnp.concatenate([picking(lists_lo, 4), picking(lists_hi, 5)], 1)


def own_kernel(
    lewis_ref, got, pick_ref,
    coef_ref, weights_ref, flat_ref, base_ref, rhs_ref, coef_pad, field_ref,
):
    species, cells, slots = base_ref.shape
    sort = diagonal(*[sorting(got[:, :cells])] * 2)
    count = (species + 2) // 2
    pair = [got[:, : count * cells], got[:, (species + 1 - count) * cells :]]
    both = dot_first(jnp.concatenate(pair, 0), sort)
    fields = [both[k * cells : (k + 1) * cells, :slots] for k in range(count)]
    fields += [
        both[k * cells : (k + 1) * cells, slots:] for k in range(2 * count - species - 1, count)
    ]
    coef_ref[...] = fields[0]
    put(coef_pad, fields[0])
    picks = [pick_ref[face] for face in range(4)]
    fill_edges(picks, [coef_pad], True)
    for k in range(species):
        put(field_ref.at[k], fields[k + 1])
        flat_ref[k] = fields[k + 1].astype(BF16)
    fill_edges(picks, [field_ref.at[k] for k in range(species)], True)
    factor = [lewis_ref[k] for k in range(species)]
    for y in range(PY):
        for odd in range(2):
            at = halves(y, odd)
            own = coef_pad[step(row(y) + odd)]
            weights = [0.5 * (own + near) for near in beside_xy(coef_pad, y, odd)]
            for f in range(4):
                weights_ref[f, at] = weights[f]
            for k in range(species):
                field = field_ref[k, step(row(y) + odd)]
                flow = weighted(weights, beside_xy(field_ref.at[k], y, odd))
                base_ref[k, at] = field + factor[k] * flow
                rhs_ref[k, at] = field


def prepare_kernel(
    head_lo, head_hi, coef0, pick0, weights0, xy_pick, z_pick,
    sort_ref, z_natural, z_halves, total0, beside_ref, total_ref, coef_ref, padded, z_ref,
):
    cells, slots = coef0.shape
    for d, head in enumerate((head_lo, head_hi)):
        rows = head[:, :cells]
        sort = sorting(rows)
        both = jnp.concatenate([sort, dot(sort, pick0[4 + d]).astype(BF16)], 1)
        sort_ref[d] = both
        coef = dot_first(rows, both)
        coef_ref[d] = coef[:, :slots]
        put(padded.at[d], coef[:, :slots])
        z_natural[d] = 0.5 * (coef0[...] + coef[:, slots:])
        fill_edges([xy_pick[d, f] for f in range(4)], [padded.at[d]], True)
    near = dot(coef0[...].astype(BF16), z_pick[0])
    z_ref[0] = near[:, :slots]
    z_ref[1] = near[:, slots:]
    for y in range(PY):
        for odd in range(2):
            at = halves(y, odd)
            total = None
            for i in range(2):
                w = z_natural[i, natural(y, odd)]
                z_halves[i, at] = w
                total = w if total is None else total + w
            for f in range(4):
                total = total + weights0[f, at]
            total0[at] = total
            for d in range(2):
                own = padded[d, step(row(y) + odd)]
                near = [*beside_xy(padded.at[d], y, odd), z_ref[d, natural(y, odd)]]
                total = None
                for f in range(5):
                    w = 0.5 * (own + near[f])
                    beside_ref[d, f, at] = w
                    total = w if total is None else total + w
                total_ref[d, natural(y, odd)] = total


def inner_kernel(
    cuts, lewis_ref, sort_ref, xy_pick, z_pick, z_halves, total0, beside_ref,
    pick0, weights0, flat_ref, base_ref, rhs_ref, parts,
    num0, scale0, num_lo, num_hi, field_ref, z_ref, phi_ref,
):
    species, cells, slots = num0.shape
    numbers = (num_lo, num_hi)
    factor = [lewis_ref[k] for k in range(species)]
    for d in range(2):
        k = 0
        for gots, skip, count in zip(parts, (cells, 0), cuts):
            both = dot_first(gots[d][:, skip:], sort_ref[d])
            for i in range(count):
                rows = slice(i * cells, (i + 1) * cells)
                put(field_ref.at[d, k], both[rows, :slots])
                z_ref[d, k] = both[rows, slots:]
                k += 1
    near = dot(flat_ref[...].reshape(species * cells, slots), z_pick[0])
    for k in range(species):
        for d in range(2):
            z_ref[2 + d, k] = near[k * cells : (k + 1) * cells, d * slots : (d + 1) * slots]
    for d in range(2):
        fill_edges(
            [xy_pick[d, f] for f in range(4)], [field_ref.at[d, k] for k in range(species)], True
        )
    for y in range(PY):
        for odd in range(2):
            at = halves(y, odd)
            weights = [z_halves[i, at] for i in range(2)]
            total = total0[at]
            for k in range(species):
                near = [z_ref[i, k, natural(y, odd)] for i in range(2)]
                number = base_ref[k, at] + factor[k] * weighted(weights, near)
                inverse = 1.0 / (1.0 + factor[k] * total)
                phi_ref[k, step(row(y) + odd)] = number * inverse
                scale0[k, natural(y, odd)] = inverse
    fill_edges([pick0[f] for f in range(4)], [phi_ref.at[k] for k in range(species)], False)
    for d in range(2):
        for y in range(PY):
            for odd in range(2):
                at = halves(y, odd)
                weights = [beside_ref[d, f, at] for f in range(5)]
                for k in range(species):
                    near = beside_xy(field_ref.at[d, k], y, odd)
                    near.append(z_ref[2 + d, k, natural(y, odd)])
                    numbers[d][k, natural(y, odd)] = (
                        field_ref[d, k, step(row(y) + odd)] + factor[k] * weighted(weights, near)
                    )
    for y in range(PY):
        for odd in range(2):
            at = halves(y, odd)
            weights = [weights0[f, at] for f in range(4)]
            for k in range(species):
                near = beside_xy(phi_ref.at[k], y, odd)
                inverse = scale0[k, natural(y, odd)]
                number = rhs_ref[k, at] + factor[k] * weighted(weights, near)
                num0[k, natural(y, odd)] = number * inverse
                scale0[k, natural(y, odd)] = factor[k] * inverse


def both_kernel(
    cuts, lewis_ref, got_lo, got_hi, later_lo, later_hi,
    coef0, pick0, weights0, xy_pick, z_pick, flat_ref, base_ref, rhs_ref,
    z_natural, total_ref, coef_ref, num0, scale0, num_lo, num_hi,
    sort_ref, z_halves, total0, beside_ref, padded, near_ref, field_ref, z_ref, phi_ref,
):
    prepare_kernel(
        got_lo, got_hi, coef0, pick0, weights0, xy_pick, z_pick,
        sort_ref, z_natural, z_halves, total0, beside_ref, total_ref, coef_ref, padded, near_ref,
    )
    inner_kernel(
        cuts, lewis_ref, sort_ref, xy_pick, z_pick, z_halves, total0, beside_ref,
        pick0, weights0, flat_ref, base_ref, rhs_ref, ((got_lo, got_hi), (later_lo, later_hi)),
        num0, scale0, num_lo, num_hi, field_ref, z_ref, phi_ref,
    )


def far_kernel(pick0, z_pick, total_ref, coef_ref, head_lo2, head_hi2, far_ref, w_ref, t_ref, two_ref):
    cells = coef_ref.shape[1]
    slots = coef_ref.shape[2]
    rows = [head_lo2[:, :cells], head_hi2[:, :cells]]
    fars = []
    for i in range(2):
        fars.append(dot(sorting(rows[i]), z_pick[1, :, i * slots : (i + 1) * slots]).astype(BF16))
        two_ref[i] = twice(pick0[4 + i])
    far = diagonal(*fars)
    far_ref[...] = far
    near = dot_first(jnp.concatenate(rows, 0), far)
    for i in range(2):
        w = 0.5 * (coef_ref[i] + near[:, i * slots : (i + 1) * slots])
        w_ref[i] = w
        t_ref[i] = total_ref[i] + w


def finish(ghosts, phi_of, two_ref, z_natural, num0, scale0, first, out_ref):
    count, slots, cells = out_ref.shape
    terms = []
    for i in range(2):
        phis = [
            split(phi_of(k, i, ghosts[k * cells : (k + 1) * cells, i * slots : (i + 1) * slots]))
            for k in range(count)
        ]
        terms.append(dot(jnp.concatenate(phis, 0), two_ref[i]))
    for k in range(count):
        rows = slice(k * cells, (k + 1) * cells)
        flow = z_natural[0] * terms[0][rows] + z_natural[1] * terms[1][rows]
        out_ref[k] = jnp.transpose(num0[first + k] + scale0[first + k] * flow, (1, 0))
        yield k


def first_outer_kernel(
    lewis_ref, pick0, z_pick, total_ref, coef_ref, z_natural, num0, scale0, num_lo, num_hi,
    got_lo2, got_hi2, far_ref, two_ref, offset_ref, slope_ref, out_ref, w_ref, t_ref,
):
    far_kernel(
        pick0, z_pick, total_ref, coef_ref, got_lo2, got_hi2, far_ref, w_ref, t_ref, two_ref
    )
    cut, slots, cells = out_ref.shape
    numbers = (num_lo, num_hi)
    factor = [lewis_ref[k] for k in range(num0.shape[0])]
    ghosts = dot_first(
        jnp.concatenate([got_lo2[:, cells:], got_hi2[:, cells:]], 0), far_ref[...]
    )

    def phi_of(k, i, ghost):
        number = numbers[i][k] + factor[k] * (w_ref[i] * ghost)
        return number * (1.0 / (1.0 + factor[k] * t_ref[i]))

    for k in finish(ghosts, phi_of, two_ref, z_natural, num0, scale0, 0, out_ref):
        pass
    for k in range(cut, num0.shape[0]):
        for i in range(2):
            inverse = 1.0 / (1.0 + factor[k] * t_ref[i])
            offset_ref[i, k - cut] = numbers[i][k] * inverse
            slope_ref[i, k - cut] = factor[k] * (w_ref[i] * inverse)


def second_outer_kernel(
    far_ref, two_ref, offset_ref, slope_ref, z_natural, num0, scale0, later_lo2, later_hi2, early,
    out_hbm, out_ref, sems,
):
    count, slots, cells = out_ref.shape
    cut = num0.shape[0] - count
    copies = [pltpu.make_async_copy(early, out_hbm.at[:cut], sems.at[count])]
    copies[-1].start()
    ghosts = dot_first(jnp.concatenate([later_lo2[...], later_hi2[...]], 0), far_ref[...])

    def phi_of(k, i, ghost):
        return offset_ref[i, k] + slope_ref[i, k] * ghost

    for k in finish(ghosts, phi_of, two_ref, z_natural, num0, scale0, cut, out_ref):
        copies.append(pltpu.make_async_copy(out_ref.at[k], out_hbm.at[cut + k], sems.at[k]))
        copies[-1].start()
    for copy in copies:
        copy.wait()


def call(
    kernel, out_shape, scratch, operands, specs=None, outs=None, flops=0, limit=0,
    grid=(1,),
):
    whole = pl.BlockSpec(memory_space=pltpu.VMEM)
    specs = specs or {}
    moved = sum(o.size * o.dtype.itemsize for o in operands)
    moved += sum(o.size * o.dtype.itemsize for o in out_shape)
    return pl.pallas_call(
        kernel,
        out_shape=out_shape,
        grid=grid,
        in_specs=[specs.get(i, whole) for i in range(len(operands))],
        out_specs=outs or [whole] * len(out_shape),
        scratch_shapes=scratch,
        compiler_params=pltpu.CompilerParams(vmem_limit_bytes=limit or VMEM_LIMIT),
        cost_estimate=pl.CostEstimate(flops=flops, bytes_accessed=moved, transcendentals=0),
    )(*operands)


def per_device(state, coef, new_group, face_lists, lewis):
    groups = lax.axis_size("group")
    members = lax.axis_size("member")
    along = ("group", "member")

    def pairs(shift, ends):
        inside = range(members) if ends else range(1, members - 1)
        return [
            (g * members + i, g * members + i + shift)
            for g in range(groups)
            for i in inside
            if 0 <= i + shift < members
        ]

    one, two = pairs(-1, True), pairs(1, True)
    one_on, two_on = pairs(-1, False), pairs(1, False)
    slots, species, cells = state.shape[2:]
    capacity = slots // groups
    cuts = (species - species // 2, species // 2)
    width = (1 + species) * cells
    middle = (1 + cuts[0]) * cells
    smem = pl.BlockSpec(memory_space=pltpu.SMEM)
    anywhere = pl.BlockSpec(memory_space=pl.ANY)

    def shape(*dims, dtype=F32):
        return jax.ShapeDtypeStruct(dims, dtype)

    send, lists = call(
        functools.partial(pack_kernel, groups, capacity),
        [shape(slots, width, dtype=BF16), shape(8, slots, dtype=jnp.int32)],
        [],
        (
            new_group[0],
            jnp.transpose(face_lists[0], (1, 0, 2)),
            jnp.transpose(state[0, 0], (1, 0, 2)),
            coef[0, 0],
        ),
        limit=PACK_LIMIT,
        grid=(),
    )
    rows = lax.all_to_all(send, "group", split_axis=0, concat_axis=0, tiled=True)
    lists_lo = lax.ppermute(lists, along, one)
    lists_hi = lax.ppermute(lists, along, two)
    pick0, xy_pick, z_pick = call(
        pick_kernel,
        [
            shape(FACES, slots, slots, dtype=BF16),
            shape(2, 4, slots, slots, dtype=BF16),
            shape(2, slots, 2 * slots, dtype=BF16),
        ],
        [],
        (lists, lists_lo, lists_hi),
    )
    rows, pick0, xy_pick, z_pick = lax.optimization_barrier((rows, pick0, xy_pick, z_pick))
    soon = rows[:, :middle]
    got_lo = [lax.ppermute(soon, along, one)]
    got_hi = [lax.ppermute(soon, along, two)]
    coef0, weights0, flat, base, rhs = call(
        own_kernel,
        [
            shape(cells, slots),
            shape(4, cells, slots),
            shape(species, cells, slots, dtype=BF16),
            shape(species, cells, slots),
            shape(species, cells, slots),
        ],
        [pltpu.VMEM((PADDED, slots), F32), pltpu.VMEM((species, PADDED, slots), F32)],
        (lewis, rows, pick0),
        specs={0: smem},
        flops=500_000_000,
    )
    later, coef0, weights0, flat, base, rhs = lax.optimization_barrier(
        (rows[:, middle:], coef0, weights0, flat, base, rhs)
    )
    got_lo.append(lax.ppermute(later, along, one))
    got_hi.append(lax.ppermute(later, along, two))
    got_lo2 = [lax.ppermute(part, along, one_on) for part in got_lo]
    got_hi2 = [lax.ppermute(part, along, two_on) for part in got_hi]

    z_natural, total, coefs, *numbers = call(
        functools.partial(both_kernel, cuts),
        [shape(2, cells, slots)] * 3 + [shape(species, cells, slots)] * 4,
        [
            pltpu.VMEM((2, slots, 2 * slots), BF16),
            pltpu.VMEM((2, cells, slots), F32),
            pltpu.VMEM((cells, slots), F32),
            pltpu.VMEM((2, 5, cells, slots), F32),
            pltpu.VMEM((2, PADDED, slots), F32),
            pltpu.VMEM((2, cells, slots), F32),
            pltpu.VMEM((2, species, PADDED, slots), F32),
            pltpu.VMEM((4, species, cells, slots), F32),
            pltpu.VMEM((species, PADDED, slots), F32),
        ],
        (
            lewis, got_lo[0], got_hi[0], got_lo[1], got_hi[1],
            coef0, pick0, weights0, xy_pick, z_pick, flat, base, rhs,
        ),
        specs={0: smem},
        flops=200_000_000 * species,
    )
    far, twos, offset, slope, early = call(
        first_outer_kernel,
        [
            shape(2 * slots, 2 * slots, dtype=BF16),
            shape(2, 2 * slots, slots, dtype=BF16),
            shape(2, cuts[1], cells, slots),
            shape(2, cuts[1], cells, slots),
            shape(cuts[0], slots, cells),
        ],
        [pltpu.VMEM((2, cells, slots), F32), pltpu.VMEM((2, cells, slots), F32)],
        (lewis, pick0, z_pick, total, coefs, z_natural, *numbers, got_lo2[0], got_hi2[0]),
        specs={0: smem},
        flops=100_000_000 * cuts[0],
    )
    (out,) = call(
        second_outer_kernel,
        [shape(species, slots, cells)],
        [pltpu.VMEM((cuts[1], slots, cells), F32), pltpu.SemaphoreType.DMA((cuts[1] + 1,))],
        (
            far, twos, offset, slope, z_natural, numbers[0], numbers[1],
            got_lo2[1], got_hi2[1], early,
        ),
        outs=[anywhere],
        flops=100_000_000 * cuts[1],
    )
    return jnp.transpose(out, (1, 0, 2))[None, None]


def solution(mesh):
    return jax.shard_map(
        per_device,
        mesh=mesh,
        in_specs=(
            P("group", "member", None, None, None),
            P("group", "member", None, None),
            P("group", "member", None),
            P("group", "member", None, None),
            P(),
        ),
        out_specs=P("group", "member", None, None, None),
        check_vma=False,
    )
```

```python
import functools

import jax
import jax.numpy as jnp
from jax import lax
from jax.experimental import pallas as pl
from jax.experimental.pallas import tpu as pltpu
from jax.sharding import PartitionSpec as P

PX = 16
PY = 16
FACES = 6
LANES = 128
HALF = PX // 2
PITCH = PX + 8
F32 = jnp.float32
BF16 = jnp.bfloat16
VMEM_LIMIT = 28 * 1024 * 1024
PACK_LIMIT = 60 * 1024 * 1024


def dot(a, b):
    return jnp.dot(a, b, preferred_element_type=F32)


def dot_first(a, b):
    return lax.dot_general(a, b, (((0,), (0,)), ((), ())), preferred_element_type=F32)


def iota(shape, dim):
    return lax.broadcasted_iota(jnp.int32, shape, dim)


def ones_where(mask):
    return jnp.where(mask, 1.0, 0.0).astype(BF16)


def up_first(group):
    return group % 4 == 2


def pack_kernel(groups, capacity, dest_ref, lists_ref, state_ref, coef_ref, send_ref, lists_out):
    species, slots, cells = state_ref.shape
    dest = dest_ref[...]
    onehot = iota((groups, slots), 0) == dest
    earlier = dot(
        ones_where(onehot), ones_where(iota((slots, slots), 0) < iota((slots, slots), 1))
    )
    running = jnp.sum(jnp.where(onehot, earlier, 0.0), axis=0, keepdims=True).astype(jnp.int32)
    position = jnp.where(dest >= 0, dest * capacity + running, -1)
    place = ones_where(iota((slots, slots), 0) == position)
    send_ref[:, :cells] = dot(place, coef_ref[...]).astype(BF16)
    for k in range(species):
        at = slice((k + 1) * cells, (k + 2) * cells)
        send_ref[:, at] = dot(place, state_ref[k]).astype(BF16)
    none = jnp.zeros((1, slots), jnp.int32)
    rows = [lists_ref[f] + 1 for f in range(FACES)] + [none] * (8 - FACES)
    same = up_first(lax.axis_index("group"))
    rows[4], rows[5] = jnp.where(same, rows[4], rows[5]), jnp.where(same, rows[5], rows[4])
    lists_out[...] = jnp.concatenate(rows, 0)


def sorting(coef_rows):
    slots = coef_rows.shape[0]
    lead = coef_rows[:, :slots].astype(F32)[:, :1]
    valid = jnp.broadcast_to(lead, (slots, slots)) > 0.0
    slot = dot(
        ones_where(iota((slots, slots), 1) < iota((slots, slots), 0)), ones_where(valid)
    ).astype(jnp.int32)
    return ones_where(valid & (slot == iota((slots, slots), 1)))


def picking(entry):
    slots = entry.shape[1]
    return ones_where(iota((slots, slots), 0) == entry)


def diagonal(a, b):
    none = jnp.zeros_like(a)
    return jnp.concatenate(
        [jnp.concatenate([a, none], 1), jnp.concatenate([none, b], 1)], 0
    )


def twice(matrix):
    return jnp.concatenate([matrix, matrix], 0)


def split(field):
    high = field.astype(BF16)
    low = (field - high.astype(F32)).astype(BF16)
    return jnp.concatenate([high, low], 1)


PADDED = (PY + 2) * PITCH


def row(y):
    return (y + 1) * PITCH + PITCH - PX


def step(start):
    return pl.ds(start, HALF, stride=2)


def natural(y, odd):
    return step(y * PX + odd)


def halves(y, odd):
    return slice(y * PX + odd * HALF, y * PX + (odd + 1) * HALF)


def put(padded, field):
    for y in range(PY):
        padded[row(y) : row(y) + PX] = field[y * PX : (y + 1) * PX]


def beside_xy(padded, y, odd):
    at = row(y) + odd
    return [padded[step(at + shift)] for shift in (-1, 1, -PITCH, PITCH)]


def weighted(weights, values):
    flow = weights[0] * values[0]
    for w, v in zip(weights[1:], values[1:]):
        flow = flow + w * v
    return flow


def fill_edges(picks, fields, exact):
    x_first, x_last = row(0), row(0) + PX - 1
    places = (
        (pl.ds(x_last, PY, stride=PITCH), pl.ds(x_first - 1, PY, stride=PITCH)),
        (pl.ds(x_first, PY, stride=PITCH), pl.ds(x_last + 1, PY, stride=PITCH)),
        (pl.ds(row(PY - 1), PX), pl.ds(row(-1), PX)),
        (pl.ds(row(0), PX), pl.ds(row(PY), PX)),
    )
    for pick, (source, target) in zip(picks, places):
        taken = jnp.concatenate([field[source] for field in fields], 0)
        got = dot(taken.astype(BF16), pick) if exact else dot(split(taken), twice(pick))
        for i, field in enumerate(fields):
            field[target] = got[i * PX : (i + 1) * PX]


def pick_kernel(lists0, lists_lo, lists_hi, pick_ref, xy_pick, z_pick):
    slots = lists0.shape[1]

    def picking(lists, face):
        return ones_where(iota((slots, slots), 0) == lists[face : face + 1] - 1)

    for face in range(FACES):
        pick_ref[face] = picking(lists0, face)
    for d, lists in enumerate((lists_lo, lists_hi)):
        for face in range(4):
            xy_pick[d, face] = picking(lists, face)
    z_pick[0] = jnp.concatenate([picking(lists_lo, 5), picking(lists_hi, 4)], 1)
    z_pick[1] = jnp.concatenate([picking(lists_lo, 4), picking(lists_hi, 5)], 1)


def own_kernel(
    lewis_ref, got, pick_ref,
    coef_ref, weights_ref, flat_ref, base_ref, rhs_ref, coef_pad, field_ref,
):
    species, cells, slots = base_ref.shape
    sort = diagonal(*[sorting(got[:, :cells])] * 2)
    count = (species + 2) // 2
    pair = [got[:, : count * cells], got[:, (species + 1 - count) * cells :]]
    both = dot_first(jnp.concatenate(pair, 0), sort)
    fields = [both[k * cells : (k + 1) * cells, :slots] for k in range(count)]
    fields += [
        both[k * cells : (k + 1) * cells, slots:] for k in range(2 * count - species - 1, count)
    ]
    coef_ref[...] = fields[0]
    put(coef_pad, fields[0])
    picks = [pick_ref[face] for face in range(4)]
    fill_edges(picks, [coef_pad], True)
    for k in range(species):
        put(field_ref.at[k], fields[k + 1])
        flat_ref[k] = fields[k + 1].astype(BF16)
    fill_edges(picks, [field_ref.at[k] for k in range(species)], True)
    factor = [lewis_ref[k] for k in range(species)]
    for y in range(PY):
        for odd in range(2):
            at = halves(y, odd)
            own = coef_pad[step(row(y) + odd)]
            weights = [0.5 * (own + near) for near in beside_xy(coef_pad, y, odd)]
            for f in range(4):
                weights_ref[f, at] = weights[f]
            for k in range(species):
                field = field_ref[k, step(row(y) + odd)]
                flow = weighted(weights, beside_xy(field_ref.at[k], y, odd))
                base_ref[k, at] = field + factor[k] * flow
                rhs_ref[k, at] = field


def prepare_kernel(
    head_lo, head_hi, coef0, pick0, weights0, xy_pick, z_pick,
    sort_ref, z_natural, z_halves, total0, beside_ref, total_ref, coef_ref, padded, z_ref,
):
    cells, slots = coef0.shape
    for d, head in enumerate((head_lo, head_hi)):
        rows = head[:, :cells]
        sort = sorting(rows)
        both = jnp.concatenate([sort, dot(sort, pick0[4 + d]).astype(BF16)], 1)
        sort_ref[d] = both
        coef = dot_first(rows, both)
        coef_ref[d] = coef[:, :slots]
        put(padded.at[d], coef[:, :slots])
        z_natural[d] = 0.5 * (coef0[...] + coef[:, slots:])
        fill_edges([xy_pick[d, f] for f in range(4)], [padded.at[d]], True)
    near = dot(coef0[...].astype(BF16), z_pick[0])
    z_ref[0] = near[:, :slots]
    z_ref[1] = near[:, slots:]
    for y in range(PY):
        for odd in range(2):
            at = halves(y, odd)
            total = None
            for i in range(2):
                w = z_natural[i, natural(y, odd)]
                z_halves[i, at] = w
                total = w if total is None else total + w
            for f in range(4):
                total = total + weights0[f, at]
            total0[at] = total
            for d in range(2):
                own = padded[d, step(row(y) + odd)]
                near = [*beside_xy(padded.at[d], y, odd), z_ref[d, natural(y, odd)]]
                total = None
                for f in range(5):
                    w = 0.5 * (own + near[f])
                    beside_ref[d, f, at] = w
                    total = w if total is None else total + w
                total_ref[d, natural(y, odd)] = total


def inner_kernel(
    cuts, lewis_ref, sort_ref, xy_pick, z_pick, z_halves, total0, beside_ref,
    pick0, weights0, flat_ref, base_ref, rhs_ref, parts,
    num0, scale0, num_lo, num_hi, field_ref, z_ref, phi_ref,
):
    species, cells, slots = num0.shape
    numbers = (num_lo, num_hi)
    factor = [lewis_ref[k] for k in range(species)]
    for d in range(2):
        k = 0
        for gots, skip, count in zip(parts, (cells, 0), cuts):
            both = dot_first(gots[d][:, skip:], sort_ref[d])
            for i in range(count):
                rows = slice(i * cells, (i + 1) * cells)
                put(field_ref.at[d, k], both[rows, :slots])
                z_ref[d, k] = both[rows, slots:]
                k += 1
    near = dot(flat_ref[...].reshape(species * cells, slots), z_pick[0])
    for k in range(species):
        for d in range(2):
            z_ref[2 + d, k] = near[k * cells : (k + 1) * cells, d * slots : (d + 1) * slots]
    for d in range(2):
        fill_edges(
            [xy_pick[d, f] for f in range(4)], [field_ref.at[d, k] for k in range(species)], True
        )
    for y in range(PY):
        for odd in range(2):
            at = halves(y, odd)
            weights = [z_halves[i, at] for i in range(2)]
            total = total0[at]
            for k in range(species):
                near = [z_ref[i, k, natural(y, odd)] for i in range(2)]
                number = base_ref[k, at] + factor[k] * weighted(weights, near)
                inverse = 1.0 / (1.0 + factor[k] * total)
                phi_ref[k, step(row(y) + odd)] = number * inverse
                scale0[k, natural(y, odd)] = inverse
    fill_edges([pick0[f] for f in range(4)], [phi_ref.at[k] for k in range(species)], False)
    for d in range(2):
        for y in range(PY):
            for odd in range(2):
                at = halves(y, odd)
                weights = [beside_ref[d, f, at] for f in range(5)]
                for k in range(species):
                    near = beside_xy(field_ref.at[d, k], y, odd)
                    near.append(z_ref[2 + d, k, natural(y, odd)])
                    numbers[d][k, natural(y, odd)] = (
                        field_ref[d, k, step(row(y) + odd)] + factor[k] * weighted(weights, near)
                    )
    for y in range(PY):
        for odd in range(2):
            at = halves(y, odd)
            weights = [weights0[f, at] for f in range(4)]
            for k in range(species):
                near = beside_xy(phi_ref.at[k], y, odd)
                inverse = scale0[k, natural(y, odd)]
                number = rhs_ref[k, at] + factor[k] * weighted(weights, near)
                num0[k, natural(y, odd)] = number * inverse
                scale0[k, natural(y, odd)] = factor[k] * inverse


def both_kernel(
    cuts, lewis_ref, got_lo, got_hi, later_lo, later_hi,
    coef0, pick0, weights0, xy_pick, z_pick, flat_ref, base_ref, rhs_ref,
    z_natural, total_ref, coef_ref, num0, scale0, num_lo, num_hi,
    sort_ref, z_halves, total0, beside_ref, padded, near_ref, field_ref, z_ref, phi_ref,
):
    prepare_kernel(
        got_lo, got_hi, coef0, pick0, weights0, xy_pick, z_pick,
        sort_ref, z_natural, z_halves, total0, beside_ref, total_ref, coef_ref, padded, near_ref,
    )
    inner_kernel(
        cuts, lewis_ref, sort_ref, xy_pick, z_pick, z_halves, total0, beside_ref,
        pick0, weights0, flat_ref, base_ref, rhs_ref, ((got_lo, got_hi), (later_lo, later_hi)),
        num0, scale0, num_lo, num_hi, field_ref, z_ref, phi_ref,
    )


def far_kernel(pick0, z_pick, total_ref, coef_ref, head_lo2, head_hi2, far_ref, w_ref, t_ref, two_ref):
    cells = coef_ref.shape[1]
    slots = coef_ref.shape[2]
    rows = [head_lo2[:, :cells], head_hi2[:, :cells]]
    fars = []
    for i in range(2):
        fars.append(dot(sorting(rows[i]), z_pick[1, :, i * slots : (i + 1) * slots]).astype(BF16))
        two_ref[i] = twice(pick0[4 + i])
    far = diagonal(*fars)
    far_ref[...] = far
    near = dot_first(jnp.concatenate(rows, 0), far)
    for i in range(2):
        w = 0.5 * (coef_ref[i] + near[:, i * slots : (i + 1) * slots])
        w_ref[i] = w
        t_ref[i] = total_ref[i] + w


def finish(ghosts, phi_of, two_ref, z_natural, num0, scale0, first, out_ref):
    count, slots, cells = out_ref.shape
    terms = []
    for i in range(2):
        phis = [
            split(phi_of(k, i, ghosts[k * cells : (k + 1) * cells, i * slots : (i + 1) * slots]))
            for k in range(count)
        ]
        terms.append(dot(jnp.concatenate(phis, 0), two_ref[i]))
    for k in range(count):
        rows = slice(k * cells, (k + 1) * cells)
        flow = z_natural[0] * terms[0][rows] + z_natural[1] * terms[1][rows]
        out_ref[k] = jnp.transpose(num0[first + k] + scale0[first + k] * flow, (1, 0))
        yield k


def first_outer_kernel(
    lewis_ref, pick0, z_pick, total_ref, coef_ref, z_natural, num0, scale0, num_lo, num_hi,
    got_lo2, got_hi2, far_ref, two_ref, offset_ref, slope_ref, out_ref, w_ref, t_ref,
):
    far_kernel(
        pick0, z_pick, total_ref, coef_ref, got_lo2, got_hi2, far_ref, w_ref, t_ref, two_ref
    )
    cut, slots, cells = out_ref.shape
    numbers = (num_lo, num_hi)
    factor = [lewis_ref[k] for k in range(num0.shape[0])]
    ghosts = dot_first(
        jnp.concatenate([got_lo2[:, cells:], got_hi2[:, cells:]], 0), far_ref[...]
    )

    def phi_of(k, i, ghost):
        number = numbers[i][k] + factor[k] * (w_ref[i] * ghost)
        return number * (1.0 / (1.0 + factor[k] * t_ref[i]))

    for k in finish(ghosts, phi_of, two_ref, z_natural, num0, scale0, 0, out_ref):
        pass
    for k in range(cut, num0.shape[0]):
        for i in range(2):
            inverse = 1.0 / (1.0 + factor[k] * t_ref[i])
            offset_ref[i, k - cut] = numbers[i][k] * inverse
            slope_ref[i, k - cut] = factor[k] * (w_ref[i] * inverse)


def second_outer_kernel(
    far_ref, two_ref, offset_ref, slope_ref, z_natural, num0, scale0, later_lo2, later_hi2, early,
    out_hbm, out_ref, sems,
):
    count, slots, cells = out_ref.shape
    cut = num0.shape[0] - count
    copies = [pltpu.make_async_copy(early, out_hbm.at[:cut], sems.at[count])]
    copies[-1].start()
    ghosts = dot_first(jnp.concatenate([later_lo2[...], later_hi2[...]], 0), far_ref[...])

    def phi_of(k, i, ghost):
        return offset_ref[i, k] + slope_ref[i, k] * ghost

    for k in finish(ghosts, phi_of, two_ref, z_natural, num0, scale0, cut, out_ref):
        copies.append(pltpu.make_async_copy(out_ref.at[k], out_hbm.at[cut + k], sems.at[k]))
        copies[-1].start()
    for copy in copies:
        copy.wait()


def call(
    kernel, out_shape, scratch, operands, specs=None, outs=None, flops=0, limit=0,
    grid=(1,),
):
    whole = pl.BlockSpec(memory_space=pltpu.VMEM)
    specs = specs or {}
    moved = sum(o.size * o.dtype.itemsize for o in operands)
    moved += sum(o.size * o.dtype.itemsize for o in out_shape)
    return pl.pallas_call(
        kernel,
        out_shape=out_shape,
        grid=grid,
        in_specs=[specs.get(i, whole) for i in range(len(operands))],
        out_specs=outs or [whole] * len(out_shape),
        scratch_shapes=scratch,
        compiler_params=pltpu.CompilerParams(vmem_limit_bytes=limit or VMEM_LIMIT),
        cost_estimate=pl.CostEstimate(flops=flops, bytes_accessed=moved, transcendentals=0),
    )(*operands)


def per_device(state, coef, new_group, face_lists, lewis):
    groups = lax.axis_size("group")
    members = lax.axis_size("member")
    along = ("group", "member")

    def pairs(turn, ends):
        steps = []
        for g in range(groups):
            shift = 1 if up_first(g) == (turn == 0) else -1
            for i in range(members) if ends else range(1, members - 1):
                if 0 <= i + shift < members:
                    steps.append((g * members + i, g * members + i + shift))
        return steps

    one, two = pairs(0, True), pairs(1, True)
    one_on, two_on = pairs(0, False), pairs(1, False)
    slots, species, cells = state.shape[2:]
    capacity = slots // groups
    cuts = (species - species // 2, species // 2)
    width = (1 + species) * cells
    middle = (1 + cuts[0]) * cells
    smem = pl.BlockSpec(memory_space=pltpu.SMEM)
    anywhere = pl.BlockSpec(memory_space=pl.ANY)

    def shape(*dims, dtype=F32):
        return jax.ShapeDtypeStruct(dims, dtype)

    send, lists = call(
        functools.partial(pack_kernel, groups, capacity),
        [shape(slots, width, dtype=BF16), shape(8, slots, dtype=jnp.int32)],
        [],
        (
            new_group[0],
            jnp.transpose(face_lists[0], (1, 0, 2)),
            jnp.transpose(state[0, 0], (1, 0, 2)),
            coef[0, 0],
        ),
        limit=PACK_LIMIT,
        grid=(),
    )
    rows = lax.all_to_all(send, "group", split_axis=0, concat_axis=0, tiled=True)
    lists_lo = lax.ppermute(lists, along, one)
    lists_hi = lax.ppermute(lists, along, two)
    pick0, xy_pick, z_pick = call(
        pick_kernel,
        [
            shape(FACES, slots, slots, dtype=BF16),
            shape(2, 4, slots, slots, dtype=BF16),
            shape(2, slots, 2 * slots, dtype=BF16),
        ],
        [],
        (lists, lists_lo, lists_hi),
    )
    rows, pick0, xy_pick, z_pick = lax.optimization_barrier((rows, pick0, xy_pick, z_pick))
    soon = rows[:, :middle]
    got_lo = [lax.ppermute(soon, along, one)]
    got_hi = [lax.ppermute(soon, along, two)]
    coef0, weights0, flat, base, rhs = call(
        own_kernel,
        [
            shape(cells, slots),
            shape(4, cells, slots),
            shape(species, cells, slots, dtype=BF16),
            shape(species, cells, slots),
            shape(species, cells, slots),
        ],
        [pltpu.VMEM((PADDED, slots), F32), pltpu.VMEM((species, PADDED, slots), F32)],
        (lewis, rows, pick0),
        specs={0: smem},
        flops=500_000_000,
    )
    later, coef0, weights0, flat, base, rhs = lax.optimization_barrier(
        (rows[:, middle:], coef0, weights0, flat, base, rhs)
    )
    got_lo.append(lax.ppermute(later, along, one))
    got_hi.append(lax.ppermute(later, along, two))
    got_lo2 = [lax.ppermute(part, along, one_on) for part in got_lo]
    got_hi2 = [lax.ppermute(part, along, two_on) for part in got_hi]

    z_natural, total, coefs, *numbers = call(
        functools.partial(both_kernel, cuts),
        [shape(2, cells, slots)] * 3 + [shape(species, cells, slots)] * 4,
        [
            pltpu.VMEM((2, slots, 2 * slots), BF16),
            pltpu.VMEM((2, cells, slots), F32),
            pltpu.VMEM((cells, slots), F32),
            pltpu.VMEM((2, 5, cells, slots), F32),
            pltpu.VMEM((2, PADDED, slots), F32),
            pltpu.VMEM((2, cells, slots), F32),
            pltpu.VMEM((2, species, PADDED, slots), F32),
            pltpu.VMEM((4, species, cells, slots), F32),
            pltpu.VMEM((species, PADDED, slots), F32),
        ],
        (
            lewis, got_lo[0], got_hi[0], got_lo[1], got_hi[1],
            coef0, pick0, weights0, xy_pick, z_pick, flat, base, rhs,
        ),
        specs={0: smem},
        flops=200_000_000 * species,
    )
    far, twos, offset, slope, early = call(
        first_outer_kernel,
        [
            shape(2 * slots, 2 * slots, dtype=BF16),
            shape(2, 2 * slots, slots, dtype=BF16),
            shape(2, cuts[1], cells, slots),
            shape(2, cuts[1], cells, slots),
            shape(cuts[0], slots, cells),
        ],
        [pltpu.VMEM((2, cells, slots), F32), pltpu.VMEM((2, cells, slots), F32)],
        (lewis, pick0, z_pick, total, coefs, z_natural, *numbers, got_lo2[0], got_hi2[0]),
        specs={0: smem},
        flops=100_000_000 * cuts[0],
    )
    (out,) = call(
        second_outer_kernel,
        [shape(species, slots, cells)],
        [pltpu.VMEM((cuts[1], slots, cells), F32), pltpu.SemaphoreType.DMA((cuts[1] + 1,))],
        (
            far, twos, offset, slope, z_natural, numbers[0], numbers[1],
            got_lo2[1], got_hi2[1], early,
        ),
        outs=[anywhere],
        flops=100_000_000 * cuts[1],
    )
    return jnp.transpose(out, (1, 0, 2))[None, None]


def solution(mesh):
    return jax.shard_map(
        per_device,
        mesh=mesh,
        in_specs=(
            P("group", "member", None, None, None),
            P("group", "member", None, None),
            P("group", "member", None),
            P("group", "member", None, None),
            P(),
        ),
        out_specs=P("group", "member", None, None, None),
        check_vma=False,
    )
```

```python
import functools

import jax
import jax.numpy as jnp
from jax import lax
from jax.experimental import pallas as pl
from jax.experimental.pallas import tpu as pltpu
from jax.sharding import PartitionSpec as P

PX = 16
PY = 16
FACES = 6
LANES = 128
HALF = PX // 2
PITCH = PX + 8
F32 = jnp.float32
BF16 = jnp.bfloat16
VMEM_LIMIT = 28 * 1024 * 1024
PACK_LIMIT = 60 * 1024 * 1024


def dot(a, b):
    return jnp.dot(a, b, preferred_element_type=F32)


def dot_first(a, b):
    return lax.dot_general(a, b, (((0,), (0,)), ((), ())), preferred_element_type=F32)


def iota(shape, dim):
    return lax.broadcasted_iota(jnp.int32, shape, dim)


def ones_where(mask):
    return jnp.where(mask, 1.0, 0.0).astype(BF16)


def up_first(group):
    return group % 4 == 2


def pack_kernel(groups, capacity, dest_ref, lists_ref, state_ref, coef_ref, send_ref, lists_out):
    species, slots, cells = state_ref.shape
    dest = dest_ref[...]
    onehot = iota((groups, slots), 0) == dest
    earlier = dot(
        ones_where(onehot), ones_where(iota((slots, slots), 0) < iota((slots, slots), 1))
    )
    running = jnp.sum(jnp.where(onehot, earlier, 0.0), axis=0, keepdims=True).astype(jnp.int32)
    position = jnp.where(dest >= 0, dest * capacity + running, -1)
    place = ones_where(iota((slots, slots), 0) == position)
    send_ref[:, :cells] = dot(place, coef_ref[...]).astype(BF16)
    for k in range(species):
        at = slice((k + 1) * cells, (k + 2) * cells)
        send_ref[:, at] = dot(place, state_ref[k]).astype(BF16)
    none = jnp.zeros((1, slots), jnp.int32)
    rows = [lists_ref[f] + 1 for f in range(FACES)] + [none] * (8 - FACES)
    same = up_first(lax.axis_index("group"))
    rows[4], rows[5] = jnp.where(same, rows[4], rows[5]), jnp.where(same, rows[5], rows[4])
    lists_out[...] = jnp.concatenate(rows, 0)


def sorting(coef_rows):
    slots = coef_rows.shape[0]
    lead = coef_rows[:, :slots].astype(F32)[:, :1]
    valid = jnp.broadcast_to(lead, (slots, slots)) > 0.0
    slot = dot(
        ones_where(iota((slots, slots), 1) < iota((slots, slots), 0)), ones_where(valid)
    ).astype(jnp.int32)
    return ones_where(valid & (slot == iota((slots, slots), 1)))


def picking(entry):
    slots = entry.shape[1]
    return ones_where(iota((slots, slots), 0) == entry)


def diagonal(a, b):
    none = jnp.zeros_like(a)
    return jnp.concatenate(
        [jnp.concatenate([a, none], 1), jnp.concatenate([none, b], 1)], 0
    )


def twice(matrix):
    return jnp.concatenate([matrix, matrix], 0)


def split(field):
    high = field.astype(BF16)
    low = (field - high.astype(F32)).astype(BF16)
    return jnp.concatenate([high, low], 1)


PADDED = (PY + 2) * PITCH


def row(y):
    return (y + 1) * PITCH + PITCH - PX


def step(start):
    return pl.ds(start, HALF, stride=2)


def natural(y, odd):
    return step(y * PX + odd)


def halves(y, odd):
    return slice(y * PX + odd * HALF, y * PX + (odd + 1) * HALF)


def put(padded, field):
    for y in range(PY):
        padded[row(y) : row(y) + PX] = field[y * PX : (y + 1) * PX]


def beside_xy(padded, y):
    at = row(y)
    even, odd = padded[step(at)], padded[step(at + 1)]
    below, above = at - PITCH, at + PITCH
    return (even, odd), (
        [padded[step(at - 1)], odd, padded[step(below)], padded[step(above)]],
        [even, padded[step(at + 2)], padded[step(below + 1)], padded[step(above + 1)]],
    )


def weighted(weights, values):
    flow = weights[0] * values[0]
    for w, v in zip(weights[1:], values[1:]):
        flow = flow + w * v
    return flow


def fill_edges(picks, fields, exact):
    x_first, x_last = row(0), row(0) + PX - 1
    places = (
        (pl.ds(x_last, PY, stride=PITCH), pl.ds(x_first - 1, PY, stride=PITCH)),
        (pl.ds(x_first, PY, stride=PITCH), pl.ds(x_last + 1, PY, stride=PITCH)),
        (pl.ds(row(PY - 1), PX), pl.ds(row(-1), PX)),
        (pl.ds(row(0), PX), pl.ds(row(PY), PX)),
    )
    for pick, (source, target) in zip(picks, places):
        taken = jnp.concatenate([field[source] for field in fields], 0)
        got = dot(taken.astype(BF16), pick) if exact else dot(split(taken), twice(pick))
        for i, field in enumerate(fields):
            field[target] = got[i * PX : (i + 1) * PX]


def pick_kernel(lists0, lists_lo, lists_hi, pick_ref, xy_pick, z_pick):
    slots = lists0.shape[1]

    def picking(lists, face):
        return ones_where(iota((slots, slots), 0) == lists[face : face + 1] - 1)

    for face in range(FACES):
        pick_ref[face] = picking(lists0, face)
    for d, lists in enumerate((lists_lo, lists_hi)):
        for face in range(4):
            xy_pick[d, face] = picking(lists, face)
    z_pick[0] = jnp.concatenate([picking(lists_lo, 5), picking(lists_hi, 4)], 1)
    z_pick[1] = jnp.concatenate([picking(lists_lo, 4), picking(lists_hi, 5)], 1)


def own_kernel(
    lewis_ref, got, pick_ref,
    coef_ref, weights_ref, flat_ref, base_ref, rhs_ref, coef_pad, field_ref,
):
    species, cells, slots = base_ref.shape
    sort = diagonal(*[sorting(got[:, :cells])] * 2)
    count = (species + 2) // 2
    pair = [got[:, : count * cells], got[:, (species + 1 - count) * cells :]]
    both = dot_first(jnp.concatenate(pair, 0), sort)
    fields = [both[k * cells : (k + 1) * cells, :slots] for k in range(count)]
    fields += [
        both[k * cells : (k + 1) * cells, slots:] for k in range(2 * count - species - 1, count)
    ]
    coef_ref[...] = fields[0]
    put(coef_pad, fields[0])
    picks = [pick_ref[face] for face in range(4)]
    fill_edges(picks, [coef_pad], True)
    for k in range(species):
        put(field_ref.at[k], fields[k + 1])
        flat_ref[k] = fields[k + 1].astype(BF16)
    fill_edges(picks, [field_ref.at[k] for k in range(species)], True)
    factor = [lewis_ref[k] for k in range(species)]
    for y in range(PY):
        own, near = beside_xy(coef_pad, y)
        weights = [[0.5 * (own[odd] + n) for n in near[odd]] for odd in range(2)]
        for odd in range(2):
            for f in range(4):
                weights_ref[f, halves(y, odd)] = weights[odd][f]
        for k in range(species):
            field, near = beside_xy(field_ref.at[k], y)
            for odd in range(2):
                at = halves(y, odd)
                base_ref[k, at] = field[odd] + factor[k] * weighted(weights[odd], near[odd])
                rhs_ref[k, at] = field[odd]


def prepare_kernel(
    head_lo, head_hi, coef0, pick0, weights0, xy_pick, z_pick,
    sort_ref, z_natural, z_halves, total0, beside_ref, total_ref, coef_ref, padded, z_ref,
):
    cells, slots = coef0.shape
    for d, head in enumerate((head_lo, head_hi)):
        rows = head[:, :cells]
        sort = sorting(rows)
        both = jnp.concatenate([sort, dot(sort, pick0[4 + d]).astype(BF16)], 1)
        sort_ref[d] = both
        coef = dot_first(rows, both)
        coef_ref[d] = coef[:, :slots]
        put(padded.at[d], coef[:, :slots])
        z_natural[d] = 0.5 * (coef0[...] + coef[:, slots:])
        fill_edges([xy_pick[d, f] for f in range(4)], [padded.at[d]], True)
    near = dot(coef0[...].astype(BF16), z_pick[0])
    z_ref[0] = near[:, :slots]
    z_ref[1] = near[:, slots:]
    for y in range(PY):
        for odd in range(2):
            at = halves(y, odd)
            total = None
            for i in range(2):
                w = z_natural[i, natural(y, odd)]
                z_halves[i, at] = w
                total = w if total is None else total + w
            for f in range(4):
                total = total + weights0[f, at]
            total0[at] = total
        for d in range(2):
            own, beside = beside_xy(padded.at[d], y)
            for odd in range(2):
                at = halves(y, odd)
                near = [*beside[odd], z_ref[d, natural(y, odd)]]
                total = None
                for f in range(5):
                    w = 0.5 * (own[odd] + near[f])
                    beside_ref[d, f, at] = w
                    total = w if total is None else total + w
                total_ref[d, natural(y, odd)] = total


def inner_kernel(
    cuts, lewis_ref, sort_ref, xy_pick, z_pick, z_halves, total0, beside_ref,
    pick0, weights0, flat_ref, base_ref, rhs_ref, parts,
    num0, scale0, num_lo, num_hi, field_ref, z_ref, phi_ref,
):
    species, cells, slots = num0.shape
    numbers = (num_lo, num_hi)
    factor = [lewis_ref[k] for k in range(species)]
    for d in range(2):
        k = 0
        for gots, skip, count in zip(parts, (cells, 0), cuts):
            both = dot_first(gots[d][:, skip:], sort_ref[d])
            for i in range(count):
                rows = slice(i * cells, (i + 1) * cells)
                put(field_ref.at[d, k], both[rows, :slots])
                z_ref[d, k] = both[rows, slots:]
                k += 1
    near = dot(flat_ref[...].reshape(species * cells, slots), z_pick[0])
    for k in range(species):
        for d in range(2):
            z_ref[2 + d, k] = near[k * cells : (k + 1) * cells, d * slots : (d + 1) * slots]
    for d in range(2):
        fill_edges(
            [xy_pick[d, f] for f in range(4)], [field_ref.at[d, k] for k in range(species)], True
        )
    for y in range(PY):
        for odd in range(2):
            at = halves(y, odd)
            weights = [z_halves[i, at] for i in range(2)]
            total = total0[at]
            for k in range(species):
                near = [z_ref[i, k, natural(y, odd)] for i in range(2)]
                number = base_ref[k, at] + factor[k] * weighted(weights, near)
                inverse = 1.0 / (1.0 + factor[k] * total)
                phi_ref[k, step(row(y) + odd)] = number * inverse
                scale0[k, natural(y, odd)] = inverse
    fill_edges([pick0[f] for f in range(4)], [phi_ref.at[k] for k in range(species)], False)
    for d in range(2):
        for y in range(PY):
            weights = [[beside_ref[d, f, halves(y, odd)] for f in range(5)] for odd in range(2)]
            for k in range(species):
                field, near = beside_xy(field_ref.at[d, k], y)
                for odd in range(2):
                    at = natural(y, odd)
                    flow = weighted(weights[odd], [*near[odd], z_ref[2 + d, k, at]])
                    numbers[d][k, at] = field[odd] + factor[k] * flow
    for y in range(PY):
        weights = [[weights0[f, halves(y, odd)] for f in range(4)] for odd in range(2)]
        for k in range(species):
            _, near = beside_xy(phi_ref.at[k], y)
            for odd in range(2):
                at = natural(y, odd)
                inverse = scale0[k, at]
                number = rhs_ref[k, halves(y, odd)] + factor[k] * weighted(weights[odd], near[odd])
                num0[k, at] = number * inverse
                scale0[k, at] = factor[k] * inverse


def both_kernel(
    cuts, lewis_ref, got_lo, got_hi, later_lo, later_hi,
    coef0, pick0, weights0, xy_pick, z_pick, flat_ref, base_ref, rhs_ref,
    z_natural, total_ref, coef_ref, num0, scale0, num_lo, num_hi,
    sort_ref, z_halves, total0, beside_ref, padded, near_ref, field_ref, z_ref, phi_ref,
):
    prepare_kernel(
        got_lo, got_hi, coef0, pick0, weights0, xy_pick, z_pick,
        sort_ref, z_natural, z_halves, total0, beside_ref, total_ref, coef_ref, padded, near_ref,
    )
    inner_kernel(
        cuts, lewis_ref, sort_ref, xy_pick, z_pick, z_halves, total0, beside_ref,
        pick0, weights0, flat_ref, base_ref, rhs_ref, ((got_lo, got_hi), (later_lo, later_hi)),
        num0, scale0, num_lo, num_hi, field_ref, z_ref, phi_ref,
    )


def far_kernel(pick0, z_pick, total_ref, coef_ref, head_lo2, head_hi2, far_ref, w_ref, t_ref, two_ref):
    cells = coef_ref.shape[1]
    slots = coef_ref.shape[2]
    rows = [head_lo2[:, :cells], head_hi2[:, :cells]]
    fars = []
    for i in range(2):
        fars.append(dot(sorting(rows[i]), z_pick[1, :, i * slots : (i + 1) * slots]).astype(BF16))
        two_ref[i] = twice(pick0[4 + i])
    far = diagonal(*fars)
    far_ref[...] = far
    near = dot_first(jnp.concatenate(rows, 0), far)
    for i in range(2):
        w = 0.5 * (coef_ref[i] + near[:, i * slots : (i + 1) * slots])
        w_ref[i] = w
        t_ref[i] = total_ref[i] + w


def finish(ghosts, phi_of, two_ref, z_natural, num0, scale0, first, out_ref):
    count, slots, cells = out_ref.shape
    terms = []
    for i in range(2):
        phis = [
            split(phi_of(k, i, ghosts[k * cells : (k + 1) * cells, i * slots : (i + 1) * slots]))
            for k in range(count)
        ]
        terms.append(dot(jnp.concatenate(phis, 0), two_ref[i]))
    for k in range(count):
        rows = slice(k * cells, (k + 1) * cells)
        flow = z_natural[0] * terms[0][rows] + z_natural[1] * terms[1][rows]
        out_ref[k] = jnp.transpose(num0[first + k] + scale0[first + k] * flow, (1, 0))
        yield k


def first_outer_kernel(
    lewis_ref, pick0, z_pick, total_ref, coef_ref, z_natural, num0, scale0, num_lo, num_hi,
    got_lo2, got_hi2, far_ref, two_ref, offset_ref, slope_ref, out_ref, w_ref, t_ref,
):
    far_kernel(
        pick0, z_pick, total_ref, coef_ref, got_lo2, got_hi2, far_ref, w_ref, t_ref, two_ref
    )
    cut, slots, cells = out_ref.shape
    numbers = (num_lo, num_hi)
    factor = [lewis_ref[k] for k in range(num0.shape[0])]
    ghosts = dot_first(
        jnp.concatenate([got_lo2[:, cells:], got_hi2[:, cells:]], 0), far_ref[...]
    )

    def phi_of(k, i, ghost):
        number = numbers[i][k] + factor[k] * (w_ref[i] * ghost)
        return number * (1.0 / (1.0 + factor[k] * t_ref[i]))

    for k in finish(ghosts, phi_of, two_ref, z_natural, num0, scale0, 0, out_ref):
        pass
    for k in range(cut, num0.shape[0]):
        for i in range(2):
            inverse = 1.0 / (1.0 + factor[k] * t_ref[i])
            offset_ref[i, k - cut] = numbers[i][k] * inverse
            slope_ref[i, k - cut] = factor[k] * (w_ref[i] * inverse)


def second_outer_kernel(
    far_ref, two_ref, offset_ref, slope_ref, z_natural, num0, scale0, later_lo2, later_hi2, early,
    out_hbm, out_ref, sems,
):
    count, slots, cells = out_ref.shape
    cut = num0.shape[0] - count
    copies = [pltpu.make_async_copy(early, out_hbm.at[:cut], sems.at[count])]
    copies[-1].start()
    ghosts = dot_first(jnp.concatenate([later_lo2[...], later_hi2[...]], 0), far_ref[...])

    def phi_of(k, i, ghost):
        return offset_ref[i, k] + slope_ref[i, k] * ghost

    for k in finish(ghosts, phi_of, two_ref, z_natural, num0, scale0, cut, out_ref):
        copies.append(pltpu.make_async_copy(out_ref.at[k], out_hbm.at[cut + k], sems.at[k]))
        copies[-1].start()
    for copy in copies:
        copy.wait()


def call(
    kernel, out_shape, scratch, operands, specs=None, outs=None, flops=0, limit=0,
    grid=(1,),
):
    whole = pl.BlockSpec(memory_space=pltpu.VMEM)
    specs = specs or {}
    moved = sum(o.size * o.dtype.itemsize for o in operands)
    moved += sum(o.size * o.dtype.itemsize for o in out_shape)
    return pl.pallas_call(
        kernel,
        out_shape=out_shape,
        grid=grid,
        in_specs=[specs.get(i, whole) for i in range(len(operands))],
        out_specs=outs or [whole] * len(out_shape),
        scratch_shapes=scratch,
        compiler_params=pltpu.CompilerParams(vmem_limit_bytes=limit or VMEM_LIMIT),
        cost_estimate=pl.CostEstimate(flops=flops, bytes_accessed=moved, transcendentals=0),
    )(*operands)


def per_device(state, coef, new_group, face_lists, lewis):
    groups = lax.axis_size("group")
    members = lax.axis_size("member")
    along = ("group", "member")

    def pairs(turn, ends):
        steps = []
        for g in range(groups):
            shift = 1 if up_first(g) == (turn == 0) else -1
            for i in range(members) if ends else range(1, members - 1):
                if 0 <= i + shift < members:
                    steps.append((g * members + i, g * members + i + shift))
        return steps

    one, two = pairs(0, True), pairs(1, True)
    one_on, two_on = pairs(0, False), pairs(1, False)
    slots, species, cells = state.shape[2:]
    capacity = slots // groups
    cuts = (species - species // 2, species // 2)
    width = (1 + species) * cells
    middle = (1 + cuts[0]) * cells
    smem = pl.BlockSpec(memory_space=pltpu.SMEM)
    anywhere = pl.BlockSpec(memory_space=pl.ANY)

    def shape(*dims, dtype=F32):
        return jax.ShapeDtypeStruct(dims, dtype)

    send, lists = call(
        functools.partial(pack_kernel, groups, capacity),
        [shape(slots, width, dtype=BF16), shape(8, slots, dtype=jnp.int32)],
        [],
        (
            new_group[0],
            jnp.transpose(face_lists[0], (1, 0, 2)),
            jnp.transpose(state[0, 0], (1, 0, 2)),
            coef[0, 0],
        ),
        limit=PACK_LIMIT,
        grid=(),
    )
    rows = lax.all_to_all(send, "group", split_axis=0, concat_axis=0, tiled=True)
    lists_lo = lax.ppermute(lists, along, one)
    lists_hi = lax.ppermute(lists, along, two)
    pick0, xy_pick, z_pick = call(
        pick_kernel,
        [
            shape(FACES, slots, slots, dtype=BF16),
            shape(2, 4, slots, slots, dtype=BF16),
            shape(2, slots, 2 * slots, dtype=BF16),
        ],
        [],
        (lists, lists_lo, lists_hi),
    )
    rows, pick0, xy_pick, z_pick = lax.optimization_barrier((rows, pick0, xy_pick, z_pick))
    soon = rows[:, :middle]
    got_lo = [lax.ppermute(soon, along, one)]
    got_hi = [lax.ppermute(soon, along, two)]
    coef0, weights0, flat, base, rhs = call(
        own_kernel,
        [
            shape(cells, slots),
            shape(4, cells, slots),
            shape(species, cells, slots, dtype=BF16),
            shape(species, cells, slots),
            shape(species, cells, slots),
        ],
        [pltpu.VMEM((PADDED, slots), F32), pltpu.VMEM((species, PADDED, slots), F32)],
        (lewis, rows, pick0),
        specs={0: smem},
        flops=500_000_000,
    )
    later, coef0, weights0, flat, base, rhs = lax.optimization_barrier(
        (rows[:, middle:], coef0, weights0, flat, base, rhs)
    )
    got_lo.append(lax.ppermute(later, along, one))
    got_hi.append(lax.ppermute(later, along, two))
    got_lo2 = [lax.ppermute(part, along, one_on) for part in got_lo]
    got_hi2 = [lax.ppermute(part, along, two_on) for part in got_hi]

    z_natural, total, coefs, *numbers = call(
        functools.partial(both_kernel, cuts),
        [shape(2, cells, slots)] * 3 + [shape(species, cells, slots)] * 4,
        [
            pltpu.VMEM((2, slots, 2 * slots), BF16),
            pltpu.VMEM((2, cells, slots), F32),
            pltpu.VMEM((cells, slots), F32),
            pltpu.VMEM((2, 5, cells, slots), F32),
            pltpu.VMEM((2, PADDED, slots), F32),
            pltpu.VMEM((2, cells, slots), F32),
            pltpu.VMEM((2, species, PADDED, slots), F32),
            pltpu.VMEM((4, species, cells, slots), F32),
            pltpu.VMEM((species, PADDED, slots), F32),
        ],
        (
            lewis, got_lo[0], got_hi[0], got_lo[1], got_hi[1],
            coef0, pick0, weights0, xy_pick, z_pick, flat, base, rhs,
        ),
        specs={0: smem},
        flops=200_000_000 * species,
    )
    far, twos, offset, slope, early = call(
        first_outer_kernel,
        [
            shape(2 * slots, 2 * slots, dtype=BF16),
            shape(2, 2 * slots, slots, dtype=BF16),
            shape(2, cuts[1], cells, slots),
            shape(2, cuts[1], cells, slots),
            shape(cuts[0], slots, cells),
        ],
        [pltpu.VMEM((2, cells, slots), F32), pltpu.VMEM((2, cells, slots), F32)],
        (lewis, pick0, z_pick, total, coefs, z_natural, *numbers, got_lo2[0], got_hi2[0]),
        specs={0: smem},
        flops=100_000_000 * cuts[0],
    )
    (out,) = call(
        second_outer_kernel,
        [shape(species, slots, cells)],
        [pltpu.VMEM((cuts[1], slots, cells), F32), pltpu.SemaphoreType.DMA((cuts[1] + 1,))],
        (
            far, twos, offset, slope, z_natural, numbers[0], numbers[1],
            got_lo2[1], got_hi2[1], early,
        ),
        outs=[anywhere],
        flops=100_000_000 * cuts[1],
    )
    return jnp.transpose(out, (1, 0, 2))[None, None]


def solution(mesh):
    return jax.shard_map(
        per_device,
        mesh=mesh,
        in_specs=(
            P("group", "member", None, None, None),
            P("group", "member", None, None),
            P("group", "member", None),
            P("group", "member", None, None),
            P(),
        ),
        out_specs=P("group", "member", None, None, None),
        check_vma=False,
    )
```

```python
import functools

import jax
import jax.numpy as jnp
from jax import lax
from jax.experimental import pallas as pl
from jax.experimental.pallas import tpu as pltpu
from jax.sharding import PartitionSpec as P

PX = 16
PY = 16
FACES = 6
LANES = 128
HALF = PX // 2
PITCH = PX + 8
SPARE = 8
F32 = jnp.float32
BF16 = jnp.bfloat16
VMEM_LIMIT = 28 * 1024 * 1024
PACK_LIMIT = 60 * 1024 * 1024


def dot(a, b):
    return jnp.dot(a, b, preferred_element_type=F32)


def dot_first(a, b):
    return lax.dot_general(a, b, (((0,), (0,)), ((), ())), preferred_element_type=F32)


def iota(shape, dim):
    return lax.broadcasted_iota(jnp.int32, shape, dim)


def ones_where(mask):
    return jnp.where(mask, 1.0, 0.0).astype(BF16)


def up_first(group):
    return group % 4 == 2


def pack_kernel(groups, capacity, dest_ref, lists_ref, state_ref, coef_ref, send_ref, lists_out):
    species, slots, cells = state_ref.shape
    dest = dest_ref[...]
    onehot = iota((groups, slots), 0) == dest
    earlier = dot(
        ones_where(onehot), ones_where(iota((slots, slots), 0) < iota((slots, slots), 1))
    )
    running = jnp.sum(jnp.where(onehot, earlier, 0.0), axis=0, keepdims=True).astype(jnp.int32)
    position = jnp.where(dest >= 0, dest * capacity + running, -1)
    place = ones_where(iota((slots, slots), 0) == position)
    send_ref[:, :cells] = dot(place, coef_ref[...]).astype(BF16)
    for k in range(species):
        at = slice((k + 1) * cells, (k + 2) * cells)
        send_ref[:, at] = dot(place, state_ref[k]).astype(BF16)
    none = jnp.zeros((1, slots), jnp.int32)
    rows = [lists_ref[f] + 1 for f in range(FACES)] + [none] * (8 - FACES)
    same = up_first(lax.axis_index("group"))
    rows[4], rows[5] = jnp.where(same, rows[4], rows[5]), jnp.where(same, rows[5], rows[4])
    lists_out[...] = jnp.concatenate(rows, 0)


def sorting(coef_rows):
    slots = coef_rows.shape[0]
    lead = coef_rows[:, :slots].astype(F32)[:, :1]
    valid = jnp.broadcast_to(lead, (slots, slots)) > 0.0
    slot = dot(
        ones_where(iota((slots, slots), 1) < iota((slots, slots), 0)), ones_where(valid)
    ).astype(jnp.int32)
    return ones_where(valid & (slot == iota((slots, slots), 1)))


def picking(entry):
    slots = entry.shape[1]
    return ones_where(iota((slots, slots), 0) == entry)


def diagonal(a, b):
    none = jnp.zeros_like(a)
    return jnp.concatenate(
        [jnp.concatenate([a, none], 1), jnp.concatenate([none, b], 1)], 0
    )


def twice(matrix):
    return jnp.concatenate([matrix, matrix], 0)


def split(field):
    high = field.astype(BF16)
    low = (field - high.astype(F32)).astype(BF16)
    return jnp.concatenate([high, low], 1)


PADDED = (PY + 2) * PITCH + SPARE


def row(y):
    return (y + 1) * PITCH + PITCH - PX


def step(start):
    return pl.ds(start, HALF, stride=2)


def natural(y, odd):
    return step(y * PX + odd)


def halves(y, odd):
    return slice(y * PX + odd * HALF, y * PX + (odd + 1) * HALF)


def put(padded, field):
    for y in range(PY):
        padded[row(y) : row(y) + PX] = field[y * PX : (y + 1) * PX]


def beside_xy(padded, y, odd):
    at = row(y) + odd
    return [padded[step(at + shift)] for shift in (-1, 1, -PITCH, PITCH)]


def weighted(weights, values):
    flow = weights[0] * values[0]
    for w, v in zip(weights[1:], values[1:]):
        flow = flow + w * v
    return flow


def fill_edges(picks, fields, exact):
    x_first, x_last = row(0), row(0) + PX - 1
    places = (
        (pl.ds(x_last, PY, stride=PITCH), pl.ds(x_first - 1, PY, stride=PITCH)),
        (pl.ds(x_first, PY, stride=PITCH), pl.ds(x_last + 1, PY, stride=PITCH)),
        (pl.ds(row(PY - 1), PX), pl.ds(row(-1), PX)),
        (pl.ds(row(0), PX), pl.ds(row(PY), PX)),
    )
    for pick, (source, target) in zip(picks, places):
        taken = jnp.concatenate([field[source] for field in fields], 0)
        got = dot(taken.astype(BF16), pick) if exact else dot(split(taken), twice(pick))
        for i, field in enumerate(fields):
            field[target] = got[i * PX : (i + 1) * PX]


def pick_kernel(lists0, lists_lo, lists_hi, pick_ref, xy_pick, z_pick):
    slots = lists0.shape[1]

    def picking(lists, face):
        return ones_where(iota((slots, slots), 0) == lists[face : face + 1] - 1)

    for face in range(FACES):
        pick_ref[face] = picking(lists0, face)
    for d, lists in enumerate((lists_lo, lists_hi)):
        for face in range(4):
            xy_pick[d, face] = picking(lists, face)
    z_pick[0] = jnp.concatenate([picking(lists_lo, 5), picking(lists_hi, 4)], 1)
    z_pick[1] = jnp.concatenate([picking(lists_lo, 4), picking(lists_hi, 5)], 1)


def own_kernel(
    lewis_ref, got, pick_ref,
    coef_ref, weights_ref, flat_ref, base_ref, rhs_ref, coef_pad, field_ref,
):
    species, cells, slots = base_ref.shape
    sort = diagonal(*[sorting(got[:, :cells])] * 2)
    count = (species + 2) // 2
    pair = [got[:, : count * cells], got[:, (species + 1 - count) * cells :]]
    both = dot_first(jnp.concatenate(pair, 0), sort)
    fields = [both[k * cells : (k + 1) * cells, :slots] for k in range(count)]
    fields += [
        both[k * cells : (k + 1) * cells, slots:] for k in range(2 * count - species - 1, count)
    ]
    coef_ref[...] = fields[0]
    put(coef_pad, fields[0])
    picks = [pick_ref[face] for face in range(4)]
    fill_edges(picks, [coef_pad], True)
    for k in range(species):
        put(field_ref.at[k], fields[k + 1])
        flat_ref[k] = fields[k + 1].astype(BF16)
    fill_edges(picks, [field_ref.at[k] for k in range(species)], True)
    factor = [lewis_ref[k] for k in range(species)]
    for y in range(PY):
        for odd in range(2):
            at = halves(y, odd)
            own = coef_pad[step(row(y) + odd)]
            weights = [0.5 * (own + near) for near in beside_xy(coef_pad, y, odd)]
            for f in range(4):
                weights_ref[f, at] = weights[f]
            for k in range(species):
                field = field_ref[k, step(row(y) + odd)]
                flow = weighted(weights, beside_xy(field_ref.at[k], y, odd))
                base_ref[k, at] = field + factor[k] * flow
                rhs_ref[k, at] = field


def prepare_kernel(
    head_lo, head_hi, coef0, pick0, weights0, xy_pick, z_pick,
    sort_ref, z_natural, z_halves, total0, beside_ref, total_ref, coef_ref, padded, z_ref,
):
    cells, slots = coef0.shape
    for d, head in enumerate((head_lo, head_hi)):
        rows = head[:, :cells]
        sort = sorting(rows)
        both = jnp.concatenate([sort, dot(sort, pick0[4 + d]).astype(BF16)], 1)
        sort_ref[d] = both
        coef = dot_first(rows, both)
        coef_ref[d] = coef[:, :slots]
        put(padded.at[d], coef[:, :slots])
        z_natural[d, :cells] = 0.5 * (coef0[...] + coef[:, slots:])
        fill_edges([xy_pick[d, f] for f in range(4)], [padded.at[d]], True)
    near = dot(coef0[...].astype(BF16), z_pick[0])
    z_ref[0, :cells] = near[:, :slots]
    z_ref[1, :cells] = near[:, slots:]
    for y in range(PY):
        for odd in range(2):
            at = halves(y, odd)
            total = None
            for i in range(2):
                w = z_natural[i, natural(y, odd)]
                z_halves[i, at] = w
                total = w if total is None else total + w
            for f in range(4):
                total = total + weights0[f, at]
            total0[at] = total
            for d in range(2):
                own = padded[d, step(row(y) + odd)]
                near = [*beside_xy(padded.at[d], y, odd), z_ref[d, natural(y, odd)]]
                total = None
                for f in range(5):
                    w = 0.5 * (own + near[f])
                    beside_ref[d, f, at] = w
                    total = w if total is None else total + w
                total_ref[d, natural(y, odd)] = total


def inner_kernel(
    cuts, lewis_ref, sort_ref, xy_pick, z_pick, z_halves, total0, beside_ref,
    pick0, weights0, flat_ref, base_ref, rhs_ref, parts,
    num0, scale0, num_lo, num_hi, field_ref, z_ref, phi_ref,
):
    species, rows, slots = num0.shape
    cells = rows - SPARE
    numbers = (num_lo, num_hi)
    factor = [lewis_ref[k] for k in range(species)]
    for d in range(2):
        k = 0
        for gots, skip, count in zip(parts, (cells, 0), cuts):
            both = dot_first(gots[d][:, skip:], sort_ref[d])
            for i in range(count):
                rows = slice(i * cells, (i + 1) * cells)
                put(field_ref.at[d, k], both[rows, :slots])
                z_ref[d, k, :cells] = both[rows, slots:]
                k += 1
    near = dot(flat_ref[...].reshape(species * cells, slots), z_pick[0])
    for k in range(species):
        for d in range(2):
            z_ref[2 + d, k, :cells] = near[k * cells : (k + 1) * cells, d * slots : (d + 1) * slots]
    for d in range(2):
        fill_edges(
            [xy_pick[d, f] for f in range(4)], [field_ref.at[d, k] for k in range(species)], True
        )
    for y in range(PY):
        for odd in range(2):
            at = halves(y, odd)
            weights = [z_halves[i, at] for i in range(2)]
            total = total0[at]
            for k in range(species):
                near = [z_ref[i, k, natural(y, odd)] for i in range(2)]
                number = base_ref[k, at] + factor[k] * weighted(weights, near)
                inverse = 1.0 / (1.0 + factor[k] * total)
                phi_ref[k, step(row(y) + odd)] = number * inverse
                scale0[k, natural(y, odd)] = inverse
    fill_edges([pick0[f] for f in range(4)], [phi_ref.at[k] for k in range(species)], False)
    for d in range(2):
        for y in range(PY):
            for odd in range(2):
                at = halves(y, odd)
                weights = [beside_ref[d, f, at] for f in range(5)]
                for k in range(species):
                    near = beside_xy(field_ref.at[d, k], y, odd)
                    near.append(z_ref[2 + d, k, natural(y, odd)])
                    numbers[d][k, natural(y, odd)] = (
                        field_ref[d, k, step(row(y) + odd)] + factor[k] * weighted(weights, near)
                    )
    for y in range(PY):
        for odd in range(2):
            at = halves(y, odd)
            weights = [weights0[f, at] for f in range(4)]
            for k in range(species):
                near = beside_xy(phi_ref.at[k], y, odd)
                inverse = scale0[k, natural(y, odd)]
                number = rhs_ref[k, at] + factor[k] * weighted(weights, near)
                num0[k, natural(y, odd)] = number * inverse
                scale0[k, natural(y, odd)] = factor[k] * inverse


def both_kernel(
    cuts, lewis_ref, got_lo, got_hi, later_lo, later_hi,
    coef0, pick0, weights0, xy_pick, z_pick, flat_ref, base_ref, rhs_ref,
    z_natural, total_ref, coef_ref, num0, scale0, num_lo, num_hi,
    sort_ref, z_halves, total0, beside_ref, padded, near_ref, field_ref, z_ref, phi_ref,
):
    prepare_kernel(
        got_lo, got_hi, coef0, pick0, weights0, xy_pick, z_pick,
        sort_ref, z_natural, z_halves, total0, beside_ref, total_ref, coef_ref, padded, near_ref,
    )
    inner_kernel(
        cuts, lewis_ref, sort_ref, xy_pick, z_pick, z_halves, total0, beside_ref,
        pick0, weights0, flat_ref, base_ref, rhs_ref, ((got_lo, got_hi), (later_lo, later_hi)),
        num0, scale0, num_lo, num_hi, field_ref, z_ref, phi_ref,
    )


def far_kernel(pick0, z_pick, total_ref, coef_ref, head_lo2, head_hi2, far_ref, w_ref, t_ref, two_ref):
    cells = coef_ref.shape[1]
    slots = coef_ref.shape[2]
    rows = [head_lo2[:, :cells], head_hi2[:, :cells]]
    fars = []
    for i in range(2):
        fars.append(dot(sorting(rows[i]), z_pick[1, :, i * slots : (i + 1) * slots]).astype(BF16))
        two_ref[i] = twice(pick0[4 + i])
    far = diagonal(*fars)
    far_ref[...] = far
    near = dot_first(jnp.concatenate(rows, 0), far)
    for i in range(2):
        w = 0.5 * (coef_ref[i] + near[:, i * slots : (i + 1) * slots])
        w_ref[i] = w
        t_ref[i] = total_ref[i, :cells] + w


def finish(ghosts, phi_of, two_ref, z_natural, num0, scale0, first, out_ref):
    count, slots, cells = out_ref.shape
    terms = []
    for i in range(2):
        phis = [
            split(phi_of(k, i, ghosts[k * cells : (k + 1) * cells, i * slots : (i + 1) * slots]))
            for k in range(count)
        ]
        terms.append(dot(jnp.concatenate(phis, 0), two_ref[i]))
    for k in range(count):
        rows = slice(k * cells, (k + 1) * cells)
        flow = z_natural[0, :cells] * terms[0][rows] + z_natural[1, :cells] * terms[1][rows]
        number, scale = num0[first + k, :cells], scale0[first + k, :cells]
        out_ref[k] = jnp.transpose(number + scale * flow, (1, 0))
        yield k


def first_outer_kernel(
    lewis_ref, pick0, z_pick, total_ref, coef_ref, z_natural, num0, scale0, num_lo, num_hi,
    got_lo2, got_hi2, far_ref, two_ref, offset_ref, slope_ref, out_ref, w_ref, t_ref,
):
    far_kernel(
        pick0, z_pick, total_ref, coef_ref, got_lo2, got_hi2, far_ref, w_ref, t_ref, two_ref
    )
    cut, slots, cells = out_ref.shape
    numbers = (num_lo, num_hi)
    factor = [lewis_ref[k] for k in range(num0.shape[0])]
    ghosts = dot_first(
        jnp.concatenate([got_lo2[:, cells:], got_hi2[:, cells:]], 0), far_ref[...]
    )

    def phi_of(k, i, ghost):
        number = numbers[i][k, :cells] + factor[k] * (w_ref[i] * ghost)
        return number * (1.0 / (1.0 + factor[k] * t_ref[i]))

    for k in finish(ghosts, phi_of, two_ref, z_natural, num0, scale0, 0, out_ref):
        pass
    for k in range(cut, num0.shape[0]):
        for i in range(2):
            inverse = 1.0 / (1.0 + factor[k] * t_ref[i])
            offset_ref[i, k - cut] = numbers[i][k, :cells] * inverse
            slope_ref[i, k - cut] = factor[k] * (w_ref[i] * inverse)


def second_outer_kernel(
    far_ref, two_ref, offset_ref, slope_ref, z_natural, num0, scale0, later_lo2, later_hi2, early,
    out_hbm, out_ref, sems,
):
    count, slots, cells = out_ref.shape
    cut = num0.shape[0] - count
    copies = [pltpu.make_async_copy(early, out_hbm.at[:cut], sems.at[count])]
    copies[-1].start()
    ghosts = dot_first(jnp.concatenate([later_lo2[...], later_hi2[...]], 0), far_ref[...])

    def phi_of(k, i, ghost):
        return offset_ref[i, k] + slope_ref[i, k] * ghost

    for k in finish(ghosts, phi_of, two_ref, z_natural, num0, scale0, cut, out_ref):
        copies.append(pltpu.make_async_copy(out_ref.at[k], out_hbm.at[cut + k], sems.at[k]))
        copies[-1].start()
    for copy in copies:
        copy.wait()


def call(
    kernel, out_shape, scratch, operands, specs=None, outs=None, flops=0, limit=0,
    grid=(1,),
):
    whole = pl.BlockSpec(memory_space=pltpu.VMEM)
    specs = specs or {}
    moved = sum(o.size * o.dtype.itemsize for o in operands)
    moved += sum(o.size * o.dtype.itemsize for o in out_shape)
    return pl.pallas_call(
        kernel,
        out_shape=out_shape,
        grid=grid,
        in_specs=[specs.get(i, whole) for i in range(len(operands))],
        out_specs=outs or [whole] * len(out_shape),
        scratch_shapes=scratch,
        compiler_params=pltpu.CompilerParams(vmem_limit_bytes=limit or VMEM_LIMIT),
        cost_estimate=pl.CostEstimate(flops=flops, bytes_accessed=moved, transcendentals=0),
    )(*operands)


def per_device(state, coef, new_group, face_lists, lewis):
    groups = lax.axis_size("group")
    members = lax.axis_size("member")
    along = ("group", "member")

    def pairs(turn, ends):
        steps = []
        for g in range(groups):
            shift = 1 if up_first(g) == (turn == 0) else -1
            for i in range(members) if ends else range(1, members - 1):
                if 0 <= i + shift < members:
                    steps.append((g * members + i, g * members + i + shift))
        return steps

    one, two = pairs(0, True), pairs(1, True)
    one_on, two_on = pairs(0, False), pairs(1, False)
    slots, species, cells = state.shape[2:]
    capacity = slots // groups
    cuts = (species - species // 2, species // 2)
    width = (1 + species) * cells
    middle = (1 + cuts[0]) * cells
    long = cells + SPARE
    smem = pl.BlockSpec(memory_space=pltpu.SMEM)
    anywhere = pl.BlockSpec(memory_space=pl.ANY)

    def shape(*dims, dtype=F32):
        return jax.ShapeDtypeStruct(dims, dtype)

    send, lists = call(
        functools.partial(pack_kernel, groups, capacity),
        [shape(slots, width, dtype=BF16), shape(8, slots, dtype=jnp.int32)],
        [],
        (
            new_group[0],
            jnp.transpose(face_lists[0], (1, 0, 2)),
            jnp.transpose(state[0, 0], (1, 0, 2)),
            coef[0, 0],
        ),
        limit=PACK_LIMIT,
        grid=(),
    )
    rows = lax.all_to_all(send, "group", split_axis=0, concat_axis=0, tiled=True)
    lists_lo = lax.ppermute(lists, along, one)
    lists_hi = lax.ppermute(lists, along, two)
    pick0, xy_pick, z_pick = call(
        pick_kernel,
        [
            shape(FACES, slots, slots, dtype=BF16),
            shape(2, 4, slots, slots, dtype=BF16),
            shape(2, slots, 2 * slots, dtype=BF16),
        ],
        [],
        (lists, lists_lo, lists_hi),
    )
    rows, pick0, xy_pick, z_pick = lax.optimization_barrier((rows, pick0, xy_pick, z_pick))
    soon = rows[:, :middle]
    got_lo = [lax.ppermute(soon, along, one)]
    got_hi = [lax.ppermute(soon, along, two)]
    coef0, weights0, flat, base, rhs = call(
        own_kernel,
        [
            shape(cells, slots),
            shape(4, cells, slots),
            shape(species, cells, slots, dtype=BF16),
            shape(species, cells, slots),
            shape(species, cells, slots),
        ],
        [pltpu.VMEM((PADDED, slots), F32), pltpu.VMEM((species, PADDED, slots), F32)],
        (lewis, rows, pick0),
        specs={0: smem},
        flops=500_000_000,
    )
    later, coef0, weights0, flat, base, rhs = lax.optimization_barrier(
        (rows[:, middle:], coef0, weights0, flat, base, rhs)
    )
    got_lo.append(lax.ppermute(later, along, one))
    got_hi.append(lax.ppermute(later, along, two))
    got_lo2 = [lax.ppermute(part, along, one_on) for part in got_lo]
    got_hi2 = [lax.ppermute(part, along, two_on) for part in got_hi]

    z_natural, total, coefs, *numbers = call(
        functools.partial(both_kernel, cuts),
        [shape(2, long, slots)] * 2 + [shape(2, cells, slots)] + [shape(species, long, slots)] * 4,
        [
            pltpu.VMEM((2, slots, 2 * slots), BF16),
            pltpu.VMEM((2, cells, slots), F32),
            pltpu.VMEM((cells, slots), F32),
            pltpu.VMEM((2, 5, cells, slots), F32),
            pltpu.VMEM((2, PADDED, slots), F32),
            pltpu.VMEM((2, long, slots), F32),
            pltpu.VMEM((2, species, PADDED, slots), F32),
            pltpu.VMEM((4, species, long, slots), F32),
            pltpu.VMEM((species, PADDED, slots), F32),
        ],
        (
            lewis, got_lo[0], got_hi[0], got_lo[1], got_hi[1],
            coef0, pick0, weights0, xy_pick, z_pick, flat, base, rhs,
        ),
        specs={0: smem},
        flops=200_000_000 * species,
    )
    far, twos, offset, slope, early = call(
        first_outer_kernel,
        [
            shape(2 * slots, 2 * slots, dtype=BF16),
            shape(2, 2 * slots, slots, dtype=BF16),
            shape(2, cuts[1], cells, slots),
            shape(2, cuts[1], cells, slots),
            shape(cuts[0], slots, cells),
        ],
        [pltpu.VMEM((2, cells, slots), F32), pltpu.VMEM((2, cells, slots), F32)],
        (lewis, pick0, z_pick, total, coefs, z_natural, *numbers, got_lo2[0], got_hi2[0]),
        specs={0: smem},
        flops=100_000_000 * cuts[0],
    )
    (out,) = call(
        second_outer_kernel,
        [shape(species, slots, cells)],
        [pltpu.VMEM((cuts[1], slots, cells), F32), pltpu.SemaphoreType.DMA((cuts[1] + 1,))],
        (
            far, twos, offset, slope, z_natural, numbers[0], numbers[1],
            got_lo2[1], got_hi2[1], early,
        ),
        outs=[anywhere],
        flops=100_000_000 * cuts[1],
    )
    return jnp.transpose(out, (1, 0, 2))[None, None]


def solution(mesh):
    return jax.shard_map(
        per_device,
        mesh=mesh,
        in_specs=(
            P("group", "member", None, None, None),
            P("group", "member", None, None),
            P("group", "member", None),
            P("group", "member", None, None),
            P(),
        ),
        out_specs=P("group", "member", None, None, None),
        check_vma=False,
    )
```

```python
import functools

import jax
import jax.numpy as jnp
from jax import lax
from jax.experimental import pallas as pl
from jax.experimental.pallas import tpu as pltpu
from jax.sharding import PartitionSpec as P

PX = 16
PY = 16
FACES = 6
LANES = 128
HALF = PX // 2
PITCH = PX + 8
F32 = jnp.float32
BF16 = jnp.bfloat16
VMEM_LIMIT = 28 * 1024 * 1024
PACK_LIMIT = 60 * 1024 * 1024


def dot(a, b):
    return jnp.dot(a, b, preferred_element_type=F32)


def dot_first(a, b):
    return lax.dot_general(a, b, (((0,), (0,)), ((), ())), preferred_element_type=F32)


def iota(shape, dim):
    return lax.broadcasted_iota(jnp.int32, shape, dim)


def ones_where(mask):
    return jnp.where(mask, 1.0, 0.0).astype(BF16)


def up_first(group):
    return group % 4 == 2


def pack_kernel(groups, capacity, dest_ref, lists_ref, state_ref, coef_ref, send_ref, lists_out):
    species, slots, cells = state_ref.shape
    dest = dest_ref[...]
    onehot = iota((groups, slots), 0) == dest
    earlier = dot(
        ones_where(onehot), ones_where(iota((slots, slots), 0) < iota((slots, slots), 1))
    )
    running = jnp.sum(jnp.where(onehot, earlier, 0.0), axis=0, keepdims=True).astype(jnp.int32)
    position = jnp.where(dest >= 0, dest * capacity + running, -1)
    place = ones_where(iota((slots, slots), 0) == position)
    send_ref[:, :cells] = dot(place, coef_ref[...]).astype(BF16)
    for k in range(species):
        at = slice((k + 1) * cells, (k + 2) * cells)
        send_ref[:, at] = dot(place, state_ref[k]).astype(BF16)
    none = jnp.zeros((1, slots), jnp.int32)
    rows = [lists_ref[f] + 1 for f in range(FACES)] + [none] * (8 - FACES)
    same = up_first(lax.axis_index("group"))
    rows[4], rows[5] = jnp.where(same, rows[4], rows[5]), jnp.where(same, rows[5], rows[4])
    lists_out[...] = jnp.concatenate(rows, 0)


def sorting(coef_rows):
    slots = coef_rows.shape[0]
    lead = coef_rows[:, :slots].astype(F32)[:, :1]
    valid = jnp.broadcast_to(lead, (slots, slots)) > 0.0
    slot = dot(
        ones_where(iota((slots, slots), 1) < iota((slots, slots), 0)), ones_where(valid)
    ).astype(jnp.int32)
    return ones_where(valid & (slot == iota((slots, slots), 1)))


def picking(entry):
    slots = entry.shape[1]
    return ones_where(iota((slots, slots), 0) == entry)


def diagonal(a, b):
    none = jnp.zeros_like(a)
    return jnp.concatenate(
        [jnp.concatenate([a, none], 1), jnp.concatenate([none, b], 1)], 0
    )


def twice(matrix):
    return jnp.concatenate([matrix, matrix], 0)


def split(field):
    high = field.astype(BF16)
    low = (field - high.astype(F32)).astype(BF16)
    return jnp.concatenate([high, low], 1)


PADDED = (PY + 2) * PITCH


def row(y):
    return (y + 1) * PITCH + PITCH - PX


def step(start):
    return pl.ds(start, HALF, stride=2)


def natural(y, odd):
    return step(y * PX + odd)


def halves(y, odd):
    return slice(y * PX + odd * HALF, y * PX + (odd + 1) * HALF)


def put(padded, field):
    for y in range(PY):
        padded[row(y) : row(y) + PX] = field[y * PX : (y + 1) * PX]


def beside_xy(padded, y, odd):
    at = row(y) + odd
    return [padded[step(at + shift)] for shift in (-1, 1, -PITCH, PITCH)]


def weighted(weights, values):
    flow = weights[0] * values[0]
    for w, v in zip(weights[1:], values[1:]):
        flow = flow + w * v
    return flow


def fill_edges(picks, fields, exact):
    x_first, x_last = row(0), row(0) + PX - 1
    places = (
        (pl.ds(x_last, PY, stride=PITCH), pl.ds(x_first - 1, PY, stride=PITCH)),
        (pl.ds(x_first, PY, stride=PITCH), pl.ds(x_last + 1, PY, stride=PITCH)),
        (pl.ds(row(PY - 1), PX), pl.ds(row(-1), PX)),
        (pl.ds(row(0), PX), pl.ds(row(PY), PX)),
    )
    for pick, (source, target) in zip(picks, places):
        taken = jnp.concatenate([field[source] for field in fields], 0)
        got = dot(taken.astype(BF16), pick) if exact else dot(split(taken), twice(pick))
        for i, field in enumerate(fields):
            field[target] = got[i * PX : (i + 1) * PX]


def pick_kernel(lists0, lists_lo, lists_hi, pick_ref, xy_pick, z_pick):
    slots = lists0.shape[1]

    def picking(lists, face):
        return ones_where(iota((slots, slots), 0) == lists[face : face + 1] - 1)

    for face in range(FACES):
        pick_ref[face] = picking(lists0, face)
    for d, lists in enumerate((lists_lo, lists_hi)):
        for face in range(4):
            xy_pick[d, face] = picking(lists, face)
    z_pick[0] = jnp.concatenate([picking(lists_lo, 5), picking(lists_hi, 4)], 1)
    z_pick[1] = jnp.concatenate([picking(lists_lo, 4), picking(lists_hi, 5)], 1)


def own_kernel(
    lewis_ref, got, pick_ref,
    coef_ref, weights_ref, flat_ref, base_ref, rhs_ref, coef_pad, field_ref,
):
    species, cells, slots = base_ref.shape
    sort = diagonal(*[sorting(got[:, :cells])] * 2)
    count = (species + 2) // 2
    pair = [got[:, : count * cells], got[:, (species + 1 - count) * cells :]]
    both = dot_first(jnp.concatenate(pair, 0), sort)
    fields = [both[k * cells : (k + 1) * cells, :slots] for k in range(count)]
    fields += [
        both[k * cells : (k + 1) * cells, slots:] for k in range(2 * count - species - 1, count)
    ]
    coef_ref[...] = fields[0]
    put(coef_pad, fields[0])
    picks = [pick_ref[face] for face in range(4)]
    fill_edges(picks, [coef_pad], True)
    for k in range(species):
        put(field_ref.at[k], fields[k + 1])
        flat_ref[k] = fields[k + 1].astype(BF16)
    fill_edges(picks, [field_ref.at[k] for k in range(species)], True)
    factor = [lewis_ref[k] for k in range(species)]
    for y in range(PY):
        for odd in range(2):
            at = halves(y, odd)
            own = coef_pad[step(row(y) + odd)]
            weights = [0.5 * (own + near) for near in beside_xy(coef_pad, y, odd)]
            for f in range(4):
                weights_ref[f, at] = weights[f]
            for k in range(species):
                field = field_ref[k, step(row(y) + odd)]
                flow = weighted(weights, beside_xy(field_ref.at[k], y, odd))
                base_ref[k, at] = field + factor[k] * flow
                rhs_ref[k, at] = field


def prepare_kernel(
    head_lo, head_hi, coef0, pick0, weights0, xy_pick, z_pick,
    sort_ref, z_natural, z_halves, total0, beside_ref, total_ref, coef_ref, padded, z_ref,
):
    cells, slots = coef0.shape
    for d, head in enumerate((head_lo, head_hi)):
        rows = head[:, :cells]
        sort = sorting(rows)
        both = jnp.concatenate([sort, dot(sort, pick0[4 + d]).astype(BF16)], 1)
        sort_ref[d] = both
        coef = dot_first(rows, both)
        coef_ref[d] = coef[:, :slots]
        put(padded.at[d], coef[:, :slots])
        z_natural[d] = 0.5 * (coef0[...] + coef[:, slots:])
        fill_edges([xy_pick[d, f] for f in range(4)], [padded.at[d]], True)
    near = dot(coef0[...].astype(BF16), z_pick[0])
    z_ref[0] = near[:, :slots]
    z_ref[1] = near[:, slots:]
    for y in range(PY):
        for odd in range(2):
            at = halves(y, odd)
            total = None
            for i in range(2):
                w = z_natural[i, natural(y, odd)]
                z_halves[i, at] = w
                total = w if total is None else total + w
            for f in range(4):
                total = total + weights0[f, at]
            total0[at] = total
            for d in range(2):
                own = padded[d, step(row(y) + odd)]
                near = [*beside_xy(padded.at[d], y, odd), z_ref[d, natural(y, odd)]]
                total = None
                for f in range(5):
                    w = 0.5 * (own + near[f])
                    beside_ref[d, f, at] = w
                    total = w if total is None else total + w
                total_ref[d, natural(y, odd)] = total


def inner_kernel(
    cuts, lewis_ref, sort_ref, xy_pick, z_pick, z_halves, total0, beside_ref,
    pick0, weights0, flat_ref, base_ref, rhs_ref, parts,
    num0, scale0, num_lo, num_hi, field_ref, z_ref, phi_ref,
):
    species, cells, slots = num0.shape
    numbers = (num_lo, num_hi)
    factor = [lewis_ref[k] for k in range(species)]
    for d in range(2):
        k = 0
        for gots, skip, count in zip(parts, (cells, 0), cuts):
            both = dot_first(gots[d][:, skip:], sort_ref[d])
            for i in range(count):
                rows = slice(i * cells, (i + 1) * cells)
                put(field_ref.at[d, k], both[rows, :slots])
                z_ref[d, k] = both[rows, slots:]
                k += 1
    near = dot(flat_ref[...].reshape(species * cells, slots), z_pick[0])
    for k in range(species):
        for d in range(2):
            z_ref[2 + d, k] = near[k * cells : (k + 1) * cells, d * slots : (d + 1) * slots]
    for d in range(2):
        fill_edges(
            [xy_pick[d, f] for f in range(4)], [field_ref.at[d, k] for k in range(species)], True
        )
    for y in range(PY):
        for odd in range(2):
            at = halves(y, odd)
            weights = [z_halves[i, at] for i in range(2)]
            total = total0[at]
            for k in range(species):
                near = [z_ref[i, k, natural(y, odd)] for i in range(2)]
                number = base_ref[k, at] + factor[k] * weighted(weights, near)
                inverse = 1.0 / (1.0 + factor[k] * total)
                phi_ref[k, step(row(y) + odd)] = number * inverse
                scale0[k, natural(y, odd)] = inverse
    fill_edges([pick0[f] for f in range(4)], [phi_ref.at[k] for k in range(species)], False)
    for d in range(2):
        for y in range(PY):
            for odd in range(2):
                at = halves(y, odd)
                weights = [beside_ref[d, f, at] for f in range(5)]
                for k in range(species):
                    near = beside_xy(field_ref.at[d, k], y, odd)
                    near.append(z_ref[2 + d, k, natural(y, odd)])
                    numbers[d][k, natural(y, odd)] = (
                        field_ref[d, k, step(row(y) + odd)] + factor[k] * weighted(weights, near)
                    )
    for y in range(PY):
        for odd in range(2):
            at = halves(y, odd)
            weights = [weights0[f, at] for f in range(4)]
            for k in range(species):
                near = beside_xy(phi_ref.at[k], y, odd)
                inverse = scale0[k, natural(y, odd)]
                number = rhs_ref[k, at] + factor[k] * weighted(weights, near)
                num0[k, natural(y, odd)] = number * inverse
                scale0[k, natural(y, odd)] = factor[k] * inverse


def both_kernel(
    cuts, lewis_ref, got_lo, got_hi, later_lo, later_hi,
    coef0, pick0, weights0, xy_pick, z_pick, flat_ref, base_ref, rhs_ref,
    z_natural, total_ref, coef_ref, num0, scale0, num_lo, num_hi,
    sort_ref, z_halves, total0, beside_ref, padded, near_ref, field_ref, z_ref, phi_ref,
):
    prepare_kernel(
        got_lo, got_hi, coef0, pick0, weights0, xy_pick, z_pick,
        sort_ref, z_natural, z_halves, total0, beside_ref, total_ref, coef_ref, padded, near_ref,
    )
    inner_kernel(
        cuts, lewis_ref, sort_ref, xy_pick, z_pick, z_halves, total0, beside_ref,
        pick0, weights0, flat_ref, base_ref, rhs_ref, ((got_lo, got_hi), (later_lo, later_hi)),
        num0, scale0, num_lo, num_hi, field_ref, z_ref, phi_ref,
    )


def far_kernel(pick0, z_pick, total_ref, coef_ref, head_lo2, head_hi2, far_ref, w_ref, t_ref, two_ref):
    cells = coef_ref.shape[1]
    slots = coef_ref.shape[2]
    rows = [head_lo2[:, :cells], head_hi2[:, :cells]]
    fars = []
    for i in range(2):
        fars.append(dot(sorting(rows[i]), z_pick[1, :, i * slots : (i + 1) * slots]).astype(BF16))
        two_ref[i] = twice(pick0[4 + i])
    far = diagonal(*fars)
    far_ref[...] = far
    near = dot_first(jnp.concatenate(rows, 0), far)
    for i in range(2):
        w = 0.5 * (coef_ref[i] + near[:, i * slots : (i + 1) * slots])
        w_ref[i] = w
        t_ref[i] = total_ref[i] + w


def finish(ghosts, phi_of, two_ref, z_natural, num0, scale0, first, out_ref):
    count, slots, cells = out_ref.shape
    terms = []
    for i in range(2):
        phis = [
            split(phi_of(k, i, ghosts[k * cells : (k + 1) * cells, i * slots : (i + 1) * slots]))
            for k in range(count)
        ]
        terms.append(dot(jnp.concatenate(phis, 0), two_ref[i]))
    for k in range(count):
        rows = slice(k * cells, (k + 1) * cells)
        flow = z_natural[0] * terms[0][rows] + z_natural[1] * terms[1][rows]
        out_ref[k] = jnp.transpose(num0[first + k] + scale0[first + k] * flow, (1, 0))
        yield k


def first_outer_kernel(
    lewis_ref, pick0, z_pick, total_ref, coef_ref, z_natural, num0, scale0, num_lo, num_hi,
    got_lo2, got_hi2, far_ref, two_ref, offset_ref, slope_ref, out_ref, w_ref, t_ref,
):
    far_kernel(
        pick0, z_pick, total_ref, coef_ref, got_lo2, got_hi2, far_ref, w_ref, t_ref, two_ref
    )
    cut, slots, cells = out_ref.shape
    numbers = (num_lo, num_hi)
    factor = [lewis_ref[k] for k in range(num0.shape[0])]
    ghosts = dot_first(
        jnp.concatenate([got_lo2[:, cells:], got_hi2[:, cells:]], 0), far_ref[...]
    )

    def phi_of(k, i, ghost):
        number = numbers[i][k] + factor[k] * (w_ref[i] * ghost)
        return number * (1.0 / (1.0 + factor[k] * t_ref[i]))

    for k in finish(ghosts, phi_of, two_ref, z_natural, num0, scale0, 0, out_ref):
        pass
    for k in range(cut, num0.shape[0]):
        for i in range(2):
            inverse = 1.0 / (1.0 + factor[k] * t_ref[i])
            offset_ref[i, k - cut] = numbers[i][k] * inverse
            slope_ref[i, k - cut] = factor[k] * (w_ref[i] * inverse)


def second_outer_kernel(
    far_ref, two_ref, offset_ref, slope_ref, z_natural, num0, scale0, later_lo2, later_hi2, early,
    out_hbm, out_ref, sems,
):
    count, slots, cells = out_ref.shape
    cut = num0.shape[0] - count
    copies = [pltpu.make_async_copy(early, out_hbm.at[:cut], sems.at[count])]
    copies[-1].start()
    ghosts = dot_first(jnp.concatenate([later_lo2[...], later_hi2[...]], 0), far_ref[...])

    def phi_of(k, i, ghost):
        return offset_ref[i, k] + slope_ref[i, k] * ghost

    for k in finish(ghosts, phi_of, two_ref, z_natural, num0, scale0, cut, out_ref):
        copies.append(pltpu.make_async_copy(out_ref.at[k], out_hbm.at[cut + k], sems.at[k]))
        copies[-1].start()
    for copy in copies:
        copy.wait()


def call(
    kernel, out_shape, scratch, operands, specs=None, outs=None, flops=0, limit=0,
    grid=(1,),
):
    whole = pl.BlockSpec(memory_space=pltpu.VMEM)
    specs = specs or {}
    moved = sum(o.size * o.dtype.itemsize for o in operands)
    moved += sum(o.size * o.dtype.itemsize for o in out_shape)
    return pl.pallas_call(
        kernel,
        out_shape=out_shape,
        grid=grid,
        in_specs=[specs.get(i, whole) for i in range(len(operands))],
        out_specs=outs or [whole] * len(out_shape),
        scratch_shapes=scratch,
        compiler_params=pltpu.CompilerParams(vmem_limit_bytes=limit or VMEM_LIMIT),
        cost_estimate=pl.CostEstimate(flops=flops, bytes_accessed=moved, transcendentals=0),
    )(*operands)


def per_device(state, coef, new_group, face_lists, lewis):
    groups = lax.axis_size("group")
    members = lax.axis_size("member")
    along = ("group", "member")

    def pairs(turn, ends):
        steps = []
        for g in range(groups):
            shift = 1 if up_first(g) == (turn == 0) else -1
            for i in range(members) if ends else range(1, members - 1):
                if 0 <= i + shift < members:
                    steps.append((g * members + i, g * members + i + shift))
        return steps

    one, two = pairs(0, True), pairs(1, True)
    one_on, two_on = pairs(0, False), pairs(1, False)
    slots, species, cells = state.shape[2:]
    capacity = slots // groups
    cuts = (species // 2, species - species // 2)
    width = (1 + species) * cells
    middle = (1 + cuts[0]) * cells
    smem = pl.BlockSpec(memory_space=pltpu.SMEM)
    anywhere = pl.BlockSpec(memory_space=pl.ANY)

    def shape(*dims, dtype=F32):
        return jax.ShapeDtypeStruct(dims, dtype)

    send, lists = call(
        functools.partial(pack_kernel, groups, capacity),
        [shape(slots, width, dtype=BF16), shape(8, slots, dtype=jnp.int32)],
        [],
        (
            new_group[0],
            jnp.transpose(face_lists[0], (1, 0, 2)),
            jnp.transpose(state[0, 0], (1, 0, 2)),
            coef[0, 0],
        ),
        limit=PACK_LIMIT,
        grid=(),
    )
    rows = lax.all_to_all(send, "group", split_axis=0, concat_axis=0, tiled=True)
    lists_lo = lax.ppermute(lists, along, one)
    lists_hi = lax.ppermute(lists, along, two)
    pick0, xy_pick, z_pick = call(
        pick_kernel,
        [
            shape(FACES, slots, slots, dtype=BF16),
            shape(2, 4, slots, slots, dtype=BF16),
            shape(2, slots, 2 * slots, dtype=BF16),
        ],
        [],
        (lists, lists_lo, lists_hi),
    )
    rows, pick0, xy_pick, z_pick = lax.optimization_barrier((rows, pick0, xy_pick, z_pick))
    soon = rows[:, :middle]
    got_lo = [lax.ppermute(soon, along, one)]
    got_hi = [lax.ppermute(soon, along, two)]
    coef0, weights0, flat, base, rhs = call(
        own_kernel,
        [
            shape(cells, slots),
            shape(4, cells, slots),
            shape(species, cells, slots, dtype=BF16),
            shape(species, cells, slots),
            shape(species, cells, slots),
        ],
        [pltpu.VMEM((PADDED, slots), F32), pltpu.VMEM((species, PADDED, slots), F32)],
        (lewis, rows, pick0),
        specs={0: smem},
        flops=500_000_000,
    )
    later, coef0, weights0, flat, base, rhs = lax.optimization_barrier(
        (rows[:, middle:], coef0, weights0, flat, base, rhs)
    )
    got_lo.append(lax.ppermute(later, along, one))
    got_hi.append(lax.ppermute(later, along, two))
    got_lo2 = [lax.ppermute(part, along, one_on) for part in got_lo]
    got_hi2 = [lax.ppermute(part, along, two_on) for part in got_hi]

    z_natural, total, coefs, *numbers = call(
        functools.partial(both_kernel, cuts),
        [shape(2, cells, slots)] * 3 + [shape(species, cells, slots)] * 4,
        [
            pltpu.VMEM((2, slots, 2 * slots), BF16),
            pltpu.VMEM((2, cells, slots), F32),
            pltpu.VMEM((cells, slots), F32),
            pltpu.VMEM((2, 5, cells, slots), F32),
            pltpu.VMEM((2, PADDED, slots), F32),
            pltpu.VMEM((2, cells, slots), F32),
            pltpu.VMEM((2, species, PADDED, slots), F32),
            pltpu.VMEM((4, species, cells, slots), F32),
            pltpu.VMEM((species, PADDED, slots), F32),
        ],
        (
            lewis, got_lo[0], got_hi[0], got_lo[1], got_hi[1],
            coef0, pick0, weights0, xy_pick, z_pick, flat, base, rhs,
        ),
        specs={0: smem},
        flops=200_000_000 * species,
    )
    far, twos, offset, slope, early = call(
        first_outer_kernel,
        [
            shape(2 * slots, 2 * slots, dtype=BF16),
            shape(2, 2 * slots, slots, dtype=BF16),
            shape(2, cuts[1], cells, slots),
            shape(2, cuts[1], cells, slots),
            shape(cuts[0], slots, cells),
        ],
        [pltpu.VMEM((2, cells, slots), F32), pltpu.VMEM((2, cells, slots), F32)],
        (lewis, pick0, z_pick, total, coefs, z_natural, *numbers, got_lo2[0], got_hi2[0]),
        specs={0: smem},
        flops=100_000_000 * cuts[0],
    )
    (out,) = call(
        second_outer_kernel,
        [shape(species, slots, cells)],
        [pltpu.VMEM((cuts[1], slots, cells), F32), pltpu.SemaphoreType.DMA((cuts[1] + 1,))],
        (
            far, twos, offset, slope, z_natural, numbers[0], numbers[1],
            got_lo2[1], got_hi2[1], early,
        ),
        outs=[anywhere],
        flops=100_000_000 * cuts[1],
    )
    return jnp.transpose(out, (1, 0, 2))[None, None]


def solution(mesh):
    return jax.shard_map(
        per_device,
        mesh=mesh,
        in_specs=(
            P("group", "member", None, None, None),
            P("group", "member", None, None),
            P("group", "member", None),
            P("group", "member", None, None),
            P(),
        ),
        out_specs=P("group", "member", None, None, None),
        check_vma=False,
    )
```
